32 devices in a mesh: dp: 2 (over core), far: 4 (over y, x), near: 4 (over z).
Axes of the slice: x: 2, y: 2, z: 4, core: 2. Of those that a mesh axis runs over, the one named last changes fastest.
Arguments:
- grad_out: bfloat16 [1024, 4096], P(('dp', 'far', 'near')), may hold values from -6 to 6
- hidden: bfloat16 [1024, 8, 768], P(('dp', 'far', 'near')), may hold values from -6 to 6
- gates: float32 [1024, 8], P(('dp', 'far', 'near')), may hold values from 0.05 to 1
- expert_ids: int32 [1024, 8], P(('dp', 'far', 'near')), may hold values from 0 to 15, all different within a row; in each aligned block of 32 rows (0 to 31, 32 to 63, ...) at most 16 rows name the same one
- w_down: bfloat16 [16, 768, 4096], P(('far', 'near')), may hold values from -0.09375 to 0.09375
Outputs:
- grad_hidden: bfloat16 [1024, 8, 768], P(('dp', 'far', 'near'))
- grad_gates: float32 [1024, 8], P(('dp', 'far', 'near'))
- grad_down: bfloat16 [16, 768, 4096], P(('far', 'near'), 'dp')
The draws below stay inside these ranges and needn't reach their ends.
Inputs may be any that keep to these rules, and one draw needn't show every extreme that they name: `expert_ids`: each token names 8 different experts; among the tokens of one device no expert is named by more than 16 tokens, a bound that some block reaches.
All inputs are finite; a program needn't handle non-finite values.
Results may differ from the reference program's by a relative error of at most 0.008.
Values may be sent and summed in bfloat16 or wider, within the bound.
No kernel may reach another device: no remote copies, remote signals or barrier semaphores. Data moves between devices by JAX's collectives and lax.ppermute only.
A program may use at most 64 MiB of HBM per device.

```python
import math
import jax
import jax.numpy as jnp
import numpy as np
from jax import lax

D = 4096
TOP = 8
H = 768
TOK_DEV = 32
EXPERTS = 16
CAP = 16
TOKENS = 1024
N_DP = 2
N_FAR = 4
N_NEAR = 4


def block_scale(rng, extent, shards, low, largest):
    loudness, own = 1.0, jax.random.fold_in(rng, 6)
    for position, shards_of in shards:
        heights = jnp.exp(jax.random.uniform(jax.random.fold_in(own, position), (shards_of,), jnp.float32, low / len(shards), largest / len(shards)))
        loudness = loudness * jnp.repeat(heights, extent[position] // shards_of).reshape([-1 if axis == position else 1 for axis in range(len(extent))])
    return loudness


def shared_out(key, own, number, rows, number_of, top, reach, lean):
    order = jax.random.permutation(key, number_of)
    heavy_load, ordinary = load_shares(number_of, rows * top, reach, lean, True), load_shares(number_of, rows * top, reach, lean, False)
    places = jnp.arange(number_of)

    def named(tallies, rotation):
        used = int((tallies > 0).sum())
        fixed = max(1, used // 4)
        passed = fixed + (places - fixed + rotation * (used - fixed)) % max(1, number_of - fixed)
        return jnp.zeros((number_of,), jnp.int32).at[order[jnp.where(places < fixed, places, passed)]].set(jnp.asarray(tallies, jnp.int32))

    tallies = jnp.where(number % 4 == 0, named(heavy_load, number // 4), named(ordinary, number - number // 4 - 1))
    mixed = jax.random.permutation(jax.random.fold_in(own, 3), number_of)
    donor, sink = mixed[0:number_of // 2 * 2:2], mixed[1:number_of // 2 * 2:2]
    slack = jnp.minimum(tallies[donor] - 1, reach - tallies[sink]) // 2
    slack = jnp.where((donor == order[0]) | (sink == order[0]) | (tallies[sink] == 0), 0, jnp.maximum(slack, 0))
    passed = jax.random.randint(jax.random.fold_in(own, 4), (number_of // 2,), 0, 1 << 20) % (slack + 1)
    tallies = tallies.at[donor].add(-passed).at[sink].add(passed)
    labels = jnp.searchsorted(jnp.cumsum(tallies), jnp.arange(rows * top), side="right").astype(jnp.int32)
    table = labels.reshape(top, rows).T
    table = table[jax.random.permutation(jax.random.fold_in(own, 1), rows)]
    rotation = jax.random.randint(jax.random.fold_in(own, 2), (rows, 1), 0, top)
    return jnp.take_along_axis(table, (jnp.arange(top)[None, :] + rotation) % top, axis=1)


def load_shares(number_of, total, limit, slope, full):
    weights = [(1 << 20) // math.isqrt(standing ** slope) + 1 for standing in range(1, number_of + 1)]
    largest = limit if full else min(limit, max(-(-total // number_of), total * weights[0] // sum(weights)))
    least = 1 if total - largest >= number_of - 1 else 0
    given, surplus = [largest] + [least] * (number_of - 1), total - largest - least * (number_of - 1)
    while surplus > 0:
        candidates = [i for i in range(1, number_of) if given[i] < largest] or [i for i in range(1, number_of) if given[i] < limit]
        mass, budget = sum([weights[i] for i in candidates]), surplus
        for i in candidates:
            extra = min(limit - given[i], max(1, budget * weights[i] // mass), surplus)
            given[i] = given[i] + extra
            surplus = surplus - extra
    return np.array(given)


def gaussian(rng, extent, scale, reach, split=(), kind=jnp.bfloat16):
    values = scale * jax.random.normal(rng, extent, jnp.float32)
    if split:
        values = values * block_scale(rng, extent, split, -0.22, 0.18)
    return jnp.clip(values, -reach, reach).astype(kind)


def setup_inputs(seed: int = 0) -> dict:
    keys = jax.random.split(jax.random.key(seed), 6)
    grad_out = gaussian(keys[0], (TOKENS, D), 1.0, 6.0, ((0, 32),))
    hidden = gaussian(keys[1], (TOKENS, TOP, H), 1.0, 6.0, ((0, 32),))
    gates = jnp.clip(jnp.exp(math.log(1.0) - 2.9957323 * jax.random.uniform(keys[2], (TOKENS, TOP), jnp.float32) ** block_scale(keys[2], (TOKENS, TOP), ((0, 32),), -0.2, 0.2)), 0.05, 1.0)
    expert_ids_keys = jax.random.split(jax.random.fold_in(keys[3], 1), TOKENS // TOK_DEV)
    expert_ids_turns = jax.random.permutation(jax.random.fold_in(keys[3], 3), TOKENS // TOK_DEV)
    expert_ids = jax.vmap(lambda own, number: shared_out(jax.random.fold_in(keys[3], 2), own, number, TOK_DEV, EXPERTS, TOP, CAP, 2))(expert_ids_keys, expert_ids_turns).reshape((TOKENS, TOP))
    w_down = gaussian(keys[4], (EXPERTS, H, D), D ** -0.5, 0.09375, ((0, 16),))
    return dict(grad_out=grad_out, hidden=hidden, gates=gates, expert_ids=expert_ids, w_down=w_down)


def reference(grad_out, hidden, gates, expert_ids, w_down):
    tok_replica = TOKENS // N_DP
    rows_replica = tok_replica * TOP
    bound_rows = N_FAR * N_NEAR * CAP
    scaled = (gates[:, :, None] * hidden.astype(jnp.float32)).astype(jnp.bfloat16)
    scaled = scaled.reshape(N_DP, rows_replica, H)
    flat_ids = expert_ids.reshape(N_DP, rows_replica)
    sorted_rows = jnp.argsort(flat_ids, axis=1, stable=True).astype(jnp.int32)
    sorted_rows = jnp.concatenate([sorted_rows, jnp.zeros((N_DP, bound_rows), jnp.int32)], axis=1)
    expert_range = jnp.arange(EXPERTS, dtype=jnp.int32)
    counts = jnp.sum((flat_ids[:, :, None] == expert_range[None, None, :]).astype(jnp.int32), axis=1)
    starts = (jnp.cumsum(counts, axis=1) - counts).astype(jnp.int32)
    zero_value = jnp.zeros((), jnp.bfloat16)

    def per_expert(expert):
        weight = w_down[expert]
        summed = jnp.zeros((H, D), jnp.float32)
        returned_all = []
        places_all = []
        for replica in range(N_DP):
            places = lax.dynamic_slice_in_dim(sorted_rows[replica], starts[replica, expert], bound_rows)
            is_live = jnp.arange(bound_rows, dtype=jnp.int32) < counts[replica, expert]
            token_index = (places // TOP + replica * tok_replica).astype(jnp.int32)
            token_rows = grad_out[token_index]
            scaled_rows = jnp.where(is_live[:, None], scaled[replica][places], zero_value)
            returned = lax.dot_general(token_rows, weight, (((1,), (1,)), ((), ())),
                                       preferred_element_type=jnp.float32).astype(jnp.bfloat16)
            partial_value = lax.dot_general(scaled_rows, token_rows, (((0,), (0,)), ((), ())),
                                      preferred_element_type=jnp.float32).astype(jnp.bfloat16)
            summed = summed + partial_value.astype(jnp.float32)
            returned_all.append(returned)
            places_all.append(jnp.where(is_live, places + replica * rows_replica, N_DP * rows_replica).astype(jnp.int32))
        return summed.astype(jnp.bfloat16), jnp.stack(returned_all), jnp.stack(places_all)

    grad_down, returned_all, places_all = lax.map(per_expert, expert_range)
    back_flat = jnp.zeros((N_DP * rows_replica, H), jnp.bfloat16)
    back_flat = back_flat.at[places_all.reshape(-1)].set(returned_all.reshape(-1, H), mode="drop")
    back_rows = back_flat.reshape(TOKENS, TOP, H)
    grad_hidden = (gates[:, :, None] * back_rows.astype(jnp.float32)).astype(jnp.bfloat16)
    grad_gates = jnp.sum(back_rows.astype(jnp.float32) * hidden.astype(jnp.float32), axis=-1)
    return grad_hidden, grad_gates, grad_down
```

```python
import jax
import jax.numpy as jnp
from jax import lax
from jax.sharding import PartitionSpec as P


def partner(array, axis, apart):
    return lax.ppermute(array, axis, [(i, i ^ 1 << apart) for i in range(lax.axis_size(axis))])


def local(grad_out, hidden, gates, expert_ids, w_down):
    tok_local, top_count = expert_ids.shape
    far_count = lax.axis_size("far")
    near_count = lax.axis_size("near")
    experts = far_count * near_count
    capacity = max(4, (tok_local * top_count + experts - 1) // experts)
    width = grad_out.shape[1]
    hidden_width = hidden.shape[2]
    row_total = tok_local * top_count
    slot_total = experts * capacity
    me = lax.axis_index("far") * near_count + lax.axis_index("near")

    all_ids = lax.all_gather(expert_ids, ("far", "near"), axis=0, tiled=True)
    all_out = lax.all_gather(grad_out, ("far", "near"), axis=0, tiled=True)

    flat_ids = expert_ids.reshape(-1)
    one_hot = (flat_ids[:, None] == jnp.arange(experts, dtype=jnp.int32)[None, :]).astype(jnp.int32)
    ranks = jnp.sum(jnp.cumsum(one_hot, axis=0) * one_hot, axis=1) - 1
    slots = flat_ids * capacity + ranks
    place = (jnp.arange(slot_total, dtype=jnp.int32)[:, None] == slots[None, :]).astype(jnp.bfloat16)
    scaled = (
        (gates[:, :, None] * hidden.astype(jnp.float32))
        .astype(jnp.bfloat16)
        .reshape(row_total, hidden_width)
    )
    send_hid = jnp.dot(place, scaled, preferred_element_type=jnp.float32).astype(jnp.bfloat16)
    recv_hid = lax.all_to_all(
        send_hid.reshape(experts, capacity, hidden_width),
        ("far", "near"),
        split_axis=0,
        concat_axis=0,
        tiled=True,
    ).reshape(slot_total, hidden_width)

    named = jnp.any(all_ids == me, axis=1).reshape(experts, tok_local)
    rank = jnp.cumsum(named.astype(jnp.int32), axis=1) - 1
    slot = jnp.where(
        named, jnp.arange(experts, dtype=jnp.int32)[:, None] * capacity + rank, -1
    ).reshape(-1)
    pick = (jnp.arange(slot_total, dtype=jnp.int32)[:, None] == slot[None, :]).astype(jnp.bfloat16)
    recv_out = jnp.dot(pick, all_out, preferred_element_type=jnp.float32).astype(jnp.bfloat16)

    weight = w_down[0]
    returned = lax.dot_general(
        recv_out, weight, (((1,), (1,)), ((), ())), preferred_element_type=jnp.float32
    ).astype(jnp.bfloat16)
    share = hidden_width // lax.axis_size("dp")
    replica = lax.axis_index("dp")
    own_start = replica * share
    peer_start = (1 - replica) * share
    peer_cols = lax.dynamic_slice_in_dim(recv_hid, peer_start, share, 1)
    peer_out, peer_hid = partner((recv_out, peer_cols), "dp", 0)
    own_cols = lax.dynamic_slice_in_dim(recv_hid, own_start, share, 1)
    own_part = lax.dot_general(
        own_cols, recv_out, (((0,), (0,)), ((), ())), preferred_element_type=jnp.float32
    ).astype(jnp.bfloat16)
    peer_part = lax.dot_general(
        peer_hid, peer_out, (((0,), (0,)), ((), ())), preferred_element_type=jnp.float32
    ).astype(jnp.bfloat16)
    summed = own_part.astype(jnp.float32) + peer_part.astype(jnp.float32)
    grad_down = summed.astype(jnp.bfloat16)[None]
    came_back = lax.all_to_all(
        returned.reshape(experts, capacity, hidden_width),
        ("far", "near"),
        split_axis=0,
        concat_axis=0,
        tiled=True,
    )
    back_rows = lax.dot_general(
        place,
        came_back.reshape(slot_total, hidden_width),
        (((0,), (0,)), ((), ())),
        preferred_element_type=jnp.float32,
    ).reshape(tok_local, top_count, hidden_width)
    grad_hidden = (gates[:, :, None] * back_rows).astype(jnp.bfloat16)
    grad_gates = jnp.sum(back_rows * hidden.astype(jnp.float32), axis=-1)
    return (grad_hidden, grad_gates, grad_down)


def solution(mesh):
    placed = (
        P(("dp", "far", "near"), None),
        P(("dp", "far", "near"), None, None),
        P(("dp", "far", "near"), None),
        P(("dp", "far", "near"), None),
        P(("far", "near"), None, None),
    )
    return jax.shard_map(
        local,
        mesh=mesh,
        in_specs=placed,
        out_specs=(
            P(("dp", "far", "near"), None, None),
            P(("dp", "far", "near"), None),
            P(("far", "near"), "dp", None),
        ),
        check_vma=False,
    )
```

```python
import jax
import jax.numpy as jnp
from jax import lax
from jax.sharding import PartitionSpec as P


def local(grad_out, hidden, gates, expert_ids, w_down):
    tok_local, top_count = expert_ids.shape
    far_count = lax.axis_size("far")
    near_count = lax.axis_size("near")
    experts = far_count * near_count
    capacity = max(4, (tok_local * top_count + experts - 1) // experts)
    width = grad_out.shape[1]
    hidden_width = hidden.shape[2]
    row_total = tok_local * top_count
    slot_total = experts * capacity
    far = lax.axis_index("far")
    near = lax.axis_index("near")

    def shift(array, steps):
        return lax.ppermute(
            array, "near", [(i, (i + steps) % near_count) for i in range(near_count)]
        )

    def across(array, apart):
        if apart == 0:
            return array
        return lax.ppermute(array, "far", [(i, i ^ apart) for i in range(far_count)])

    def direct(array, apart, steps):
        if apart == 0 and steps % near_count == 0:
            return array
        return lax.ppermute(
            array,
            ("far", "near"),
            [
                (f * near_count + n, (f ^ apart) * near_count + (n + steps) % near_count)
                for f in range(far_count)
                for n in range(near_count)
            ],
        )

    blocks = [grad_out]
    ids = [expert_ids]
    for step in range(1, near_count):
        ids.append(shift(expert_ids, step))
    for step in range(1, near_count):
        blocks.append(shift(blocks[-1], 1))

    flat_ids = expert_ids.reshape(-1)
    one_hot = (flat_ids[:, None] == jnp.arange(experts, dtype=jnp.int32)[None, :]).astype(jnp.int32)
    ranks = jnp.sum(jnp.cumsum(one_hot, axis=0) * one_hot, axis=1) - 1
    apart_of = (flat_ids // near_count) ^ far
    steps_of = (flat_ids % near_count - near + near_count) % near_count
    slots = (steps_of * far_count + apart_of) * capacity + ranks
    place = (jnp.arange(slot_total, dtype=jnp.int32)[:, None] == slots[None, :]).astype(jnp.bfloat16)
    scaled = (
        (gates[:, :, None] * hidden.astype(jnp.float32))
        .astype(jnp.bfloat16)
        .reshape(row_total, hidden_width)
    )
    send_hid = (
        jnp.dot(place, scaled, preferred_element_type=jnp.float32)
        .astype(jnp.bfloat16)
        .reshape(near_count, far_count, capacity, hidden_width)
    )

    weight = w_down[0]
    plane = (jnp.arange(far_count, dtype=jnp.int32) ^ far) * near_count + near
    recv_out = []
    recv_hid = []
    back = []
    for step in range(near_count):
        named = jnp.any(ids[step][None] == plane[:, None, None], axis=2)
        rank = jnp.cumsum(named.astype(jnp.int32), axis=1) - 1
        pick = (
            named[:, None, :]
            & (rank[:, None, :] == jnp.arange(capacity, dtype=jnp.int32)[None, :, None])
        ).astype(jnp.bfloat16)
        picked = (
            jnp.dot(
                pick.reshape(far_count * capacity, tok_local),
                blocks[step],
                preferred_element_type=jnp.float32,
            )
            .astype(jnp.bfloat16)
            .reshape(far_count, capacity, width)
        )
        rows = jnp.concatenate([across(picked[apart], apart) for apart in range(far_count)], axis=0)
        recv_out.append(rows)
        recv_hid.extend(direct(send_hid[step, apart], apart, step) for apart in range(far_count))
        returned = (
            lax.dot_general(rows, weight, (((1,), (1,)), ((), ())), preferred_element_type=jnp.float32)
            .astype(jnp.bfloat16)
            .reshape(far_count, capacity, hidden_width)
        )
        back.extend(direct(returned[apart], apart, -step) for apart in range(far_count))
    recv_out = jnp.concatenate(recv_out, axis=0)
    recv_hid = jnp.concatenate(recv_hid, axis=0)

    share = hidden_width // lax.axis_size("dp")
    replica = lax.axis_index("dp")
    swap = [(i, i ^ 1) for i in range(lax.axis_size("dp"))]
    peer_cols = lax.dynamic_slice_in_dim(recv_hid, (1 - replica) * share, share, 1)
    peer_out = lax.ppermute(recv_out, "dp", swap)
    peer_hid = lax.ppermute(peer_cols, "dp", swap)
    own_cols = lax.dynamic_slice_in_dim(recv_hid, replica * share, share, 1)
    own_part = lax.dot_general(
        own_cols, recv_out, (((0,), (0,)), ((), ())), preferred_element_type=jnp.float32
    ).astype(jnp.bfloat16)
    peer_part = lax.dot_general(
        peer_hid, peer_out, (((0,), (0,)), ((), ())), preferred_element_type=jnp.float32
    ).astype(jnp.bfloat16)
    summed = own_part.astype(jnp.float32) + peer_part.astype(jnp.float32)
    grad_down = summed.astype(jnp.bfloat16)[None]

    back_rows = lax.dot_general(
        place,
        jnp.concatenate(back, axis=0),
        (((0,), (0,)), ((), ())),
        preferred_element_type=jnp.float32,
    ).reshape(tok_local, top_count, hidden_width)
    grad_hidden = (gates[:, :, None] * back_rows).astype(jnp.bfloat16)
    grad_gates = jnp.sum(back_rows * hidden.astype(jnp.float32), axis=-1)
    return (grad_hidden, grad_gates, grad_down)


def solution(mesh):
    placed = (
        P(("dp", "far", "near"), None),
        P(("dp", "far", "near"), None, None),
        P(("dp", "far", "near"), None),
        P(("dp", "far", "near"), None),
        P(("far", "near"), None, None),
    )
    return jax.shard_map(
        local,
        mesh=mesh,
        in_specs=placed,
        out_specs=(
            P(("dp", "far", "near"), None, None),
            P(("dp", "far", "near"), None),
            P(("far", "near"), "dp", None),
        ),
        check_vma=False,
    )
```

```python
import jax
import jax.numpy as jnp
from jax import lax
from jax.sharding import PartitionSpec as P

PARTS = 2
ID_COLS = 128


def swap(array):
    return lax.ppermute(array, "dp", [(i, i ^ 1) for i in range(lax.axis_size("dp"))])


def local(grad_out, hidden, gates, expert_ids, w_down):
    tok_local, top_count = expert_ids.shape
    far_count = lax.axis_size("far")
    near_count = lax.axis_size("near")
    experts = far_count * near_count
    capacity = max(4, (tok_local * top_count + experts - 1) // experts)
    width = grad_out.shape[1]
    part = width // PARTS
    hidden_width = hidden.shape[2]
    row_total = tok_local * top_count
    slot_total = experts * capacity
    near = lax.axis_index("near")

    id_cols = jnp.pad(expert_ids.astype(jnp.bfloat16), ((0, 0), (0, ID_COLS - top_count)))
    pieces = [grad_out[:, i * part : (i + 1) * part] for i in range(PARTS)]
    pieces[0] = jnp.concatenate([pieces[0], id_cols], axis=1)
    lines = [lax.all_gather(piece, "near", axis=0, tiled=True) for piece in pieces]

    flat_ids = expert_ids.reshape(-1)
    one_hot = (flat_ids[:, None] == jnp.arange(experts, dtype=jnp.int32)[None, :]).astype(jnp.int32)
    ranks = jnp.sum(jnp.cumsum(one_hot, axis=0) * one_hot, axis=1) - 1
    slots = flat_ids * capacity + ranks
    place = (jnp.arange(slot_total, dtype=jnp.int32)[:, None] == slots[None, :]).astype(jnp.bfloat16)
    scaled = (
        (gates[:, :, None] * hidden.astype(jnp.float32))
        .astype(jnp.bfloat16)
        .reshape(row_total, hidden_width)
    )
    send_hid = jnp.dot(place, scaled, preferred_element_type=jnp.float32).astype(jnp.bfloat16)

    line_ids = lines[0][:, part : part + top_count].astype(jnp.int32)
    plane = jnp.arange(far_count, dtype=jnp.int32) * near_count + near
    named = jnp.any(line_ids[None] == plane[:, None, None], axis=2).reshape(
        far_count, near_count, tok_local
    )
    rank = jnp.cumsum(named.astype(jnp.int32), axis=2) - 1
    slot = jnp.where(
        named, rank + jnp.arange(near_count, dtype=jnp.int32)[None, :, None] * capacity, -1
    ).reshape(far_count, 1, near_count * tok_local)
    pick = (
        (jnp.arange(near_count * capacity, dtype=jnp.int32)[None, :, None] == slot)
        .astype(jnp.bfloat16)
        .reshape(slot_total, near_count * tok_local)
    )

    weight = w_down[0]
    recv_out = []
    returned = jnp.zeros((slot_total, hidden_width), jnp.float32)
    for i, line in enumerate(lines):
        picked = jnp.dot(pick, line[:, :part], preferred_element_type=jnp.float32).astype(jnp.bfloat16)
        if i == PARTS - 1:
            picked, send_hid = lax.optimization_barrier((picked, send_hid))
        rows = lax.all_to_all(
            picked.reshape(far_count, near_count * capacity, part),
            "far",
            split_axis=0,
            concat_axis=0,
            tiled=True,
        ).reshape(slot_total, part)
        recv_out.append(rows)
        returned = returned + lax.dot_general(
            rows,
            weight[:, i * part : (i + 1) * part],
            (((1,), (1,)), ((), ())),
            preferred_element_type=jnp.float32,
        )
    recv_hid = lax.all_to_all(
        send_hid.reshape(experts, capacity, hidden_width),
        ("far", "near"),
        split_axis=0,
        concat_axis=0,
        tiled=True,
    ).reshape(slot_total, hidden_width)
    came_back = lax.all_to_all(
        returned.astype(jnp.bfloat16).reshape(experts, capacity, hidden_width),
        ("far", "near"),
        split_axis=0,
        concat_axis=0,
        tiled=True,
    )

    share = hidden_width // lax.axis_size("dp")
    replica = lax.axis_index("dp")
    peer_hid = swap(lax.dynamic_slice_in_dim(recv_hid, (1 - replica) * share, share, 1))
    own_hid = lax.dynamic_slice_in_dim(recv_hid, replica * share, share, 1)
    grad_down = []
    for rows in recv_out:
        peer_rows = swap(rows)
        own_part = lax.dot_general(
            own_hid, rows, (((0,), (0,)), ((), ())), preferred_element_type=jnp.float32
        ).astype(jnp.bfloat16)
        peer_part = lax.dot_general(
            peer_hid, peer_rows, (((0,), (0,)), ((), ())), preferred_element_type=jnp.float32
        ).astype(jnp.bfloat16)
        summed = own_part.astype(jnp.float32) + peer_part.astype(jnp.float32)
        grad_down.append(summed.astype(jnp.bfloat16))
    grad_down = jnp.concatenate(grad_down, axis=1)[None]

    back_rows = lax.dot_general(
        place,
        came_back.reshape(slot_total, hidden_width),
        (((0,), (0,)), ((), ())),
        preferred_element_type=jnp.float32,
    ).reshape(tok_local, top_count, hidden_width)
    grad_hidden = (gates[:, :, None] * back_rows).astype(jnp.bfloat16)
    grad_gates = jnp.sum(back_rows * hidden.astype(jnp.float32), axis=-1)
    return (grad_hidden, grad_gates, grad_down)


def solution(mesh):
    placed = (
        P(("dp", "far", "near"), None),
        P(("dp", "far", "near"), None, None),
        P(("dp", "far", "near"), None),
        P(("dp", "far", "near"), None),
        P(("far", "near"), None, None),
    )
    return jax.shard_map(
        local,
        mesh=mesh,
        in_specs=placed,
        out_specs=(
            P(("dp", "far", "near"), None, None),
            P(("dp", "far", "near"), None),
            P(("far", "near"), "dp", None),
        ),
        check_vma=False,
    )
```

```python
import functools

import jax
import jax.numpy as jnp
from jax import lax
from jax.experimental import pallas as pl
from jax.experimental.pallas import tpu as pltpu
from jax.sharding import PartitionSpec as P

ID_COLS = 128
ROUNDS = 2
VMEM_LIMIT = 48 * 1024 * 1024


def iota(shape, dim):
    return lax.broadcasted_iota(jnp.int32, shape, dim)


def exact_dot(one_hot, values):
    return jnp.dot(one_hot, values, preferred_element_type=jnp.float32)


def pick_kernel(far_count, near_count, capacity, near_ref, *refs):
    out_ref = refs[-1]
    count = (len(refs) - 1) // 2
    blocks, hids = refs[:count], refs[count:-1]
    tok_local = blocks[0].shape[0]
    width = blocks[0].shape[1] - ID_COLS
    near = near_ref[0]
    cols = count * tok_local
    slots = far_count * count * capacity
    ids = jnp.concatenate([block[:, width:] for block in blocks], axis=0).astype(jnp.float32)
    lead = max(8, far_count)
    ones = jnp.ones((lead, ID_COLS), jnp.bfloat16)
    named = jnp.zeros((lead, cols), jnp.float32)
    for j in range(far_count):
        expert = (j * near_count + near).astype(jnp.float32)
        hit = jnp.where(ids == expert, 1.0, 0.0).astype(jnp.bfloat16)
        line = lax.dot_general(ones, hit, (((1,), (1,)), ((), ())), preferred_element_type=jnp.float32)
        named = jnp.where(iota((lead, cols), 0) == j, line, named)
    row, col = iota((cols, cols), 0), iota((cols, cols), 1)
    before = jnp.where((row < col) & (row // tok_local == col // tok_local), 1.0, 0.0).astype(jnp.bfloat16)
    named = named.astype(jnp.bfloat16)
    rank = exact_dot(named, before).astype(jnp.bfloat16)
    per_far = count * capacity
    spread = jnp.where(iota((slots, lead), 0) // per_far == iota((slots, lead), 1), 1.0, 0.0).astype(jnp.bfloat16)
    slot = iota((slots, cols), 0) % per_far
    pick = (
        (exact_dot(spread, named) > 0.5)
        & (iota((slots, cols), 1) // tok_local == slot // capacity)
        & (exact_dot(spread, rank).astype(jnp.int32) == slot % capacity)
    )
    pick = jnp.where(pick, 1.0, 0.0).astype(jnp.bfloat16)
    step = min(width, 512)
    for start in range(0, width, step):
        tokens = jnp.concatenate([block[:, start : start + step] for block in blocks], axis=0)
        out_ref[:, start : start + step] = exact_dot(pick, tokens).astype(jnp.bfloat16)
    out_row, in_row = iota((slots, slots), 0), iota((slots, slots), 1)
    per_block = far_count * capacity
    source = (
        (out_row % per_far // capacity) * per_block + (out_row // per_far) * capacity + out_row % capacity
    )
    order = jnp.where(in_row == source, 1.0, 0.0).astype(jnp.bfloat16)
    hid = jnp.concatenate([hid[...] for hid in hids], axis=0)
    out_ref[:, width:] = exact_dot(order, hid).astype(jnp.bfloat16)


def returned_kernel(far_count, near_count, capacity, near_ref, rows_ref, weight_ref, *refs):
    earlier, (out_ref, total_ref) = refs[:-2], refs[-2:]
    step = pl.program_id(0)
    tile = weight_ref.shape[1]

    @pl.when(step == 0)
    def _():
        total_ref[...] = jnp.zeros_like(total_ref)

    cols = pl.ds(pl.multiple_of(step * tile, 128), tile)
    total_ref[...] += lax.dot_general(
        rows_ref[:, cols], weight_ref[...], (((1,), (1,)), ((), ())), preferred_element_type=jnp.float32
    )

    @pl.when(step == pl.num_programs(0) - 1)
    def _():
        own = total_ref[...].astype(jnp.bfloat16)
        if not earlier:
            out_ref[...] = own
            return
        rows = jnp.concatenate([ref[...] for ref in earlier] + [own], axis=0)
        total = rows.shape[0]
        near = near_ref[0]
        count = near_count // ROUNDS
        out_row, in_row = iota((total, total), 0), iota((total, total), 1)
        back = lax.rem(near - out_row // capacity % near_count + near_count, near_count)
        source = (
            (back // count) * (far_count * count * capacity)
            + (out_row // (near_count * capacity)) * (count * capacity)
            + (back % count) * capacity
            + out_row % capacity
        )
        order = jnp.where(in_row == source, 1.0, 0.0).astype(jnp.bfloat16)
        out_ref[...] = exact_dot(order, rows).astype(jnp.bfloat16)


def down_kernel(width, replica_ref, *refs):
    rows, (out_ref, turned_ref) = refs[:-2], refs[-2:]
    step = pl.program_id(0)
    share, tile = out_ref.shape
    lines = rows[0].shape[0]

    @pl.when(step == 0)
    def _():
        start = pl.multiple_of(width + replica_ref[0] * share, 128)
        for i, ref in enumerate(rows):
            hid = ref[:, pl.ds(start, share)].astype(jnp.float32)
            turned_ref[:, i * lines : (i + 1) * lines] = hid.T.astype(jnp.bfloat16)

    cols = pl.ds(pl.multiple_of(step * tile, 128), tile)
    tokens = jnp.concatenate([ref[:, cols] for ref in rows], axis=0)
    out_ref[...] = exact_dot(turned_ref[...], tokens).astype(jnp.bfloat16)


def scalar_spec():
    return pl.BlockSpec(memory_space=pltpu.SMEM)


def params():
    return pltpu.CompilerParams(vmem_limit_bytes=VMEM_LIMIT)


def pick_rows(far_count, near_count, capacity, near, blocks, hids):
    width = blocks[0].shape[1] - ID_COLS
    slots = far_count * capacity * len(blocks)
    shape = (slots, width + hids[0].shape[1])
    return pl.pallas_call(
        functools.partial(pick_kernel, far_count, near_count, capacity),
        out_shape=jax.ShapeDtypeStruct(shape, jnp.bfloat16),
        in_specs=[scalar_spec()] + [pl.BlockSpec(memory_space=pltpu.VMEM)] * (2 * len(blocks)),
        out_specs=pl.BlockSpec(memory_space=pltpu.VMEM),
        compiler_params=params(),
        cost_estimate=pl.CostEstimate(flops=2 * slots * 64 * shape[1], bytes_accessed=4 * slots * shape[1], transcendentals=0),
        name="pick_rows",
    )(near, *blocks, *hids)


def returned_rows(far_count, near_count, capacity, near, rows, weight, earlier):
    lines = rows.shape[0]
    hidden_width, width = weight.shape
    tile = min(width, 512)
    total = lines * ROUNDS if earlier else lines
    whole = lambda array: pl.BlockSpec(array.shape, lambda i: (0, 0))
    return pl.pallas_call(
        functools.partial(returned_kernel, far_count, near_count, capacity),
        grid=(width // tile,),
        out_shape=jax.ShapeDtypeStruct((total, hidden_width), jnp.bfloat16),
        in_specs=[scalar_spec(), whole(rows), pl.BlockSpec((hidden_width, tile), lambda i: (0, i))]
        + [whole(array) for array in earlier],
        out_specs=pl.BlockSpec((total, hidden_width), lambda i: (0, 0)),
        scratch_shapes=[pltpu.VMEM((lines, hidden_width), jnp.float32)],
        compiler_params=params(),
        cost_estimate=pl.CostEstimate(
            flops=2 * lines * width * hidden_width, bytes_accessed=2 * width * hidden_width, transcendentals=0
        ),
        name="returned_rows",
    )(near, rows, weight, *earlier)


def down_rows(replica, rows, width, share):
    tile = min(width, 512)
    lines = sum(array.shape[0] for array in rows)
    whole = lambda array: pl.BlockSpec(array.shape, lambda i: (0, 0))
    return pl.pallas_call(
        functools.partial(down_kernel, width),
        grid=(width // tile,),
        out_shape=jax.ShapeDtypeStruct((share, width), jnp.bfloat16),
        in_specs=[scalar_spec()] + [whole(array) for array in rows],
        out_specs=pl.BlockSpec((share, tile), lambda i: (0, i)),
        scratch_shapes=[pltpu.VMEM((share, lines), jnp.bfloat16)],
        compiler_params=params(),
        cost_estimate=pl.CostEstimate(
            flops=2 * lines * width * share, bytes_accessed=2 * width * (lines + share), transcendentals=0
        ),
        name="down_rows",
    )(replica, *rows)


def local(grad_out, hidden, gates, expert_ids, w_down):
    tok_local, top_count = expert_ids.shape
    far_count = lax.axis_size("far")
    near_count = lax.axis_size("near")
    experts = far_count * near_count
    capacity = max(4, (tok_local * top_count + experts - 1) // experts)
    width = grad_out.shape[1]
    hidden_width = hidden.shape[2]
    row_total = tok_local * top_count
    slot_total = experts * capacity
    near = lax.axis_index("near")
    near_ref = near.astype(jnp.int32).reshape(1)
    count = near_count // ROUNDS
    weight = w_down[0]

    def along(array, steps):
        return lax.ppermute(array, "near", [(i, (i + steps) % near_count) for i in range(near_count)])

    def swap(array):
        return lax.ppermute(array, "dp", [(i, i ^ 1) for i in range(lax.axis_size("dp"))])

    id_cols = jnp.pad(
        expert_ids.astype(jnp.bfloat16), ((0, 0), (0, ID_COLS - top_count)), constant_values=-1
    )
    blocks = [jnp.concatenate([grad_out, id_cols], axis=1)]
    for _ in range(1, near_count):
        blocks.append(along(blocks[-1], 1))

    flat_ids = expert_ids.reshape(-1)
    one_hot = (flat_ids[:, None] == jnp.arange(experts, dtype=jnp.int32)[None, :]).astype(jnp.int32)
    ranks = jnp.sum(jnp.cumsum(one_hot, axis=0) * one_hot, axis=1) - 1
    steps = (flat_ids % near_count - near + near_count) % near_count
    out_slots = (steps * far_count + flat_ids // near_count) * capacity + ranks
    back_slots = flat_ids * capacity + ranks
    slot_range = jnp.arange(slot_total, dtype=jnp.int32)[:, None]
    out_place = (slot_range == out_slots[None, :]).astype(jnp.bfloat16)
    back_place = (slot_range == back_slots[None, :]).astype(jnp.bfloat16)
    scaled = (
        (gates[:, :, None] * hidden.astype(jnp.float32))
        .astype(jnp.bfloat16)
        .reshape(row_total, hidden_width)
    )
    send_hid = exact_dot(out_place, scaled).astype(jnp.bfloat16).reshape(near_count, -1, hidden_width)
    hids = [send_hid[0]] + [along(send_hid[step], step) for step in range(1, near_count)]

    rows, peers, returned = [], [], []
    for turn in range(ROUNDS):
        part = slice(turn * count, (turn + 1) * count)
        picked = pick_rows(far_count, near_count, capacity, near_ref, blocks[part], hids[part])
        got = lax.all_to_all(
            picked.reshape(far_count, -1, picked.shape[1]), "far", split_axis=0, concat_axis=0, tiled=True
        ).reshape(picked.shape)
        rows.append(got)
        peers.append(swap(got))
        returned.append(
            returned_rows(
                far_count, near_count, capacity, near_ref, got, weight, returned if turn == ROUNDS - 1 else []
            )
        )
    came_back = lax.all_to_all(
        returned[-1].reshape(experts, capacity, hidden_width),
        ("far", "near"),
        split_axis=0,
        concat_axis=0,
        tiled=True,
    )

    replica = lax.axis_index("dp").astype(jnp.int32).reshape(1)
    grad_down = down_rows(replica, rows + peers, width, hidden_width // lax.axis_size("dp"))
    came_back, grad_down = lax.optimization_barrier((came_back, grad_down))

    back_rows = lax.dot_general(
        back_place,
        came_back.reshape(slot_total, hidden_width),
        (((0,), (0,)), ((), ())),
        preferred_element_type=jnp.float32,
    ).reshape(tok_local, top_count, hidden_width)
    grad_hidden = (gates[:, :, None] * back_rows).astype(jnp.bfloat16)
    grad_gates = jnp.sum(back_rows * hidden.astype(jnp.float32), axis=-1)
    return (grad_hidden, grad_gates, grad_down[None])


def solution(mesh):
    placed = (
        P(("dp", "far", "near"), None),
        P(("dp", "far", "near"), None, None),
        P(("dp", "far", "near"), None),
        P(("dp", "far", "near"), None),
        P(("far", "near"), None, None),
    )
    return jax.shard_map(
        local,
        mesh=mesh,
        in_specs=placed,
        out_specs=(
            P(("dp", "far", "near"), None, None),
            P(("dp", "far", "near"), None),
            P(("far", "near"), "dp", None),
        ),
        check_vma=False,
    )
```

```python
import functools

import jax
import jax.numpy as jnp
from jax import lax
from jax.experimental import pallas as pl
from jax.experimental.pallas import tpu as pltpu
from jax.sharding import PartitionSpec as P

ID_COLS = 128
ROUNDS = 2
VMEM_LIMIT = 48 * 1024 * 1024


def iota(shape, dim):
    return lax.broadcasted_iota(jnp.int32, shape, dim)


def exact_dot(one_hot, values):
    return jnp.dot(one_hot, values, preferred_element_type=jnp.float32)


def send_kernel(far_count, near_count, capacity, near_ref, ids_ref, gates_ref, hidden_ref, *refs):
    sends, back_ref = refs[:-1], refs[-1]
    tok_local, top_count = ids_ref.shape
    hidden_width = hidden_ref.shape[1]
    rows = tok_local * top_count
    experts = far_count * near_count
    slots = experts * capacity
    near = near_ref[0]
    wide = jnp.where(iota((top_count, rows), 1) % top_count == iota((top_count, rows), 0), 1.0, 0.0).astype(jnp.bfloat16)
    mine = iota((tok_local, rows), 1) // top_count == iota((tok_local, rows), 0)

    def line(values):
        spread = jnp.zeros((tok_local, rows), jnp.float32)
        for _ in range(3):
            piece = values.astype(jnp.bfloat16)
            values = values - piece.astype(jnp.float32)
            spread = spread + exact_dot(piece, wide)
        return jnp.sum(jnp.where(mine, spread, 0.0), axis=0, keepdims=True)

    ids = line(ids_ref[...].astype(jnp.float32)).astype(jnp.int32)
    gates = line(gates_ref[...])
    named = iota((experts, rows), 0) == ids
    before = jnp.where(iota((rows, rows), 0) < iota((rows, rows), 1), 1.0, 0.0).astype(jnp.bfloat16)
    counts = exact_dot(jnp.where(named, 1.0, 0.0).astype(jnp.bfloat16), before)
    ranks = jnp.sum(jnp.where(named, counts, 0.0), axis=0, keepdims=True).astype(jnp.int32)
    steps = (ids % near_count - near + near_count) % near_count
    out_slots = (steps * far_count + ids // near_count) * capacity + ranks
    back_slots = ids * capacity + ranks
    back_ref[...] = jnp.where(iota((slots, rows), 0) == back_slots, 1.0, 0.0).astype(jnp.bfloat16)
    lines = far_count * capacity
    tokens = (iota((lines, rows), 1) // top_count + 1).astype(jnp.float32)
    for step, ref in enumerate(sends):
        place = iota((lines, rows), 0) + step * lines == out_slots
        gate = jnp.sum(jnp.where(place, gates, 0.0), axis=1, keepdims=True)
        token = jnp.sum(jnp.where(place, tokens, 0.0), axis=1, keepdims=True) - 1.0
        picked = exact_dot(jnp.where(place, 1.0, 0.0).astype(jnp.bfloat16), hidden_ref[...])
        ref[:, :hidden_width] = (picked * gate).astype(jnp.bfloat16)
        ref[:, hidden_width:] = jnp.broadcast_to(token, (lines, ID_COLS)).astype(jnp.bfloat16)


def pick_kernel(far_count, capacity, *refs):
    out_ref = refs[-1]
    count = (len(refs) - 1) // 2
    blocks, hids = refs[:count], refs[count:-1]
    tok_local, width = blocks[0].shape
    hidden_width = hids[0].shape[1] - ID_COLS
    cols = count * tok_local
    slots = far_count * count * capacity
    per_far, per_block = count * capacity, far_count * capacity
    out_row, in_row = iota((slots, slots), 0), iota((slots, slots), 1)
    source = (
        (out_row % per_far // capacity) * per_block + (out_row // per_far) * capacity + out_row % capacity
    )
    order = jnp.where(in_row == source, 1.0, 0.0).astype(jnp.bfloat16)
    hid = exact_dot(order, jnp.concatenate([hid[...] for hid in hids], axis=0))
    out_ref[:, width:] = hid[:, :hidden_width].astype(jnp.bfloat16)
    token = hid[:, hidden_width : hidden_width + cols].astype(jnp.int32)
    row, col = iota((slots, cols), 0), iota((slots, cols), 1)
    pick = (token == col % tok_local) & (col // tok_local == row % per_far // capacity)
    pick = jnp.where(pick, 1.0, 0.0).astype(jnp.bfloat16)
    step = min(width, 512)
    for start in range(0, width, step):
        tokens = jnp.concatenate([block[:, start : start + step] for block in blocks], axis=0)
        out_ref[:, start : start + step] = exact_dot(pick, tokens).astype(jnp.bfloat16)


def returned_kernel(far_count, near_count, capacity, near_ref, rows_ref, weight_ref, *refs):
    earlier, (out_ref, total_ref) = refs[:-2], refs[-2:]
    step = pl.program_id(0)
    tile = weight_ref.shape[1]

    @pl.when(step == 0)
    def _():
        total_ref[...] = jnp.zeros_like(total_ref)

    cols = pl.ds(pl.multiple_of(step * tile, 128), tile)
    total_ref[...] += lax.dot_general(
        weight_ref[...], rows_ref[:, cols], (((1,), (1,)), ((), ())), preferred_element_type=jnp.float32
    )

    @pl.when(step == pl.num_programs(0) - 1)
    def _():
        own = total_ref[...].T.astype(jnp.bfloat16)
        if not earlier:
            out_ref[...] = own
            return
        rows = jnp.concatenate([ref[...] for ref in earlier] + [own], axis=0)
        total = rows.shape[0]
        near = near_ref[0]
        count = near_count // ROUNDS
        out_row, in_row = iota((total, total), 0), iota((total, total), 1)
        back = lax.rem(near - out_row // capacity % near_count + near_count, near_count)
        source = (
            (back // count) * (far_count * count * capacity)
            + (out_row // (near_count * capacity)) * (count * capacity)
            + (back % count) * capacity
            + out_row % capacity
        )
        order = jnp.where(in_row == source, 1.0, 0.0).astype(jnp.bfloat16)
        out_ref[...] = exact_dot(order, rows).astype(jnp.bfloat16)


def down_kernel(width, replica_ref, *refs):
    rows, (out_ref, turned_ref) = refs[:-2], refs[-2:]
    step = pl.program_id(0)
    share, tile = out_ref.shape
    lines = rows[0].shape[0]

    @pl.when(step == 0)
    def _():
        start = pl.multiple_of(width + replica_ref[0] * share, 128)
        for i, ref in enumerate(rows):
            hid = ref[:, pl.ds(start, share)].astype(jnp.float32)
            turned_ref[:, i * lines : (i + 1) * lines] = hid.T.astype(jnp.bfloat16)

    cols = pl.ds(pl.multiple_of(step * tile, 128), tile)
    tokens = jnp.concatenate([ref[:, cols] for ref in rows], axis=0)
    out_ref[...] = exact_dot(turned_ref[...], tokens).astype(jnp.bfloat16)


def scalar_spec():
    return pl.BlockSpec(memory_space=pltpu.SMEM)


def params():
    return pltpu.CompilerParams(vmem_limit_bytes=VMEM_LIMIT)


def send_rows(far_count, near_count, capacity, near, ids, gates, hidden):
    lines = far_count * capacity
    wide = hidden.shape[1] + ID_COLS
    rows = hidden.shape[0]
    vmem = pl.BlockSpec(memory_space=pltpu.VMEM)
    return pl.pallas_call(
        functools.partial(send_kernel, far_count, near_count, capacity),
        out_shape=[jax.ShapeDtypeStruct((lines, wide), jnp.bfloat16)] * near_count
        + [jax.ShapeDtypeStruct((near_count * lines, rows), jnp.bfloat16)],
        in_specs=[scalar_spec()] + [vmem] * 3,
        out_specs=[vmem] * (near_count + 1),
        compiler_params=params(),
        cost_estimate=pl.CostEstimate(flops=2 * rows * rows * wide, bytes_accessed=4 * rows * wide, transcendentals=0),
        name="send_rows",
    )(near, ids, gates, hidden)


def pick_rows(far_count, capacity, blocks, hids):
    width = blocks[0].shape[1]
    slots = far_count * capacity * len(blocks)
    shape = (slots, width + hids[0].shape[1] - ID_COLS)
    return pl.pallas_call(
        functools.partial(pick_kernel, far_count, capacity),
        out_shape=jax.ShapeDtypeStruct(shape, jnp.bfloat16),
        in_specs=[pl.BlockSpec(memory_space=pltpu.VMEM)] * (2 * len(blocks)),
        out_specs=pl.BlockSpec(memory_space=pltpu.VMEM),
        compiler_params=params(),
        cost_estimate=pl.CostEstimate(flops=2 * slots * 64 * shape[1], bytes_accessed=4 * slots * shape[1], transcendentals=0),
        name="pick_rows",
    )(*blocks, *hids)


def returned_rows(far_count, near_count, capacity, near, rows, weight, earlier):
    lines = rows.shape[0]
    hidden_width, width = weight.shape
    tile = min(width, 512)
    total = lines * ROUNDS if earlier else lines
    whole = lambda array: pl.BlockSpec(array.shape, lambda i: (0, 0))
    return pl.pallas_call(
        functools.partial(returned_kernel, far_count, near_count, capacity),
        grid=(width // tile,),
        out_shape=jax.ShapeDtypeStruct((total, hidden_width), jnp.bfloat16),
        in_specs=[scalar_spec(), whole(rows), pl.BlockSpec((hidden_width, tile), lambda i: (0, i))]
        + [whole(array) for array in earlier],
        out_specs=pl.BlockSpec((total, hidden_width), lambda i: (0, 0)),
        scratch_shapes=[pltpu.VMEM((hidden_width, lines), jnp.float32)],
        compiler_params=params(),
        cost_estimate=pl.CostEstimate(
            flops=2 * lines * width * hidden_width, bytes_accessed=2 * width * hidden_width, transcendentals=0
        ),
        name="returned_rows",
    )(near, rows, weight, *earlier)


def down_rows(replica, rows, width, share):
    tile = min(width, 512)
    lines = sum(array.shape[0] for array in rows)
    whole = lambda array: pl.BlockSpec(array.shape, lambda i: (0, 0))
    return pl.pallas_call(
        functools.partial(down_kernel, width),
        grid=(width // tile,),
        out_shape=jax.ShapeDtypeStruct((share, width), jnp.bfloat16),
        in_specs=[scalar_spec()] + [whole(array) for array in rows],
        out_specs=pl.BlockSpec((share, tile), lambda i: (0, i)),
        scratch_shapes=[pltpu.VMEM((share, lines), jnp.bfloat16)],
        compiler_params=params(),
        cost_estimate=pl.CostEstimate(
            flops=2 * lines * width * share, bytes_accessed=2 * width * (lines + share), transcendentals=0
        ),
        name="down_rows",
    )(replica, *rows)


def local(grad_out, hidden, gates, expert_ids, w_down):
    tok_local, top_count = expert_ids.shape
    far_count = lax.axis_size("far")
    near_count = lax.axis_size("near")
    experts = far_count * near_count
    capacity = max(4, (tok_local * top_count + experts - 1) // experts)
    width = grad_out.shape[1]
    hidden_width = hidden.shape[2]
    row_total = tok_local * top_count
    slot_total = experts * capacity
    near = lax.axis_index("near")
    near_ref = near.astype(jnp.int32).reshape(1)
    count = near_count // ROUNDS
    weight = w_down[0]

    def along(array, steps):
        return lax.ppermute(array, "near", [(i, (i + steps) % near_count) for i in range(near_count)])

    def swap(array):
        return lax.ppermute(array, "dp", [(i, i ^ 1) for i in range(lax.axis_size("dp"))])

    blocks = [grad_out, along(grad_out, 1)]
    *sends, back_place = send_rows(
        far_count, near_count, capacity, near_ref, expert_ids, gates, hidden.reshape(row_total, hidden_width)
    )
    later, sends[1] = lax.optimization_barrier((grad_out, sends[1]))
    hids = [sends[0]] + [along(sends[step], step) for step in range(1, near_count)]
    blocks += [along(later, step) for step in range(2, near_count)]

    rows, peers, returned = [], [], []
    for turn in range(ROUNDS):
        part = slice(turn * count, (turn + 1) * count)
        picked = pick_rows(far_count, capacity, blocks[part], hids[part])
        if rows:
            picked, rows[-1] = lax.optimization_barrier((picked, rows[-1]))
        got = lax.all_to_all(
            picked.reshape(far_count, -1, picked.shape[1]), "far", split_axis=0, concat_axis=0, tiled=True
        ).reshape(picked.shape)
        rows.append(got)
    for turn in range(ROUNDS):
        if returned:
            rows[turn], returned[-1] = lax.optimization_barrier((rows[turn], returned[-1]))
        got = rows[turn]
        peers.append(swap(got))
        returned.append(
            returned_rows(
                far_count, near_count, capacity, near_ref, got, weight, returned if turn == ROUNDS - 1 else []
            )
        )
    came_back = lax.all_to_all(
        returned[-1].reshape(experts, capacity, hidden_width),
        ("far", "near"),
        split_axis=0,
        concat_axis=0,
        tiled=True,
    )

    replica = lax.axis_index("dp").astype(jnp.int32).reshape(1)
    grad_down = down_rows(replica, rows + peers, width, hidden_width // lax.axis_size("dp"))
    came_back, grad_down = lax.optimization_barrier((came_back, grad_down))

    back_rows = lax.dot_general(
        back_place,
        came_back.reshape(slot_total, hidden_width),
        (((0,), (0,)), ((), ())),
        preferred_element_type=jnp.float32,
    ).reshape(tok_local, top_count, hidden_width)
    grad_hidden = (gates[:, :, None] * back_rows).astype(jnp.bfloat16)
    grad_gates = jnp.sum(back_rows * hidden.astype(jnp.float32), axis=-1)
    return (grad_hidden, grad_gates, grad_down[None])


def solution(mesh):
    placed = (
        P(("dp", "far", "near"), None),
        P(("dp", "far", "near"), None, None),
        P(("dp", "far", "near"), None),
        P(("dp", "far", "near"), None),
        P(("far", "near"), None, None),
    )
    return jax.shard_map(
        local,
        mesh=mesh,
        in_specs=placed,
        out_specs=(
            P(("dp", "far", "near"), None, None),
            P(("dp", "far", "near"), None),
            P(("far", "near"), "dp", None),
        ),
        check_vma=False,
    )
```

```python
import functools

import jax
import jax.numpy as jnp
from jax import lax
from jax.experimental import pallas as pl
from jax.experimental.pallas import tpu as pltpu
from jax.sharding import PartitionSpec as P

ID_COLS = 128
VMEM_LIMIT = 48 * 1024 * 1024


def iota(shape, dim):
    return lax.broadcasted_iota(jnp.int32, shape, dim)


def exact_dot(one_hot, values):
    return jnp.dot(one_hot, values, preferred_element_type=jnp.float32)


def send_kernel(far_count, near_count, capacity, near_ref, ids_ref, gates_ref, hidden_ref, *refs):
    sends, back_ref = refs[:-1], refs[-1]
    top_count, tok_local = ids_ref.shape
    hidden_width = hidden_ref.shape[1]
    rows = tok_local * top_count
    experts = far_count * near_count
    slots = experts * capacity
    near = near_ref[0]
    wide = jnp.where(iota((tok_local, rows), 1) // top_count == iota((tok_local, rows), 0), 1.0, 0.0).astype(jnp.bfloat16)
    mine = iota((top_count, rows), 1) % top_count == iota((top_count, rows), 0)

    def line(values):
        spread = jnp.zeros((top_count, rows), jnp.float32)
        for _ in range(3):
            piece = values.astype(jnp.bfloat16)
            values = values - piece.astype(jnp.float32)
            spread = spread + exact_dot(piece, wide)
        return jnp.sum(jnp.where(mine, spread, 0.0), axis=0, keepdims=True)

    ids = line(ids_ref[...].astype(jnp.float32)).astype(jnp.int32)
    gates = line(gates_ref[...])
    named = iota((experts, rows), 0) == ids
    before = jnp.where(iota((rows, rows), 0) < iota((rows, rows), 1), 1.0, 0.0).astype(jnp.bfloat16)
    counts = exact_dot(jnp.where(named, 1.0, 0.0).astype(jnp.bfloat16), before)
    ranks = jnp.sum(jnp.where(named, counts, 0.0), axis=0, keepdims=True).astype(jnp.int32)
    steps = (ids % near_count - near + near_count) % near_count
    out_slots = (steps * far_count + ids // near_count) * capacity + ranks
    back_slots = ids * capacity + ranks
    back_ref[...] = jnp.where(iota((slots, rows), 0) == back_slots, 1.0, 0.0).astype(jnp.bfloat16)
    lines = far_count * capacity
    tokens = (iota((lines, rows), 1) // top_count + 1).astype(jnp.float32)
    for step, ref in enumerate(sends):
        place = iota((lines, rows), 0) + step * lines == out_slots
        gate = jnp.sum(jnp.where(place, gates, 0.0), axis=1, keepdims=True)
        token = jnp.sum(jnp.where(place, tokens, 0.0), axis=1, keepdims=True) - 1.0
        picked = exact_dot(jnp.where(place, 1.0, 0.0).astype(jnp.bfloat16), hidden_ref[...])
        ref[:, :hidden_width] = (picked * gate).astype(jnp.bfloat16)
        ref[:, hidden_width:] = jnp.broadcast_to(token, (lines, ID_COLS)).astype(jnp.bfloat16)


def pick_kernel(far_count, capacity, *refs):
    out_ref = refs[-1]
    count = (len(refs) - 1) // 2
    blocks, hids = refs[:count], refs[count:-1]
    tok_local, width = blocks[0].shape
    hidden_width = hids[0].shape[1] - ID_COLS
    cols = count * tok_local
    slots = far_count * count * capacity
    per_far, per_block = count * capacity, far_count * capacity
    out_row, in_row = iota((slots, slots), 0), iota((slots, slots), 1)
    source = (
        (out_row % per_far // capacity) * per_block + (out_row // per_far) * capacity + out_row % capacity
    )
    order = jnp.where(in_row == source, 1.0, 0.0).astype(jnp.bfloat16)
    hid = exact_dot(order, jnp.concatenate([hid[...] for hid in hids], axis=0))
    out_ref[:, width:] = hid[:, :hidden_width].astype(jnp.bfloat16)
    token = hid[:, hidden_width : hidden_width + 1].astype(jnp.int32)
    row, col = iota((slots, cols), 0), iota((slots, cols), 1)
    pick = (token == col % tok_local) & (col // tok_local == row % per_far // capacity)
    pick = jnp.where(pick, 1.0, 0.0).astype(jnp.bfloat16)
    step = min(width, 512)
    for start in range(0, width, step):
        tokens = jnp.concatenate([block[:, start : start + step] for block in blocks], axis=0)
        out_ref[:, start : start + step] = exact_dot(pick, tokens).astype(jnp.bfloat16)


def down_kernel(width, replica_ref, *refs):
    rows, (out_ref, turned_ref) = refs[:-2], refs[-2:]
    step = pl.program_id(0)
    share, tile = out_ref.shape

    @pl.when(step == 0)
    def _():
        start = pl.multiple_of(width + replica_ref[0] * share, 128)
        hid = jnp.concatenate([ref[:, pl.ds(start, share)] for ref in rows], axis=0)
        turned_ref[...] = hid.astype(jnp.float32).T.astype(jnp.bfloat16)

    cols = pl.ds(pl.multiple_of(step * tile, 128), tile)
    tokens = jnp.concatenate([ref[:, cols] for ref in rows], axis=0)
    out_ref[...] = exact_dot(turned_ref[...], tokens).astype(jnp.bfloat16)


def scalar_spec():
    return pl.BlockSpec(memory_space=pltpu.SMEM)


def params():
    return pltpu.CompilerParams(vmem_limit_bytes=VMEM_LIMIT)


def send_rows(far_count, near_count, capacity, near, ids, gates, hidden):
    lines = far_count * capacity
    wide = hidden.shape[1] + ID_COLS
    rows = hidden.shape[0]
    vmem = pl.BlockSpec(memory_space=pltpu.VMEM)
    return pl.pallas_call(
        functools.partial(send_kernel, far_count, near_count, capacity),
        out_shape=[jax.ShapeDtypeStruct((lines, wide), jnp.bfloat16)] * near_count
        + [jax.ShapeDtypeStruct((near_count * lines, rows), jnp.bfloat16)],
        in_specs=[scalar_spec()] + [vmem] * 3,
        out_specs=[vmem] * (near_count + 1),
        compiler_params=params(),
        cost_estimate=pl.CostEstimate(flops=2 * rows * rows * wide, bytes_accessed=4 * rows * wide, transcendentals=0),
        name="send_rows",
    )(near, ids, gates, hidden)


def pick_rows(far_count, capacity, blocks, hids):
    width = blocks[0].shape[1]
    slots = far_count * capacity * len(blocks)
    shape = (slots, width + hids[0].shape[1] - ID_COLS)
    return pl.pallas_call(
        functools.partial(pick_kernel, far_count, capacity),
        out_shape=jax.ShapeDtypeStruct(shape, jnp.bfloat16),
        in_specs=[pl.BlockSpec(memory_space=pltpu.VMEM)] * (2 * len(blocks)),
        out_specs=pl.BlockSpec(memory_space=pltpu.VMEM),
        compiler_params=params(),
        cost_estimate=pl.CostEstimate(flops=2 * slots * 64 * shape[1], bytes_accessed=4 * slots * shape[1], transcendentals=0),
        name="pick_rows",
    )(*blocks, *hids)


def back_order(far_count, near_count, capacity, near, groups):
    slots = far_count * near_count * capacity
    row = jnp.arange(slots, dtype=jnp.int32)
    far, rank = row // (near_count * capacity), row % capacity
    step = (near - row // capacity % near_count + near_count) % near_count
    source = jnp.zeros_like(row)
    start = 0
    for group in groups:
        count = len(group)
        place = start + (far * count + step - group[0]) * capacity + rank
        source = jnp.where((step >= group[0]) & (step <= group[-1]), place, source)
        start += far_count * count * capacity
    return (source[:, None] == row[None, :]).astype(jnp.bfloat16)


def down_rows(replica, rows, width, share):
    tile = min(width, 512)
    lines = sum(array.shape[0] for array in rows)
    whole = lambda array: pl.BlockSpec(array.shape, lambda i: (0, 0))
    return pl.pallas_call(
        functools.partial(down_kernel, width),
        grid=(width // tile,),
        out_shape=jax.ShapeDtypeStruct((share, width), jnp.bfloat16),
        in_specs=[scalar_spec()] + [whole(array) for array in rows],
        out_specs=pl.BlockSpec((share, tile), lambda i: (0, i)),
        scratch_shapes=[pltpu.VMEM((share, lines), jnp.bfloat16)],
        compiler_params=params(),
        cost_estimate=pl.CostEstimate(
            flops=2 * lines * width * share, bytes_accessed=2 * width * (lines + share), transcendentals=0
        ),
        name="down_rows",
    )(replica, *rows)


def local(grad_out, hidden, gates, expert_ids, w_down):
    tok_local, top_count = expert_ids.shape
    far_count = lax.axis_size("far")
    near_count = lax.axis_size("near")
    experts = far_count * near_count
    capacity = max(4, (tok_local * top_count + experts - 1) // experts)
    width = grad_out.shape[1]
    hidden_width = hidden.shape[2]
    row_total = tok_local * top_count
    slot_total = experts * capacity
    near = lax.axis_index("near")
    near_ref = near.astype(jnp.int32).reshape(1)
    groups = [list(range(near_count - 1)), [near_count - 1]]
    weight = w_down[0]

    def along(array, steps):
        return lax.ppermute(array, "near", [(i, (i + steps) % near_count) for i in range(near_count)])

    def swap(array):
        return lax.ppermute(array, "dp", [(i, i ^ 1) for i in range(lax.axis_size("dp"))])

    blocks = [grad_out, along(grad_out, 1)]
    *sends, back_place = send_rows(
        far_count, near_count, capacity, near_ref, expert_ids.T, gates.T, hidden.reshape(row_total, hidden_width)
    )
    blocks[1], sends[1] = lax.optimization_barrier((blocks[1], sends[1]))
    for _ in range(2, near_count):
        blocks.append(along(blocks[-1], 1))
    hids = [sends[0]] + [along(sends[step], step) for step in range(1, near_count)]

    rows, peers, returned = [], [], []
    for group in groups:
        picked = pick_rows(far_count, capacity, [blocks[step] for step in group], [hids[step] for step in group])
        if rows:
            picked, rows[-1] = lax.optimization_barrier((picked, rows[-1]))
        got = lax.all_to_all(
            picked.reshape(far_count, -1, picked.shape[1]), "far", split_axis=0, concat_axis=0, tiled=True
        ).reshape(picked.shape)
        rows.append(got)
    for turn in range(len(rows)):
        if returned:
            rows[turn], returned[-1] = lax.optimization_barrier((rows[turn], returned[-1]))
        got = rows[turn]
        peers.append(swap(got))
        returned.append(
            lax.dot_general(
                got[:, :width], weight, (((1,), (1,)), ((), ())), preferred_element_type=jnp.float32
            ).astype(jnp.bfloat16)
        )
    order = back_order(far_count, near_count, capacity, near, groups)
    returned = exact_dot(order, jnp.concatenate(returned, axis=0)).astype(jnp.bfloat16)
    came_back = lax.all_to_all(
        returned.reshape(experts, capacity, hidden_width),
        ("far", "near"),
        split_axis=0,
        concat_axis=0,
        tiled=True,
    )

    replica = lax.axis_index("dp").astype(jnp.int32).reshape(1)
    grad_down = down_rows(replica, rows + peers, width, hidden_width // lax.axis_size("dp"))
    came_back, grad_down = lax.optimization_barrier((came_back, grad_down))

    back_rows = lax.dot_general(
        back_place,
        came_back.reshape(slot_total, hidden_width),
        (((0,), (0,)), ((), ())),
        preferred_element_type=jnp.float32,
    ).reshape(tok_local, top_count, hidden_width)
    grad_hidden = (gates[:, :, None] * back_rows).astype(jnp.bfloat16)
    grad_gates = jnp.sum(back_rows * hidden.astype(jnp.float32), axis=-1)
    return (grad_hidden, grad_gates, grad_down[None])


def solution(mesh):
    placed = (
        P(("dp", "far", "near"), None),
        P(("dp", "far", "near"), None, None),
        P(("dp", "far", "near"), None),
        P(("dp", "far", "near"), None),
        P(("far", "near"), None, None),
    )
    return jax.shard_map(
        local,
        mesh=mesh,
        in_specs=placed,
        out_specs=(
            P(("dp", "far", "near"), None, None),
            P(("dp", "far", "near"), None),
            P(("far", "near"), "dp", None),
        ),
        check_vma=False,
    )
```

```python
import functools

import jax
import jax.numpy as jnp
from jax import lax
from jax.experimental import pallas as pl
from jax.experimental.pallas import tpu as pltpu
from jax.sharding import PartitionSpec as P

MIB = 1024 * 1024


def iota(shape, dim):
    return lax.broadcasted_iota(jnp.int32, shape, dim)


def exact_dot(one_hot, values):
    return jnp.dot(one_hot, values, preferred_element_type=jnp.float32)


def send_kernel(far_count, near_count, capacity, near_ref, ids_ref, gates_ref, hidden_ref, *refs):
    sends, back_ref = refs[:-1], refs[-1]
    top_count, tok_local = ids_ref.shape
    rows = tok_local * top_count
    experts = far_count * near_count
    slots = experts * capacity
    near = near_ref[0]
    wide = jnp.where(iota((tok_local, rows), 1) // top_count == iota((tok_local, rows), 0), 1.0, 0.0).astype(jnp.bfloat16)
    mine = iota((top_count, rows), 1) % top_count == iota((top_count, rows), 0)

    def line(values):
        spread = jnp.zeros((top_count, rows), jnp.float32)
        for _ in range(3):
            piece = values.astype(jnp.bfloat16)
            values = values - piece.astype(jnp.float32)
            spread = spread + exact_dot(piece, wide)
        return jnp.sum(jnp.where(mine, spread, 0.0), axis=0, keepdims=True)

    ids = line(ids_ref[...].astype(jnp.float32)).astype(jnp.int32)
    gates = line(gates_ref[...])
    named = iota((experts, rows), 0) == ids
    before = jnp.where(iota((rows, rows), 0) < iota((rows, rows), 1), 1.0, 0.0).astype(jnp.bfloat16)
    counts = exact_dot(jnp.where(named, 1.0, 0.0).astype(jnp.bfloat16), before)
    ranks = jnp.sum(jnp.where(named, counts, 0.0), axis=0, keepdims=True).astype(jnp.int32)
    steps = (ids % near_count - near + near_count) % near_count
    out_slots = (steps * far_count + ids // near_count) * capacity + ranks
    back_slots = ids * capacity + ranks
    back_ref[...] = jnp.where(iota((slots, rows), 0) == back_slots, 1.0, 0.0).astype(jnp.bfloat16)
    lines = far_count * capacity
    for step, ref in enumerate(sends):
        place = iota((lines, rows), 0) + step * lines == out_slots
        gate = jnp.sum(jnp.where(place, gates, 0.0), axis=1, keepdims=True)
        picked = exact_dot(jnp.where(place, 1.0, 0.0).astype(jnp.bfloat16), hidden_ref[...])
        ref[...] = (picked * gate).astype(jnp.bfloat16)


def pick_kernel(far_count, near_count, capacity, count, near_ref, *refs):
    ids, blocks, hids, out_ref = refs[:count], refs[count : 2 * count], refs[2 * count : -1], refs[-1]
    tok_local, width = blocks[0].shape
    cols = count * tok_local
    slots = far_count * count * capacity
    near = near_ref[0]
    ids = jnp.concatenate([ref[...] for ref in ids], axis=1)
    lead = max(8, far_count)
    named = jnp.zeros((lead, cols), jnp.float32)
    for far in range(far_count):
        hit = jnp.where(ids == far * near_count + near, 1.0, 0.0)
        named = jnp.where(iota((lead, cols), 0) == far, jnp.sum(hit, axis=0, keepdims=True), named)
    row, col = iota((cols, cols), 0), iota((cols, cols), 1)
    before = jnp.where((row < col) & (row // tok_local == col // tok_local), 1.0, 0.0).astype(jnp.bfloat16)
    named = named.astype(jnp.bfloat16)
    rank = exact_dot(named, before)
    place = jnp.where(named.astype(jnp.float32) > 0.5, rank, float(capacity)).astype(jnp.bfloat16)
    per_far = count * capacity
    spread = jnp.where(iota((slots, lead), 0) // per_far == iota((slots, lead), 1), 1.0, 0.0).astype(jnp.bfloat16)
    slot = iota((slots, cols), 0) % per_far
    pick = (iota((slots, cols), 1) // tok_local == slot // capacity) & (
        exact_dot(spread, place).astype(jnp.int32) == slot % capacity
    )
    pick = jnp.where(pick, 1.0, 0.0).astype(jnp.bfloat16)
    step = min(width, 512)
    for start in range(0, width, step):
        tokens = jnp.concatenate([block[:, start : start + step] for block in blocks], axis=0)
        out_ref[:, start : start + step] = exact_dot(pick, tokens).astype(jnp.bfloat16)
    for i, hid in enumerate(hids):
        start = width + i * hid.shape[1]
        out_ref[:, start : start + hid.shape[1]] = hid[...]


def down_kernel(far_count, capacity, width, replica_ref, *refs):
    rows, (out_ref, turned_ref) = refs[:-2], refs[-2:]
    step = pl.program_id(0)
    share, tile = out_ref.shape

    @pl.when(step == 0)
    def _():
        hids = []
        for early, late in (rows[:2], rows[2:]):
            lines, last = early.shape[0], late.shape[0]
            count = lines // last
            hidden_width = (late.shape[1] - width) // (count + 1)
            row, col = iota((lines, last), 0), iota((lines, last), 1)
            match = (row // (count * capacity) == col // capacity) & (row % capacity == col % capacity)
            total = jnp.zeros((lines, share), jnp.float32)
            for i in range(count + 1):
                start = pl.multiple_of(width + i * hidden_width + replica_ref[0] * share, 128)
                hid = late[:, pl.ds(start, share)]
                if i < count:
                    order = jnp.where(match & (row // capacity % count == i), 1.0, 0.0).astype(jnp.bfloat16)
                    total = total + exact_dot(order, hid)
                else:
                    hids += [total, hid.astype(jnp.float32)]
        turned_ref[...] = jnp.concatenate(hids, axis=0).T.astype(jnp.bfloat16)

    cols = pl.ds(pl.multiple_of(step * tile, 128), tile)
    tokens = jnp.concatenate([ref[:, cols] for ref in rows], axis=0)
    out_ref[...] = exact_dot(turned_ref[...], tokens).astype(jnp.bfloat16)


def scalar_spec():
    return pl.BlockSpec(memory_space=pltpu.SMEM)


def params(mib):
    return pltpu.CompilerParams(vmem_limit_bytes=mib * MIB)


def send_rows(far_count, near_count, capacity, near, ids, gates, hidden):
    lines = far_count * capacity
    rows, wide = hidden.shape
    vmem = pl.BlockSpec(memory_space=pltpu.VMEM)
    return pl.pallas_call(
        functools.partial(send_kernel, far_count, near_count, capacity),
        out_shape=[jax.ShapeDtypeStruct((lines, wide), jnp.bfloat16)] * near_count
        + [jax.ShapeDtypeStruct((near_count * lines, rows), jnp.bfloat16)],
        in_specs=[scalar_spec()] + [vmem] * 3,
        out_specs=[vmem] * (near_count + 1),
        compiler_params=params(12),
        cost_estimate=pl.CostEstimate(flops=2 * rows * rows * wide, bytes_accessed=4 * rows * wide, transcendentals=0),
        name="send_rows",
    )(near, ids, gates, hidden)


def pick_rows(far_count, near_count, capacity, near, ids, blocks, hids):
    width = blocks[0].shape[1]
    slots = far_count * capacity * len(blocks)
    shape = (slots, width + sum(hid.shape[1] for hid in hids))
    operands = ids + blocks + hids
    return pl.pallas_call(
        functools.partial(pick_kernel, far_count, near_count, capacity, len(blocks)),
        out_shape=jax.ShapeDtypeStruct(shape, jnp.bfloat16),
        in_specs=[scalar_spec()] + [pl.BlockSpec(memory_space=pltpu.VMEM)] * len(operands),
        out_specs=pl.BlockSpec(memory_space=pltpu.VMEM),
        compiler_params=params(16),
        cost_estimate=pl.CostEstimate(flops=2 * slots * 64 * shape[1], bytes_accessed=4 * slots * shape[1], transcendentals=0),
        name="pick_rows",
    )(near, *operands)


def back_order(far_count, near_count, capacity, near, groups):
    slots = far_count * near_count * capacity
    row = jnp.arange(slots, dtype=jnp.int32)
    far, rank = row // (near_count * capacity), row % capacity
    step = (near - row // capacity % near_count + near_count) % near_count
    source = jnp.zeros_like(row)
    start = 0
    for group in groups:
        count = len(group)
        place = start + (far * count + step - group[0]) * capacity + rank
        source = jnp.where((step >= group[0]) & (step <= group[-1]), place, source)
        start += far_count * count * capacity
    return (source[:, None] == row[None, :]).astype(jnp.bfloat16)


def down_rows(far_count, capacity, replica, rows, width, share):
    tile = min(width, 512)
    lines = sum(array.shape[0] for array in rows)
    whole = lambda array: pl.BlockSpec(array.shape, lambda i: (0, 0))
    return pl.pallas_call(
        functools.partial(down_kernel, far_count, capacity, width),
        grid=(width // tile,),
        out_shape=jax.ShapeDtypeStruct((share, width), jnp.bfloat16),
        in_specs=[scalar_spec()] + [whole(array) for array in rows],
        out_specs=pl.BlockSpec((share, tile), lambda i: (0, i)),
        scratch_shapes=[pltpu.VMEM((share, lines), jnp.bfloat16)],
        compiler_params=params(32),
        cost_estimate=pl.CostEstimate(
            flops=2 * lines * width * share, bytes_accessed=2 * width * (lines + share), transcendentals=0
        ),
        name="down_rows",
    )(replica, *rows)


def local(grad_out, hidden, gates, expert_ids, w_down):
    tok_local, top_count = expert_ids.shape
    far_count = lax.axis_size("far")
    near_count = lax.axis_size("near")
    experts = far_count * near_count
    capacity = max(4, (tok_local * top_count + experts - 1) // experts)
    width = grad_out.shape[1]
    hidden_width = hidden.shape[2]
    row_total = tok_local * top_count
    slot_total = experts * capacity
    near = lax.axis_index("near")
    near_ref = near.astype(jnp.int32).reshape(1)
    groups = [list(range(near_count - 1)), [near_count - 1]]
    weight = w_down[0]

    def along(array, steps):
        return lax.ppermute(array, "near", [(i, (i + steps) % near_count) for i in range(near_count)])

    def swap(array):
        return lax.ppermute(array, "dp", [(i, i ^ 1) for i in range(lax.axis_size("dp"))])

    blocks = [grad_out]
    for _ in range(1, near_count):
        blocks.append(along(blocks[-1], 1))
    ids = [expert_ids.T] + [along(expert_ids.T, step) for step in range(1, near_count)]
    *sends, back_place = send_rows(
        far_count, near_count, capacity, near_ref, ids[0], gates.T, hidden.reshape(row_total, hidden_width)
    )
    rows, peers, returned = [], [], []
    for group in groups:
        hids = []
        if rows:
            hids = [sends[0]] + [along(sends[step], step) for step in range(1, near_count)]
        picked = pick_rows(
            far_count,
            near_count,
            capacity,
            near_ref,
            [ids[step] for step in group],
            [blocks[step] for step in group],
            hids,
        )
        if rows:
            picked, rows[-1] = lax.optimization_barrier((picked, rows[-1]))
        else:
            picked, sends = lax.optimization_barrier((picked, sends))
        got = lax.all_to_all(
            picked.reshape(far_count, -1, picked.shape[1]), "far", split_axis=0, concat_axis=0, tiled=True
        ).reshape(picked.shape)
        rows.append(got)
    for turn in range(len(rows)):
        if returned:
            rows[turn], returned[-1] = lax.optimization_barrier((rows[turn], returned[-1]))
        got = rows[turn]
        peers.append(swap(got))
        returned.append(
            lax.dot_general(
                got[:, :width], weight, (((1,), (1,)), ((), ())), preferred_element_type=jnp.float32
            ).astype(jnp.bfloat16)
        )
    order = back_order(far_count, near_count, capacity, near, groups)
    returned = exact_dot(order, jnp.concatenate(returned, axis=0)).astype(jnp.bfloat16)
    came_back = lax.all_to_all(
        returned.reshape(experts, capacity, hidden_width),
        ("far", "near"),
        split_axis=0,
        concat_axis=0,
        tiled=True,
    )

    replica = lax.axis_index("dp").astype(jnp.int32).reshape(1)
    grad_down = down_rows(
        far_count, capacity, replica, rows + peers, width, hidden_width // lax.axis_size("dp")
    )
    came_back, grad_down = lax.optimization_barrier((came_back, grad_down))

    back_rows = lax.dot_general(
        back_place,
        came_back.reshape(slot_total, hidden_width),
        (((0,), (0,)), ((), ())),
        preferred_element_type=jnp.float32,
    ).reshape(tok_local, top_count, hidden_width)
    grad_hidden = (gates[:, :, None] * back_rows).astype(jnp.bfloat16)
    grad_gates = jnp.sum(back_rows * hidden.astype(jnp.float32), axis=-1)
    return (grad_hidden, grad_gates, grad_down[None])


def solution(mesh):
    placed = (
        P(("dp", "far", "near"), None),
        P(("dp", "far", "near"), None, None),
        P(("dp", "far", "near"), None),
        P(("dp", "far", "near"), None),
        P(("far", "near"), None, None),
    )
    return jax.shard_map(
        local,
        mesh=mesh,
        in_specs=placed,
        out_specs=(
            P(("dp", "far", "near"), None, None),
            P(("dp", "far", "near"), None),
            P(("far", "near"), "dp", None),
        ),
        check_vma=False,
    )
```

```python
import functools

import jax
import jax.numpy as jnp
from jax import lax
from jax.experimental import pallas as pl
from jax.experimental.pallas import tpu as pltpu
from jax.sharding import PartitionSpec as P

MIB = 1024 * 1024


def iota(shape, dim):
    return lax.broadcasted_iota(jnp.int32, shape, dim)


def exact_dot(one_hot, values):
    return jnp.dot(one_hot, values, preferred_element_type=jnp.float32)


def send_kernel(far_count, near_count, capacity, near_ref, ids_ref, gates_ref, hidden_ref, send_ref, back_ref):
    top_count, tok_local = ids_ref.shape
    rows = tok_local * top_count
    experts = far_count * near_count
    slots = experts * capacity
    near = near_ref[0]
    wide = jnp.where(iota((tok_local, rows), 1) // top_count == iota((tok_local, rows), 0), 1.0, 0.0).astype(jnp.bfloat16)
    mine = iota((top_count, rows), 1) % top_count == iota((top_count, rows), 0)

    def line(values):
        spread = jnp.zeros((top_count, rows), jnp.float32)
        for _ in range(3):
            piece = values.astype(jnp.bfloat16)
            values = values - piece.astype(jnp.float32)
            spread = spread + exact_dot(piece, wide)
        return jnp.sum(jnp.where(mine, spread, 0.0), axis=0, keepdims=True)

    ids = line(ids_ref[...].astype(jnp.float32)).astype(jnp.int32)
    gates = line(gates_ref[...])
    named = iota((experts, rows), 0) == ids
    before = jnp.where(iota((rows, rows), 0) < iota((rows, rows), 1), 1.0, 0.0).astype(jnp.bfloat16)
    counts = exact_dot(jnp.where(named, 1.0, 0.0).astype(jnp.bfloat16), before)
    ranks = jnp.sum(jnp.where(named, counts, 0.0), axis=0, keepdims=True).astype(jnp.int32)
    steps = (ids % near_count - near + near_count) % near_count
    out_slots = (ids // near_count * near_count + steps) * capacity + ranks
    back_slots = ids * capacity + ranks
    back_ref[...] = jnp.where(iota((slots, rows), 0) == back_slots, 1.0, 0.0).astype(jnp.bfloat16)
    place = iota((slots, rows), 0) == out_slots
    gate = jnp.sum(jnp.where(place, gates, 0.0), axis=1, keepdims=True)
    picked = exact_dot(jnp.where(place, 1.0, 0.0).astype(jnp.bfloat16), hidden_ref[...])
    send_ref[...] = (picked * gate).astype(jnp.bfloat16)


def plan_kernel(far_count, near_count, capacity, groups, near_ref, *refs):
    all_ids, outs = refs[: -len(groups)], refs[-len(groups) :]
    tok_local = all_ids[0].shape[1]
    near = near_ref[0]
    lead = max(8, far_count)
    for group, out_ref in zip(groups, outs):
        count = len(group)
        slots, cols = out_ref.shape
        ids = jnp.concatenate([all_ids[step][...] for step in group], axis=1)
        named = jnp.zeros((lead, cols), jnp.float32)
        for far in range(far_count):
            hit = jnp.where(ids == far * near_count + near, 1.0, 0.0)
            named = jnp.where(iota((lead, cols), 0) == far, jnp.sum(hit, axis=0, keepdims=True), named)
        row, col = iota((cols, cols), 0), iota((cols, cols), 1)
        before = jnp.where((row < col) & (row // tok_local == col // tok_local), 1.0, 0.0).astype(jnp.bfloat16)
        rank = exact_dot(named.astype(jnp.bfloat16), before)
        place = jnp.where(named > 0.5, rank, float(capacity)).astype(jnp.bfloat16)
        per_far = count * capacity
        spread = jnp.where(iota((slots, lead), 0) // per_far == iota((slots, lead), 1), 1.0, 0.0).astype(jnp.bfloat16)
        slot = iota((slots, cols), 0) % per_far
        pick = (iota((slots, cols), 1) // tok_local == slot // capacity) & (
            exact_dot(spread, place).astype(jnp.int32) == slot % capacity
        )
        out_ref[...] = jnp.where(pick, 1.0, 0.0).astype(jnp.bfloat16)


def pick_kernel(pick_ref, *refs):
    blocks, (out_ref, first_ref, sem) = refs[:-3], refs[-3:]
    copy = pltpu.make_async_copy(blocks[0], first_ref, sem)
    copy.start()
    copy.wait()
    width = first_ref.shape[1]
    step = min(width, 512)
    for start in range(0, width, step):
        tokens = [first_ref[:, start : start + step]] + [block[:, start : start + step] for block in blocks[1:]]
        out_ref[:, start : start + step] = exact_dot(pick_ref[...], jnp.concatenate(tokens, axis=0)).astype(jnp.bfloat16)


def join_kernel(*refs):
    out_ref = refs[-1]
    start = 0
    for ref in refs[:-1]:
        out_ref[:, start : start + ref.shape[1]] = ref[...]
        start += ref.shape[1]


def hold_kernel(weight_ref, out_ref, sem):
    copy = pltpu.make_async_copy(weight_ref, out_ref, sem)
    copy.start()
    copy.wait()


def down_kernel(capacity, replica_ref, *refs):
    rows, (out_ref, turned_ref) = refs[:-2], refs[-2:]
    step = pl.program_id(0)
    share, tile = out_ref.shape

    @pl.when(step == 0)
    def _():
        hids = []
        for early, late in ((rows[0], rows[2]), (rows[3], rows[5])):
            lines, last = early.shape[0], late.shape[0]
            count = lines // last
            hidden_width = late.shape[1] // (count + 1)
            row, col = iota((lines, last), 0), iota((lines, last), 1)
            match = (row // (count * capacity) == col // capacity) & (row % capacity == col % capacity)
            total = jnp.zeros((lines, share), jnp.float32)
            for i in range(count + 1):
                start = pl.multiple_of(i * hidden_width + replica_ref[0] * share, 128)
                hid = late[:, pl.ds(start, share)]
                if i < count:
                    order = jnp.where(match & (row // capacity % count == i), 1.0, 0.0).astype(jnp.bfloat16)
                    total = total + exact_dot(order, hid)
                else:
                    hids += [total, hid.astype(jnp.float32)]
        turned_ref[...] = jnp.concatenate(hids, axis=0).T.astype(jnp.bfloat16)

    cols = pl.ds(pl.multiple_of(step * tile, 128), tile)
    tokens = jnp.concatenate([rows[i][:, cols] for i in (0, 1, 3, 4)], axis=0)
    out_ref[...] = exact_dot(turned_ref[...], tokens).astype(jnp.bfloat16)


def scalar_spec():
    return pl.BlockSpec(memory_space=pltpu.SMEM)


def params(mib):
    return pltpu.CompilerParams(vmem_limit_bytes=mib * MIB)


def send_rows(far_count, near_count, capacity, near, ids, gates, hidden):
    slots = far_count * near_count * capacity
    rows, wide = hidden.shape
    vmem = pl.BlockSpec(memory_space=pltpu.VMEM)
    return pl.pallas_call(
        functools.partial(send_kernel, far_count, near_count, capacity),
        out_shape=[
            jax.ShapeDtypeStruct((slots, wide), jnp.bfloat16),
            jax.ShapeDtypeStruct((slots, rows), jnp.bfloat16),
        ],
        in_specs=[scalar_spec()] + [vmem] * 3,
        out_specs=[vmem] * 2,
        compiler_params=params(12),
        cost_estimate=pl.CostEstimate(flops=2 * rows * rows * wide, bytes_accessed=4 * rows * wide, transcendentals=0),
        name="send_rows",
    )(near, ids, gates, hidden)


def plan_rows(far_count, near_count, capacity, groups, near, ids):
    tok_local = ids[0].shape[1]
    vmem = pl.BlockSpec(memory_space=pltpu.VMEM)
    return pl.pallas_call(
        functools.partial(plan_kernel, far_count, near_count, capacity, groups),
        out_shape=[
            jax.ShapeDtypeStruct((far_count * len(group) * capacity, len(group) * tok_local), jnp.bfloat16)
            for group in groups
        ],
        in_specs=[scalar_spec()] + [vmem] * len(ids),
        out_specs=[vmem] * len(groups),
        compiler_params=params(12),
        name="plan_rows",
    )(near, *ids)


def pick_rows(pick, blocks):
    width = blocks[0].shape[1]
    slots = pick.shape[0]
    vmem = pl.BlockSpec(memory_space=pltpu.VMEM)
    return pl.pallas_call(
        pick_kernel,
        out_shape=jax.ShapeDtypeStruct((slots, width), jnp.bfloat16),
        in_specs=[vmem, pl.BlockSpec(memory_space=pl.ANY)] + [vmem] * (len(blocks) - 1),
        out_specs=vmem,
        scratch_shapes=[pltpu.VMEM(blocks[0].shape, jnp.bfloat16), pltpu.SemaphoreType.DMA],
        compiler_params=params(12),
        cost_estimate=pl.CostEstimate(flops=2 * slots * 64 * width, bytes_accessed=4 * slots * width, transcendentals=0),
        name="pick_rows",
    )(pick, *blocks)


def join_rows(arrays):
    vmem = pl.BlockSpec(memory_space=pltpu.VMEM)
    shape = (arrays[0].shape[0], sum(array.shape[1] for array in arrays))
    return pl.pallas_call(
        join_kernel,
        out_shape=jax.ShapeDtypeStruct(shape, jnp.bfloat16),
        in_specs=[vmem] * len(arrays),
        out_specs=vmem,
        compiler_params=params(8),
        name="join_rows",
    )(*arrays)


def hold(weight):
    return pl.pallas_call(
        hold_kernel,
        out_shape=jax.ShapeDtypeStruct(weight.shape, weight.dtype),
        in_specs=[pl.BlockSpec(memory_space=pl.ANY)],
        out_specs=pl.BlockSpec(memory_space=pltpu.VMEM),
        scratch_shapes=[pltpu.SemaphoreType.DMA],
        compiler_params=params(14),
        cost_estimate=pl.CostEstimate(flops=0, bytes_accessed=2 * weight.size, transcendentals=0),
        name="hold_weight",
    )(weight)


def back_order(far_count, near_count, capacity, near, groups):
    slots = far_count * near_count * capacity
    row = jnp.arange(slots, dtype=jnp.int32)
    far, rank = row // (near_count * capacity), row % capacity
    step = (near - row // capacity % near_count + near_count) % near_count
    source = jnp.zeros_like(row)
    start = 0
    for group in groups:
        count = len(group)
        place = start + (far * count + step - group[0]) * capacity + rank
        source = jnp.where((step >= group[0]) & (step <= group[-1]), place, source)
        start += far_count * count * capacity
    return (source[:, None] == row[None, :]).astype(jnp.bfloat16)


def down_rows(capacity, replica, rows, share):
    width = rows[0].shape[1]
    tile = min(width, 512)
    lines = sum(rows[i].shape[0] for i in (0, 1, 3, 4))
    whole = lambda array: pl.BlockSpec(array.shape, lambda i: (0, 0))
    return pl.pallas_call(
        functools.partial(down_kernel, capacity),
        grid=(width // tile,),
        out_shape=jax.ShapeDtypeStruct((share, width), jnp.bfloat16),
        in_specs=[scalar_spec()] + [whole(array) for array in rows],
        out_specs=pl.BlockSpec((share, tile), lambda i: (0, i)),
        scratch_shapes=[pltpu.VMEM((share, lines), jnp.bfloat16)],
        compiler_params=params(32),
        cost_estimate=pl.CostEstimate(
            flops=2 * lines * width * share, bytes_accessed=2 * width * (lines + share), transcendentals=0
        ),
        name="down_rows",
    )(replica, *rows)


def local(grad_out, hidden, gates, expert_ids, w_down):
    tok_local, top_count = expert_ids.shape
    far_count = lax.axis_size("far")
    near_count = lax.axis_size("near")
    experts = far_count * near_count
    capacity = max(4, (tok_local * top_count + experts - 1) // experts)
    width = grad_out.shape[1]
    hidden_width = hidden.shape[2]
    row_total = tok_local * top_count
    slot_total = experts * capacity
    near = lax.axis_index("near")
    near_ref = near.astype(jnp.int32).reshape(1)
    groups = [list(range(near_count - 1)), [near_count - 1]]
    weight = w_down[0]

    def along(array, steps):
        return lax.ppermute(array, "near", [(i, (i + steps) % near_count) for i in range(near_count)])

    def swap(array):
        return lax.ppermute(array, "dp", [(i, i ^ 1) for i in range(lax.axis_size("dp"))])

    blocks = [grad_out, along(grad_out, 1)]
    ids = [expert_ids.T] + [along(expert_ids.T, step) for step in range(1, near_count)]
    send, back_place = send_rows(
        far_count, near_count, capacity, near_ref, ids[0], gates.T, hidden.reshape(row_total, hidden_width)
    )
    blocks[1], ids, send = lax.optimization_barrier((blocks[1], ids, send))
    for _ in range(2, near_count):
        blocks.append(along(blocks[-1], 1))
    picks = plan_rows(far_count, near_count, capacity, groups, near_ref, ids)
    weight = hold(weight)
    blocks[-2], picks, weight = lax.optimization_barrier((blocks[-2], picks, weight))
    crossed = lax.all_to_all(
        send.reshape(far_count, -1, hidden_width), "far", split_axis=0, concat_axis=0, tiled=True
    ).reshape(far_count, near_count, capacity, hidden_width)

    rows, returned = [], []
    for pick, group in zip(picks, groups):
        picked = pick_rows(pick, [blocks[step] for step in group])
        if rows:
            picked, rows[-1] = lax.optimization_barrier((picked, rows[-1]))
        else:
            picked, crossed = lax.optimization_barrier((picked, crossed))
        got = lax.all_to_all(
            picked.reshape(far_count, -1, width), "far", split_axis=0, concat_axis=0, tiled=True
        ).reshape(picked.shape)
        rows.append(got)
    hids = [crossed[:, step].reshape(-1, hidden_width) for step in range(near_count)]
    hids = join_rows(hids[:1] + [along(hids[step], step) for step in range(1, near_count)])
    for turn in range(len(rows)):
        if returned:
            rows[turn], returned[-1] = lax.optimization_barrier((rows[turn], returned[-1]))
        returned.append(
            lax.dot_general(
                rows[turn], weight, (((1,), (1,)), ((), ())), preferred_element_type=jnp.float32
            ).astype(jnp.bfloat16)
        )
    rows.append(hids)
    peers = [swap(array) for array in rows]
    order = back_order(far_count, near_count, capacity, near, groups)
    returned = exact_dot(order, jnp.concatenate(returned, axis=0)).astype(jnp.bfloat16)
    came_back = lax.all_to_all(
        returned.reshape(experts, capacity, hidden_width),
        ("far", "near"),
        split_axis=0,
        concat_axis=0,
        tiled=True,
    )

    replica = lax.axis_index("dp").astype(jnp.int32).reshape(1)
    grad_down = down_rows(capacity, replica, rows + peers, hidden_width // lax.axis_size("dp"))
    came_back, grad_down = lax.optimization_barrier((came_back, grad_down))

    back_rows = lax.dot_general(
        back_place,
        came_back.reshape(slot_total, hidden_width),
        (((0,), (0,)), ((), ())),
        preferred_element_type=jnp.float32,
    ).reshape(tok_local, top_count, hidden_width)
    grad_hidden = (gates[:, :, None] * back_rows).astype(jnp.bfloat16)
    grad_gates = jnp.sum(back_rows * hidden.astype(jnp.float32), axis=-1)
    return (grad_hidden, grad_gates, grad_down[None])


def solution(mesh):
    placed = (
        P(("dp", "far", "near"), None),
        P(("dp", "far", "near"), None, None),
        P(("dp", "far", "near"), None),
        P(("dp", "far", "near"), None),
        P(("far", "near"), None, None),
    )
    return jax.shard_map(
        local,
        mesh=mesh,
        in_specs=placed,
        out_specs=(
            P(("dp", "far", "near"), None, None),
            P(("dp", "far", "near"), None),
            P(("far", "near"), "dp", None),
        ),
        check_vma=False,
    )
```

```python
import functools

import jax
import jax.numpy as jnp
from jax import lax
from jax.experimental import pallas as pl
from jax.experimental.pallas import tpu as pltpu
from jax.sharding import PartitionSpec as P

ID_COLS = 128
PARTS = 2
MIB = 1024 * 1024


def iota(shape, dim):
    return lax.broadcasted_iota(jnp.int32, shape, dim)


def exact_dot(one_hot, values):
    return jnp.dot(one_hot, values, preferred_element_type=jnp.float32)


def send_kernel(far_count, near_count, capacity, near_ref, ids_ref, gates_ref, hidden_ref, send_ref, back_ref):
    top_count, tok_local = ids_ref.shape
    rows = tok_local * top_count
    experts = far_count * near_count
    slots = experts * capacity
    near = near_ref[0]
    wide = jnp.where(iota((tok_local, rows), 1) // top_count == iota((tok_local, rows), 0), 1.0, 0.0).astype(jnp.bfloat16)
    mine = iota((top_count, rows), 1) % top_count == iota((top_count, rows), 0)

    def line(values):
        spread = jnp.zeros((top_count, rows), jnp.float32)
        for _ in range(3):
            piece = values.astype(jnp.bfloat16)
            values = values - piece.astype(jnp.float32)
            spread = spread + exact_dot(piece, wide)
        return jnp.sum(jnp.where(mine, spread, 0.0), axis=0, keepdims=True)

    ids = line(ids_ref[...].astype(jnp.float32)).astype(jnp.int32)
    gates = line(gates_ref[...])
    named = iota((experts, rows), 0) == ids
    before = jnp.where(iota((rows, rows), 0) < iota((rows, rows), 1), 1.0, 0.0).astype(jnp.bfloat16)
    counts = exact_dot(jnp.where(named, 1.0, 0.0).astype(jnp.bfloat16), before)
    ranks = jnp.sum(jnp.where(named, counts, 0.0), axis=0, keepdims=True).astype(jnp.int32)
    steps = (ids % near_count - near + near_count) % near_count
    out_slots = (ids // near_count * near_count + steps) * capacity + ranks
    back_slots = ids * capacity + ranks
    back_ref[...] = jnp.where(iota((slots, rows), 0) == back_slots, 1.0, 0.0).astype(jnp.bfloat16)
    place = iota((slots, rows), 0) == out_slots
    gate = jnp.sum(jnp.where(place, gates, 0.0), axis=1, keepdims=True)
    picked = exact_dot(jnp.where(place, 1.0, 0.0).astype(jnp.bfloat16), hidden_ref[...])
    send_ref[...] = (picked * gate).astype(jnp.bfloat16)


def split_kernel(ids_ref, tokens_ref, *refs):
    outs, sem = refs[:-1], refs[-1]
    part = outs[1].shape[1]
    copies = [
        pltpu.make_async_copy(tokens_ref.at[:, i * part : (i + 1) * part], out.at[:, :part], sem.at[i])
        for i, out in enumerate(outs)
    ]
    for copy in copies:
        copy.start()
    top_count, tok_local = ids_ref.shape
    same = jnp.where(iota((top_count, ID_COLS), 0) == iota((top_count, ID_COLS), 1), 1.0, 0.0).astype(jnp.bfloat16)
    ids = lax.dot_general(
        ids_ref[...].astype(jnp.float32).astype(jnp.bfloat16),
        same,
        (((0,), (0,)), ((), ())),
        preferred_element_type=jnp.float32,
    )
    ids = jnp.where(iota((tok_local, ID_COLS), 1) < top_count, ids, -1.0)
    outs[0][:, part:] = ids.astype(jnp.bfloat16)
    for copy in copies:
        copy.wait()


def picked_rows(pick, blocks, out_ref):
    width = out_ref.shape[1]
    step = min(width, 512)
    for start in range(0, width, step):
        tokens = jnp.concatenate([block[:, start : start + step] for block in blocks], axis=0)
        out_ref[:, start : start + step] = exact_dot(pick, tokens).astype(jnp.bfloat16)


def first_pick_kernel(far_count, near_count, capacity, near_ref, *refs):
    blocks, (out_ref, pick_ref) = refs[:-2], refs[-2:]
    tok_local = blocks[0].shape[0]
    width = out_ref.shape[1]
    near = near_ref[0]
    cols = near_count * tok_local
    slots = far_count * near_count * capacity
    lead = max(8, far_count)
    ids = jnp.concatenate([block[:, width:] for block in blocks], axis=0).astype(jnp.float32)
    ones = jnp.ones((lead, ID_COLS), jnp.bfloat16)
    named = jnp.zeros((lead, cols), jnp.float32)
    for far in range(far_count):
        expert = (far * near_count + near).astype(jnp.float32)
        hit = jnp.where(ids == expert, 1.0, 0.0).astype(jnp.bfloat16)
        line = lax.dot_general(ones, hit, (((1,), (1,)), ((), ())), preferred_element_type=jnp.float32)
        named = jnp.where(iota((lead, cols), 0) == far, line, named)
    row, col = iota((cols, cols), 0), iota((cols, cols), 1)
    before = jnp.where((row < col) & (row // tok_local == col // tok_local), 1.0, 0.0).astype(jnp.bfloat16)
    rank = exact_dot(named.astype(jnp.bfloat16), before)
    place = jnp.where(named > 0.5, rank, float(capacity)).astype(jnp.bfloat16)
    per_far = near_count * capacity
    spread = jnp.where(iota((slots, lead), 0) // per_far == iota((slots, lead), 1), 1.0, 0.0).astype(jnp.bfloat16)
    slot = iota((slots, cols), 0) % per_far
    block = (near - slot // capacity + near_count) % near_count
    pick = (iota((slots, cols), 1) // tok_local == block) & (
        exact_dot(spread, place).astype(jnp.int32) == slot % capacity
    )
    pick = jnp.where(pick, 1.0, 0.0).astype(jnp.bfloat16)
    pick_ref[...] = pick
    picked_rows(pick, blocks, out_ref)


def pick_kernel(pick_ref, *refs):
    picked_rows(pick_ref[...], refs[:-1], refs[-1])


def join_kernel(*refs):
    out_ref = refs[-1]
    start = 0
    for ref in refs[:-1]:
        out_ref[:, start : start + ref.shape[1]] = ref[...]
        start += ref.shape[1]


def down_kernel(near_count, capacity, scalars_ref, *refs):
    rows, hids, (out_ref, turned_ref) = refs[: 2 * PARTS], refs[2 * PARTS : -2], refs[-2:]
    step = pl.program_id(0)
    share, tile = out_ref.shape
    near, replica = scalars_ref[0], scalars_ref[1]

    @pl.when(step == 0)
    def _():
        slots, lines = rows[0].shape[0], hids[0].shape[0]
        hidden_width = hids[0].shape[1] // near_count
        row, col = iota((slots, lines), 0), iota((slots, lines), 1)
        match = (row // (near_count * capacity) == col // capacity) & (row % capacity == col % capacity)
        block = (near - row // capacity % near_count + near_count) % near_count
        for i, ref in enumerate(hids):
            total = jnp.zeros((slots, share), jnp.float32)
            for j in range(near_count):
                start = pl.multiple_of(j * hidden_width + replica * share, 128)
                order = jnp.where(match & (block == j), 1.0, 0.0).astype(jnp.bfloat16)
                total = total + exact_dot(order, ref[:, pl.ds(start, share)])
            turned_ref[:, i * slots : (i + 1) * slots] = total.T.astype(jnp.bfloat16)

    steps = rows[0].shape[1] // tile
    for part in range(PARTS):

        @pl.when(step // steps == part)
        def _(part=part):
            cols = pl.ds(pl.multiple_of(step % steps * tile, 128), tile)
            tokens = jnp.concatenate([ref[:, cols] for ref in rows[part::PARTS]], axis=0)
            out_ref[...] = exact_dot(turned_ref[...], tokens).astype(jnp.bfloat16)


def scalar_spec():
    return pl.BlockSpec(memory_space=pltpu.SMEM)


def params(mib):
    return pltpu.CompilerParams(vmem_limit_bytes=mib * MIB)


def send_rows(far_count, near_count, capacity, near, ids, gates, hidden):
    slots = far_count * near_count * capacity
    rows, wide = hidden.shape
    vmem = pl.BlockSpec(memory_space=pltpu.VMEM)
    return pl.pallas_call(
        functools.partial(send_kernel, far_count, near_count, capacity),
        out_shape=[
            jax.ShapeDtypeStruct((slots, wide), jnp.bfloat16),
            jax.ShapeDtypeStruct((slots, rows), jnp.bfloat16),
        ],
        in_specs=[scalar_spec()] + [vmem] * 3,
        out_specs=[vmem] * 2,
        compiler_params=params(12),
        cost_estimate=pl.CostEstimate(flops=2 * rows * rows * wide, bytes_accessed=4 * rows * wide, transcendentals=0),
        name="send_rows",
    )(near, ids, gates, hidden)


def split_rows(ids, tokens):
    tok_local, width = tokens.shape
    part = width // PARTS
    vmem = pl.BlockSpec(memory_space=pltpu.VMEM)
    return pl.pallas_call(
        split_kernel,
        out_shape=[
            jax.ShapeDtypeStruct((tok_local, part + (ID_COLS if i == 0 else 0)), jnp.bfloat16) for i in range(PARTS)
        ],
        in_specs=[vmem, pl.BlockSpec(memory_space=pl.ANY)],
        out_specs=[vmem] * PARTS,
        scratch_shapes=[pltpu.SemaphoreType.DMA((PARTS,))],
        compiler_params=params(8),
        name="split_rows",
    )(ids, tokens)


def first_pick(far_count, near_count, capacity, near, blocks):
    tok_local, wide = blocks[0].shape
    slots = far_count * near_count * capacity
    vmem = pl.BlockSpec(memory_space=pltpu.VMEM)
    return pl.pallas_call(
        functools.partial(first_pick_kernel, far_count, near_count, capacity),
        out_shape=[
            jax.ShapeDtypeStruct((slots, wide - ID_COLS), jnp.bfloat16),
            jax.ShapeDtypeStruct((slots, near_count * tok_local), jnp.bfloat16),
        ],
        in_specs=[scalar_spec()] + [vmem] * len(blocks),
        out_specs=[vmem] * 2,
        compiler_params=params(16),
        name="first_pick",
    )(near, *blocks)


def pick_rows(pick, blocks):
    vmem = pl.BlockSpec(memory_space=pltpu.VMEM)
    return pl.pallas_call(
        pick_kernel,
        out_shape=jax.ShapeDtypeStruct((pick.shape[0], blocks[0].shape[1]), jnp.bfloat16),
        in_specs=[vmem] * (1 + len(blocks)),
        out_specs=vmem,
        compiler_params=params(16),
        name="pick_rows",
    )(pick, *blocks)


def join_rows(arrays):
    vmem = pl.BlockSpec(memory_space=pltpu.VMEM)
    shape = (arrays[0].shape[0], sum(array.shape[1] for array in arrays))
    return pl.pallas_call(
        join_kernel,
        out_shape=jax.ShapeDtypeStruct(shape, jnp.bfloat16),
        in_specs=[vmem] * len(arrays),
        out_specs=vmem,
        compiler_params=params(8),
        name="join_rows",
    )(*arrays)


def down_rows(near_count, capacity, scalars, rows, hids, share):
    part = rows[0].shape[1]
    tile = min(part, 512)
    lines = 2 * rows[0].shape[0]
    width = part * PARTS
    whole = lambda array: pl.BlockSpec(array.shape, lambda i: (0, 0))
    return pl.pallas_call(
        functools.partial(down_kernel, near_count, capacity),
        grid=(width // tile,),
        out_shape=jax.ShapeDtypeStruct((share, width), jnp.bfloat16),
        in_specs=[scalar_spec()] + [whole(array) for array in rows + hids],
        out_specs=pl.BlockSpec((share, tile), lambda i: (0, i)),
        scratch_shapes=[pltpu.VMEM((share, lines), jnp.bfloat16)],
        compiler_params=params(32),
        cost_estimate=pl.CostEstimate(
            flops=2 * lines * width * share, bytes_accessed=2 * width * (lines + share), transcendentals=0
        ),
        name="down_rows",
    )(scalars, *rows, *hids)


def local(grad_out, hidden, gates, expert_ids, w_down):
    tok_local, top_count = expert_ids.shape
    far_count = lax.axis_size("far")
    near_count = lax.axis_size("near")
    experts = far_count * near_count
    capacity = max(4, (tok_local * top_count + experts - 1) // experts)
    width = grad_out.shape[1]
    hidden_width = hidden.shape[2]
    row_total = tok_local * top_count
    slot_total = experts * capacity
    near = lax.axis_index("near")
    near_ref = near.astype(jnp.int32).reshape(1)
    part = width // PARTS
    weight = w_down[0]

    def along(array, steps):
        return lax.ppermute(array, "near", [(i, (i + steps) % near_count) for i in range(near_count)])

    def swap(array):
        return lax.ppermute(array, "dp", [(i, i ^ 1) for i in range(lax.axis_size("dp"))])

    def line(array):
        return [array] + [along(array, step) for step in range(1, near_count)]

    ids = expert_ids.T
    parts = list(split_rows(ids, grad_out))
    blocks = line(parts[0])
    send, back_place = send_rows(
        far_count, near_count, capacity, near_ref, ids, gates.T, hidden.reshape(row_total, hidden_width)
    )
    crossed = lax.all_to_all(
        send.reshape(far_count, -1, hidden_width), "far", split_axis=0, concat_axis=0, tiled=True
    ).reshape(far_count, near_count, capacity, hidden_width)

    rows, total = [], None
    for i in range(PARTS):
        if i == 0:
            picked, pick = first_pick(far_count, near_count, capacity, near_ref, blocks)
            picked, crossed, parts[1] = lax.optimization_barrier((picked, crossed, parts[1]))
        else:
            picked = pick_rows(pick, line(parts[i]))
            picked, rows[-1] = lax.optimization_barrier((picked, rows[-1]))
        got = lax.all_to_all(
            picked.reshape(far_count, -1, part), "far", split_axis=0, concat_axis=0, tiled=True
        ).reshape(slot_total, part)
        rows.append(got)
    rows[0], crossed = lax.optimization_barrier((rows[0], crossed))
    hids = [crossed[:, step].reshape(-1, hidden_width) for step in range(near_count)]
    hids = join_rows(hids[:1] + [along(hids[step], step) for step in range(1, near_count)])
    for i in range(PARTS):
        if i:
            rows[i], total, hids = lax.optimization_barrier((rows[i], total, hids))
        product = lax.dot_general(
            rows[i],
            weight[:, i * part : (i + 1) * part],
            (((1,), (1,)), ((), ())),
            preferred_element_type=jnp.float32,
        )
        total = product if total is None else total + product
    came_back = lax.all_to_all(
        total.astype(jnp.bfloat16).reshape(experts, capacity, hidden_width),
        ("far", "near"),
        split_axis=0,
        concat_axis=0,
        tiled=True,
    )

    scalars = jnp.stack([near, lax.axis_index("dp")]).astype(jnp.int32)
    grad_down = down_rows(
        near_count,
        capacity,
        scalars,
        rows + [swap(array) for array in rows],
        [hids, swap(hids)],
        hidden_width // lax.axis_size("dp"),
    )
    came_back, grad_down = lax.optimization_barrier((came_back, grad_down))

    back_rows = lax.dot_general(
        back_place,
        came_back.reshape(slot_total, hidden_width),
        (((0,), (0,)), ((), ())),
        preferred_element_type=jnp.float32,
    ).reshape(tok_local, top_count, hidden_width)
    grad_hidden = (gates[:, :, None] * back_rows).astype(jnp.bfloat16)
    grad_gates = jnp.sum(back_rows * hidden.astype(jnp.float32), axis=-1)
    return (grad_hidden, grad_gates, grad_down[None])


def solution(mesh):
    placed = (
        P(("dp", "far", "near"), None),
        P(("dp", "far", "near"), None, None),
        P(("dp", "far", "near"), None),
        P(("dp", "far", "near"), None),
        P(("far", "near"), None, None),
    )
    return jax.shard_map(
        local,
        mesh=mesh,
        in_specs=placed,
        out_specs=(
            P(("dp", "far", "near"), None, None),
            P(("dp", "far", "near"), None),
            P(("far", "near"), "dp", None),
        ),
        check_vma=False,
    )
```

```python
import functools

import jax
import jax.numpy as jnp
from jax import lax
from jax.experimental import pallas as pl
from jax.experimental.pallas import tpu as pltpu
from jax.sharding import PartitionSpec as P

ID_COLS = 128
PARTS = 2
MIB = 1024 * 1024


def iota(shape, dim):
    return lax.broadcasted_iota(jnp.int32, shape, dim)


def exact_dot(one_hot, values):
    return jnp.dot(one_hot, values, preferred_element_type=jnp.float32)


def prepare_kernel(far_count, near_count, capacity, near_ref, ids_ref, gates_ref, hidden_hbm, tokens_hbm, *refs):
    outs, (send_ref, back_ref, hidden_ref, sem) = refs[:PARTS], refs[PARTS:]
    part = outs[1].shape[1]
    copies = [
        pltpu.make_async_copy(tokens_hbm.at[:, i * part : (i + 1) * part], out.at[:, :part], sem.at[i])
        for i, out in enumerate(outs)
    ]
    copies.append(pltpu.make_async_copy(hidden_hbm, hidden_ref, sem.at[PARTS]))
    for copy in copies:
        copy.start()
    top_count, tok_local = ids_ref.shape
    rows = tok_local * top_count
    experts = far_count * near_count
    slots = experts * capacity
    near = near_ref[0]
    own_ids = ids_ref[...].astype(jnp.float32)
    same = jnp.where(iota((top_count, ID_COLS), 0) == iota((top_count, ID_COLS), 1), 1.0, 0.0).astype(jnp.bfloat16)
    id_cols = lax.dot_general(
        own_ids.astype(jnp.bfloat16), same, (((0,), (0,)), ((), ())), preferred_element_type=jnp.float32
    )
    id_cols = jnp.where(iota((tok_local, ID_COLS), 1) < top_count, id_cols, -1.0)
    outs[0][:, part:] = id_cols.astype(jnp.bfloat16)
    wide = jnp.where(iota((tok_local, rows), 1) // top_count == iota((tok_local, rows), 0), 1.0, 0.0).astype(jnp.bfloat16)
    mine = iota((top_count, rows), 1) % top_count == iota((top_count, rows), 0)

    def line(values):
        spread = jnp.zeros((top_count, rows), jnp.float32)
        for _ in range(3):
            piece = values.astype(jnp.bfloat16)
            values = values - piece.astype(jnp.float32)
            spread = spread + exact_dot(piece, wide)
        return jnp.sum(jnp.where(mine, spread, 0.0), axis=0, keepdims=True)

    ids = line(own_ids).astype(jnp.int32)
    gates = line(gates_ref[...])
    named = iota((experts, rows), 0) == ids
    before = jnp.where(iota((rows, rows), 0) < iota((rows, rows), 1), 1.0, 0.0).astype(jnp.bfloat16)
    counts = exact_dot(jnp.where(named, 1.0, 0.0).astype(jnp.bfloat16), before)
    ranks = jnp.sum(jnp.where(named, counts, 0.0), axis=0, keepdims=True).astype(jnp.int32)
    steps = (ids % near_count - near + near_count) % near_count
    out_slots = (ids // near_count * near_count + steps) * capacity + ranks
    back_slots = ids * capacity + ranks
    back_ref[...] = jnp.where(iota((slots, rows), 0) == back_slots, 1.0, 0.0).astype(jnp.bfloat16)
    place = iota((slots, rows), 0) == out_slots
    gate = jnp.sum(jnp.where(place, gates, 0.0), axis=1, keepdims=True)
    place = jnp.where(place, 1.0, 0.0).astype(jnp.bfloat16)
    for copy in copies:
        copy.wait()
    send_ref[...] = (exact_dot(place, hidden_ref[...]) * gate).astype(jnp.bfloat16)


def close_kernel(back_ref, came_ref, gates_ref, hidden_hbm, hid_ref, gates_out_ref, hidden_ref, sem):
    copy = pltpu.make_async_copy(hidden_hbm, hidden_ref, sem)
    copy.start()
    top_count, tok_local = gates_ref.shape
    rows = tok_local * top_count
    back = lax.dot_general(
        back_ref[...], came_ref[...], (((0,), (0,)), ((), ())), preferred_element_type=jnp.float32
    )
    mine = iota((tok_local, top_count, tok_local), 0) == iota((tok_local, top_count, tok_local), 2)
    gate = jnp.where(mine, gates_ref[...][None], 0.0).reshape(rows, tok_local)
    gate = jnp.sum(gate, axis=1, keepdims=True)
    hid_ref[...] = (gate * back).astype(jnp.bfloat16)
    copy.wait()
    sums = jnp.sum(back * hidden_ref[...].astype(jnp.float32), axis=1, keepdims=True)
    spread = jnp.broadcast_to(sums, (rows, tok_local)).reshape(tok_local, top_count, tok_local)
    gates_out_ref[...] = jnp.sum(jnp.where(mine, spread, 0.0), axis=0)


def picked_rows(pick, blocks, out_ref):
    width = out_ref.shape[1]
    step = min(width, 512)
    for start in range(0, width, step):
        tokens = jnp.concatenate([block[:, start : start + step] for block in blocks], axis=0)
        out_ref[:, start : start + step] = exact_dot(pick, tokens).astype(jnp.bfloat16)


def first_pick_kernel(far_count, near_count, capacity, near_ref, *refs):
    blocks, (out_ref, pick_ref) = refs[:-2], refs[-2:]
    tok_local = blocks[0].shape[0]
    width = out_ref.shape[1]
    near = near_ref[0]
    cols = near_count * tok_local
    slots = far_count * near_count * capacity
    lead = max(8, far_count)
    ids = jnp.concatenate([block[:, width:] for block in blocks], axis=0).astype(jnp.float32)
    ones = jnp.ones((lead, ID_COLS), jnp.bfloat16)
    named = jnp.zeros((lead, cols), jnp.float32)
    for far in range(far_count):
        expert = (far * near_count + near).astype(jnp.float32)
        hit = jnp.where(ids == expert, 1.0, 0.0).astype(jnp.bfloat16)
        line = lax.dot_general(ones, hit, (((1,), (1,)), ((), ())), preferred_element_type=jnp.float32)
        named = jnp.where(iota((lead, cols), 0) == far, line, named)
    row, col = iota((cols, cols), 0), iota((cols, cols), 1)
    before = jnp.where((row < col) & (row // tok_local == col // tok_local), 1.0, 0.0).astype(jnp.bfloat16)
    rank = exact_dot(named.astype(jnp.bfloat16), before)
    place = jnp.where(named > 0.5, rank, float(capacity)).astype(jnp.bfloat16)
    per_far = near_count * capacity
    spread = jnp.where(iota((slots, lead), 0) // per_far == iota((slots, lead), 1), 1.0, 0.0).astype(jnp.bfloat16)
    slot = iota((slots, cols), 0) % per_far
    block = (near - slot // capacity + near_count) % near_count
    pick = (iota((slots, cols), 1) // tok_local == block) & (
        exact_dot(spread, place).astype(jnp.int32) == slot % capacity
    )
    pick = jnp.where(pick, 1.0, 0.0).astype(jnp.bfloat16)
    pick_ref[...] = pick
    picked_rows(pick, blocks, out_ref)


def pick_kernel(pick_ref, *refs):
    picked_rows(pick_ref[...], refs[:-1], refs[-1])


def join_kernel(*refs):
    out_ref = refs[-1]
    start = 0
    for ref in refs[:-1]:
        out_ref[:, start : start + ref.shape[1]] = ref[...]
        start += ref.shape[1]


def down_kernel(near_count, capacity, scalars_ref, *refs):
    rows, hids, (out_ref, turned_ref) = refs[: 2 * PARTS], refs[2 * PARTS : -2], refs[-2:]
    step = pl.program_id(0)
    share, tile = out_ref.shape
    near, replica = scalars_ref[0], scalars_ref[1]

    @pl.when(step == 0)
    def _():
        slots, lines = rows[0].shape[0], hids[0].shape[0]
        hidden_width = hids[0].shape[1] // near_count
        row, col = iota((slots, lines), 0), iota((slots, lines), 1)
        match = (row // (near_count * capacity) == col // capacity) & (row % capacity == col % capacity)
        block = (near - row // capacity % near_count + near_count) % near_count
        for i, ref in enumerate(hids):
            total = jnp.zeros((slots, share), jnp.float32)
            for j in range(near_count):
                start = pl.multiple_of(j * hidden_width + replica * share, 128)
                order = jnp.where(match & (block == j), 1.0, 0.0).astype(jnp.bfloat16)
                total = total + exact_dot(order, ref[:, pl.ds(start, share)])
            turned_ref[:, i * slots : (i + 1) * slots] = total.T.astype(jnp.bfloat16)

    steps = rows[0].shape[1] // tile
    for part in range(PARTS):

        @pl.when(step // steps == part)
        def _(part=part):
            cols = pl.ds(pl.multiple_of(step % steps * tile, 128), tile)
            tokens = jnp.concatenate([ref[:, cols] for ref in rows[part::PARTS]], axis=0)
            out_ref[...] = exact_dot(turned_ref[...], tokens).astype(jnp.bfloat16)


def scalar_spec():
    return pl.BlockSpec(memory_space=pltpu.SMEM)


def params(mib):
    return pltpu.CompilerParams(vmem_limit_bytes=mib * MIB)


def prepare(far_count, near_count, capacity, near, ids, gates, hidden, tokens):
    slots = far_count * near_count * capacity
    rows, wide = hidden.shape
    tok_local, width = tokens.shape
    part = width // PARTS
    vmem, hbm = pl.BlockSpec(memory_space=pltpu.VMEM), pl.BlockSpec(memory_space=pl.ANY)
    shapes = [(tok_local, part + (ID_COLS if i == 0 else 0)) for i in range(PARTS)] + [(slots, wide), (slots, rows)]
    return pl.pallas_call(
        functools.partial(prepare_kernel, far_count, near_count, capacity),
        out_shape=[jax.ShapeDtypeStruct(shape, jnp.bfloat16) for shape in shapes],
        in_specs=[scalar_spec(), vmem, vmem, hbm, hbm],
        out_specs=[vmem] * len(shapes),
        scratch_shapes=[pltpu.VMEM(hidden.shape, jnp.bfloat16), pltpu.SemaphoreType.DMA((PARTS + 1,))],
        compiler_params=params(12),
        cost_estimate=pl.CostEstimate(flops=2 * rows * rows * wide, bytes_accessed=4 * rows * wide, transcendentals=0),
        name="prepare_rows",
    )(near, ids, gates, hidden, tokens)


def close(back_place, came_back, gates, hidden):
    vmem = pl.BlockSpec(memory_space=pltpu.VMEM)
    return pl.pallas_call(
        close_kernel,
        out_shape=[
            jax.ShapeDtypeStruct(hidden.shape, jnp.bfloat16),
            jax.ShapeDtypeStruct(gates.shape, jnp.float32),
        ],
        in_specs=[vmem, vmem, vmem, pl.BlockSpec(memory_space=pl.ANY)],
        out_specs=[vmem] * 2,
        scratch_shapes=[pltpu.VMEM(hidden.shape, jnp.bfloat16), pltpu.SemaphoreType.DMA],
        compiler_params=params(12),
        name="close_rows",
    )(back_place, came_back, gates, hidden)


def first_pick(far_count, near_count, capacity, near, blocks):
    tok_local, wide = blocks[0].shape
    slots = far_count * near_count * capacity
    vmem = pl.BlockSpec(memory_space=pltpu.VMEM)
    return pl.pallas_call(
        functools.partial(first_pick_kernel, far_count, near_count, capacity),
        out_shape=[
            jax.ShapeDtypeStruct((slots, wide - ID_COLS), jnp.bfloat16),
            jax.ShapeDtypeStruct((slots, near_count * tok_local), jnp.bfloat16),
        ],
        in_specs=[scalar_spec()] + [vmem] * len(blocks),
        out_specs=[vmem] * 2,
        compiler_params=params(16),
        name="first_pick",
    )(near, *blocks)


def pick_rows(pick, blocks):
    vmem = pl.BlockSpec(memory_space=pltpu.VMEM)
    return pl.pallas_call(
        pick_kernel,
        out_shape=jax.ShapeDtypeStruct((pick.shape[0], blocks[0].shape[1]), jnp.bfloat16),
        in_specs=[vmem] * (1 + len(blocks)),
        out_specs=vmem,
        compiler_params=params(16),
        name="pick_rows",
    )(pick, *blocks)


def join_rows(arrays):
    vmem = pl.BlockSpec(memory_space=pltpu.VMEM)
    shape = (arrays[0].shape[0], sum(array.shape[1] for array in arrays))
    return pl.pallas_call(
        join_kernel,
        out_shape=jax.ShapeDtypeStruct(shape, jnp.bfloat16),
        in_specs=[vmem] * len(arrays),
        out_specs=vmem,
        compiler_params=params(8),
        name="join_rows",
    )(*arrays)


def down_rows(near_count, capacity, scalars, rows, hids, share):
    part = rows[0].shape[1]
    tile = min(part, 512)
    lines = 2 * rows[0].shape[0]
    width = part * PARTS
    whole = lambda array: pl.BlockSpec(array.shape, lambda i: (0, 0))
    return pl.pallas_call(
        functools.partial(down_kernel, near_count, capacity),
        grid=(width // tile,),
        out_shape=jax.ShapeDtypeStruct((share, width), jnp.bfloat16),
        in_specs=[scalar_spec()] + [whole(array) for array in rows + hids],
        out_specs=pl.BlockSpec((share, tile), lambda i: (0, i)),
        scratch_shapes=[pltpu.VMEM((share, lines), jnp.bfloat16)],
        compiler_params=params(32),
        cost_estimate=pl.CostEstimate(
            flops=2 * lines * width * share, bytes_accessed=2 * width * (lines + share), transcendentals=0
        ),
        name="down_rows",
    )(scalars, *rows, *hids)


def local(grad_out, hidden, gates, expert_ids, w_down):
    tok_local, top_count = expert_ids.shape
    far_count = lax.axis_size("far")
    near_count = lax.axis_size("near")
    experts = far_count * near_count
    capacity = max(4, (tok_local * top_count + experts - 1) // experts)
    width = grad_out.shape[1]
    hidden_width = hidden.shape[2]
    row_total = tok_local * top_count
    slot_total = experts * capacity
    near = lax.axis_index("near")
    near_ref = near.astype(jnp.int32).reshape(1)
    part = width // PARTS
    weight = w_down[0]

    def along(array, steps):
        return lax.ppermute(array, "near", [(i, (i + steps) % near_count) for i in range(near_count)])

    def swap(array):
        return lax.ppermute(array, "dp", [(i, i ^ 1) for i in range(lax.axis_size("dp"))])

    def line(array):
        return [array] + [along(array, step) for step in range(1, near_count)]

    hidden_rows = hidden.reshape(row_total, hidden_width)
    *parts, send, back_place = prepare(
        far_count, near_count, capacity, near_ref, expert_ids.T, gates.T, hidden_rows, grad_out
    )
    blocks = line(parts[0])
    crossed = lax.all_to_all(
        send.reshape(far_count, -1, hidden_width), "far", split_axis=0, concat_axis=0, tiled=True
    ).reshape(far_count, near_count, capacity, hidden_width)

    rows, total = [], None
    for i in range(PARTS):
        if i == 0:
            picked, pick = first_pick(far_count, near_count, capacity, near_ref, blocks)
            picked, crossed, parts[1] = lax.optimization_barrier((picked, crossed, parts[1]))
        else:
            picked = pick_rows(pick, line(parts[i]))
            picked, rows[-1] = lax.optimization_barrier((picked, rows[-1]))
        got = lax.all_to_all(
            picked.reshape(far_count, -1, part), "far", split_axis=0, concat_axis=0, tiled=True
        ).reshape(slot_total, part)
        rows.append(got)
    rows[0], crossed = lax.optimization_barrier((rows[0], crossed))
    hids = [crossed[:, step].reshape(-1, hidden_width) for step in range(near_count)]
    hids = join_rows(hids[:1] + [along(hids[step], step) for step in range(1, near_count)])
    for i in range(PARTS):
        if i:
            rows[i], total, hids = lax.optimization_barrier((rows[i], total, hids))
        product = lax.dot_general(
            rows[i],
            weight[:, i * part : (i + 1) * part],
            (((1,), (1,)), ((), ())),
            preferred_element_type=jnp.float32,
        )
        total = product if total is None else total + product
    came_back = lax.all_to_all(
        total.astype(jnp.bfloat16).reshape(experts, capacity, hidden_width),
        ("far", "near"),
        split_axis=0,
        concat_axis=0,
        tiled=True,
    )

    scalars = jnp.stack([near, lax.axis_index("dp")]).astype(jnp.int32)
    grad_down = down_rows(
        near_count,
        capacity,
        scalars,
        rows + [swap(array) for array in rows],
        [hids, swap(hids)],
        hidden_width // lax.axis_size("dp"),
    )
    came_back, grad_down = lax.optimization_barrier((came_back, grad_down))

    grad_hidden, grad_gates = close(
        back_place, came_back.reshape(slot_total, hidden_width), gates.T, hidden_rows
    )
    return (grad_hidden.reshape(hidden.shape), grad_gates.T, grad_down[None])


def solution(mesh):
    placed = (
        P(("dp", "far", "near"), None),
        P(("dp", "far", "near"), None, None),
        P(("dp", "far", "near"), None),
        P(("dp", "far", "near"), None),
        P(("far", "near"), None, None),
    )
    return jax.shard_map(
        local,
        mesh=mesh,
        in_specs=placed,
        out_specs=(
            P(("dp", "far", "near"), None, None),
            P(("dp", "far", "near"), None),
            P(("far", "near"), "dp", None),
        ),
        check_vma=False,
    )
```

```python
import functools

import jax
import jax.numpy as jnp
from jax import lax
from jax.experimental import pallas as pl
from jax.experimental.pallas import tpu as pltpu
from jax.sharding import PartitionSpec as P

ID_COLS = 128
PARTS = 2
MIB = 1024 * 1024


def iota(shape, dim):
    return lax.broadcasted_iota(jnp.int32, shape, dim)


def exact_dot(one_hot, values):
    return jnp.dot(one_hot, values, preferred_element_type=jnp.float32)


def prepare_kernel(far_count, near_count, capacity, scalars_ref, ids_hbm, gates_hbm, hidden_hbm, tokens_hbm, *refs):
    outs, sends, (back_ref, ids_ref, gates_ref, hidden_ref, sem) = refs[:PARTS], refs[PARTS:-5], refs[-5:]
    part = outs[1].shape[1]
    copies = [
        pltpu.make_async_copy(tokens_hbm.at[:, i * part : (i + 1) * part], out.at[:, :part], sem.at[i])
        for i, out in enumerate(outs)
    ]
    copies.append(pltpu.make_async_copy(hidden_hbm, hidden_ref, sem.at[PARTS]))
    small = [
        pltpu.make_async_copy(ids_hbm, ids_ref, sem.at[PARTS + 1]),
        pltpu.make_async_copy(gates_hbm, gates_ref, sem.at[PARTS + 2]),
    ]
    for copy in small + copies:
        copy.start()
    top_count, tok_local = ids_ref.shape
    rows = tok_local * top_count
    experts = far_count * near_count
    slots = experts * capacity
    near, own_far = scalars_ref[0], scalars_ref[1]
    for copy in small:
        copy.wait()
    own_ids = ids_ref[...].astype(jnp.float32)
    same = jnp.where(iota((top_count, ID_COLS), 0) == iota((top_count, ID_COLS), 1), 1.0, 0.0).astype(jnp.bfloat16)
    id_cols = lax.dot_general(
        own_ids.astype(jnp.bfloat16), same, (((0,), (0,)), ((), ())), preferred_element_type=jnp.float32
    )
    id_cols = jnp.where(iota((tok_local, ID_COLS), 1) < top_count, id_cols, -1.0)
    outs[0][:, part:] = id_cols.astype(jnp.bfloat16)
    wide = jnp.where(iota((tok_local, rows), 1) // top_count == iota((tok_local, rows), 0), 1.0, 0.0).astype(jnp.bfloat16)
    mine = iota((top_count, rows), 1) % top_count == iota((top_count, rows), 0)

    def line(values):
        spread = jnp.zeros((top_count, rows), jnp.float32)
        for _ in range(3):
            piece = values.astype(jnp.bfloat16)
            values = values - piece.astype(jnp.float32)
            spread = spread + exact_dot(piece, wide)
        return jnp.sum(jnp.where(mine, spread, 0.0), axis=0, keepdims=True)

    ids = line(own_ids).astype(jnp.int32)
    gates = line(gates_ref[...])
    named = iota((experts, rows), 0) == ids
    before = jnp.where(iota((rows, rows), 0) < iota((rows, rows), 1), 1.0, 0.0).astype(jnp.bfloat16)
    counts = exact_dot(jnp.where(named, 1.0, 0.0).astype(jnp.bfloat16), before)
    ranks = jnp.sum(jnp.where(named, counts, 0.0), axis=0, keepdims=True).astype(jnp.int32)
    steps = (ids % near_count - near + near_count) % near_count
    out_slots = ((ids // near_count ^ own_far) * near_count + steps) * capacity + ranks
    back_slots = ids * capacity + ranks
    back_ref[...] = jnp.where(iota((slots, rows), 0) == back_slots, 1.0, 0.0).astype(jnp.bfloat16)
    place = iota((slots, rows), 0) == out_slots
    gate = jnp.sum(jnp.where(place, gates, 0.0), axis=1, keepdims=True)
    place = jnp.where(place, 1.0, 0.0).astype(jnp.bfloat16)
    for copy in copies:
        copy.wait()
    send = (exact_dot(place, hidden_ref[...]) * gate).astype(jnp.bfloat16)
    for i, ref in enumerate(sends):
        ref[...] = send[i * ref.shape[0] : (i + 1) * ref.shape[0]]


def regroup_kernel(far_count, near_count, capacity, *refs):
    ins, outs = refs[:far_count], refs[far_count:]
    rows = jnp.concatenate([ref[...] for ref in ins], axis=0)
    for step, ref in enumerate(outs):
        shape = (ref.shape[0], rows.shape[0])
        row, col = iota(shape, 0), iota(shape, 1)
        source = (row // capacity * near_count + step) * capacity + row % capacity
        ref[...] = exact_dot(jnp.where(col == source, 1.0, 0.0).astype(jnp.bfloat16), rows).astype(jnp.bfloat16)


def close_kernel(back_ref, came_ref, gates_hbm, hidden_hbm, hid_ref, gates_out_ref, gates_ref, hidden_ref, sem):
    copy = pltpu.make_async_copy(hidden_hbm, hidden_ref, sem.at[0])
    small = pltpu.make_async_copy(gates_hbm, gates_ref, sem.at[1])
    small.start()
    copy.start()
    top_count, tok_local = gates_ref.shape
    rows = tok_local * top_count
    back = lax.dot_general(
        back_ref[...], came_ref[...], (((0,), (0,)), ((), ())), preferred_element_type=jnp.float32
    )
    small.wait()
    mine = iota((tok_local, top_count, tok_local), 0) == iota((tok_local, top_count, tok_local), 2)
    gate = jnp.where(mine, gates_ref[...][None], 0.0).reshape(rows, tok_local)
    gate = jnp.sum(gate, axis=1, keepdims=True)
    hid_ref[...] = (gate * back).astype(jnp.bfloat16)
    copy.wait()
    sums = jnp.sum(back * hidden_ref[...].astype(jnp.float32), axis=1, keepdims=True)
    spread = jnp.broadcast_to(sums, (rows, tok_local)).reshape(tok_local, top_count, tok_local)
    gates_out_ref[...] = jnp.sum(jnp.where(mine, spread, 0.0), axis=0)


def picked_rows(pick, blocks, out_ref):
    width = out_ref.shape[1]
    step = min(width, 512)
    for start in range(0, width, step):
        tokens = jnp.concatenate([block[:, start : start + step] for block in blocks], axis=0)
        out_ref[:, start : start + step] = exact_dot(pick, tokens).astype(jnp.bfloat16)


def first_pick_kernel(far_count, near_count, capacity, near_ref, *refs):
    blocks, (out_ref, pick_ref) = refs[:-2], refs[-2:]
    tok_local = blocks[0].shape[0]
    width = out_ref.shape[1]
    near = near_ref[0]
    cols = near_count * tok_local
    slots = far_count * near_count * capacity
    lead = max(8, far_count)
    ids = jnp.concatenate([block[:, width:] for block in blocks], axis=0).astype(jnp.float32)
    ones = jnp.ones((lead, ID_COLS), jnp.bfloat16)
    named = jnp.zeros((lead, cols), jnp.float32)
    for far in range(far_count):
        expert = (far * near_count + near).astype(jnp.float32)
        hit = jnp.where(ids == expert, 1.0, 0.0).astype(jnp.bfloat16)
        line = lax.dot_general(ones, hit, (((1,), (1,)), ((), ())), preferred_element_type=jnp.float32)
        named = jnp.where(iota((lead, cols), 0) == far, line, named)
    row, col = iota((cols, cols), 0), iota((cols, cols), 1)
    before = jnp.where((row < col) & (row // tok_local == col // tok_local), 1.0, 0.0).astype(jnp.bfloat16)
    rank = exact_dot(named.astype(jnp.bfloat16), before)
    place = jnp.where(named > 0.5, rank, float(capacity)).astype(jnp.bfloat16)
    per_far = near_count * capacity
    spread = jnp.where(iota((slots, lead), 0) // per_far == iota((slots, lead), 1), 1.0, 0.0).astype(jnp.bfloat16)
    slot = iota((slots, cols), 0) % per_far
    block = (near - slot // capacity + near_count) % near_count
    pick = (iota((slots, cols), 1) // tok_local == block) & (
        exact_dot(spread, place).astype(jnp.int32) == slot % capacity
    )
    pick = jnp.where(pick, 1.0, 0.0).astype(jnp.bfloat16)
    pick_ref[...] = pick
    picked_rows(pick, blocks, out_ref)


def pick_kernel(pick_ref, *refs):
    picked_rows(pick_ref[...], refs[:-1], refs[-1])


def join_kernel(*refs):
    out_ref = refs[-1]
    start = 0
    for ref in refs[:-1]:
        out_ref[:, start : start + ref.shape[1]] = ref[...]
        start += ref.shape[1]


def down_kernel(near_count, capacity, scalars_ref, *refs):
    rows, hids, (out_ref, turned_ref) = refs[: 2 * PARTS], refs[2 * PARTS : -2], refs[-2:]
    step = pl.program_id(0)
    share, tile = out_ref.shape
    near, far, replica = scalars_ref[0], scalars_ref[1], scalars_ref[2]

    @pl.when(step == 0)
    def _():
        slots, lines = rows[0].shape[0], hids[0].shape[0]
        hidden_width = hids[0].shape[1] // near_count
        row, col = iota((slots, lines), 0), iota((slots, lines), 1)
        match = (row // (near_count * capacity) ^ far == col // capacity) & (row % capacity == col % capacity)
        block = (near - row // capacity % near_count + near_count) % near_count
        for i, ref in enumerate(hids):
            total = jnp.zeros((slots, share), jnp.float32)
            for j in range(near_count):
                start = pl.multiple_of(j * hidden_width + replica * share, 128)
                order = jnp.where(match & (block == j), 1.0, 0.0).astype(jnp.bfloat16)
                total = total + exact_dot(order, ref[:, pl.ds(start, share)])
            turned_ref[:, i * slots : (i + 1) * slots] = total.T.astype(jnp.bfloat16)

    steps = rows[0].shape[1] // tile
    for part in range(PARTS):

        @pl.when(step // steps == part)
        def _(part=part):
            cols = pl.ds(pl.multiple_of(step % steps * tile, 128), tile)
            tokens = jnp.concatenate([ref[:, cols] for ref in rows[part::PARTS]], axis=0)
            out_ref[...] = exact_dot(turned_ref[...], tokens).astype(jnp.bfloat16)


def scalar_spec():
    return pl.BlockSpec(memory_space=pltpu.SMEM)


def params(mib):
    return pltpu.CompilerParams(vmem_limit_bytes=mib * MIB)


def hbm_spec():
    return pl.BlockSpec(memory_space=pltpu.HBM)


def prepare(far_count, near_count, capacity, scalars, ids, gates, hidden, tokens):
    slots = far_count * near_count * capacity
    rows, wide = hidden.shape
    tok_local, width = tokens.shape
    part = width // PARTS
    vmem = pl.BlockSpec(memory_space=pltpu.VMEM)
    shapes = [(tok_local, part + (ID_COLS if i == 0 else 0)) for i in range(PARTS)]
    shapes += [(slots // far_count, wide)] * far_count + [(slots, rows)]
    return pl.pallas_call(
        functools.partial(prepare_kernel, far_count, near_count, capacity),
        out_shape=[jax.ShapeDtypeStruct(shape, jnp.bfloat16) for shape in shapes],
        in_specs=[scalar_spec()] + [hbm_spec()] * 4,
        out_specs=[vmem] * len(shapes),
        scratch_shapes=[pltpu.VMEM(array.shape, array.dtype) for array in (ids, gates, hidden)]
        + [pltpu.SemaphoreType.DMA((PARTS + 3,))],
        compiler_params=params(12),
        cost_estimate=pl.CostEstimate(flops=2 * rows * rows * wide, bytes_accessed=4 * rows * wide, transcendentals=0),
        name="prepare_rows",
    )(scalars, ids, gates, hidden, tokens)


def regroup(near_count, capacity, arrays):
    lines = len(arrays) * capacity
    vmem = pl.BlockSpec(memory_space=pltpu.VMEM)
    return pl.pallas_call(
        functools.partial(regroup_kernel, len(arrays), near_count, capacity),
        out_shape=[jax.ShapeDtypeStruct((lines, arrays[0].shape[1]), jnp.bfloat16)] * near_count,
        in_specs=[vmem] * len(arrays),
        out_specs=[vmem] * near_count,
        compiler_params=params(8),
        name="regroup_rows",
    )(*arrays)


def close(back_place, came_back, gates, hidden):
    vmem = pl.BlockSpec(memory_space=pltpu.VMEM)
    return pl.pallas_call(
        close_kernel,
        out_shape=[
            jax.ShapeDtypeStruct(hidden.shape, jnp.bfloat16),
            jax.ShapeDtypeStruct(gates.shape, jnp.float32),
        ],
        in_specs=[vmem, vmem, hbm_spec(), hbm_spec()],
        out_specs=[vmem] * 2,
        scratch_shapes=[
            pltpu.VMEM(gates.shape, gates.dtype),
            pltpu.VMEM(hidden.shape, hidden.dtype),
            pltpu.SemaphoreType.DMA((2,)),
        ],
        compiler_params=params(12),
        name="close_rows",
    )(back_place, came_back, gates, hidden)


def first_pick(far_count, near_count, capacity, near, blocks):
    tok_local, wide = blocks[0].shape
    slots = far_count * near_count * capacity
    vmem = pl.BlockSpec(memory_space=pltpu.VMEM)
    return pl.pallas_call(
        functools.partial(first_pick_kernel, far_count, near_count, capacity),
        out_shape=[
            jax.ShapeDtypeStruct((slots, wide - ID_COLS), jnp.bfloat16),
            jax.ShapeDtypeStruct((slots, near_count * tok_local), jnp.bfloat16),
        ],
        in_specs=[scalar_spec()] + [vmem] * len(blocks),
        out_specs=[vmem] * 2,
        compiler_params=params(16),
        name="first_pick",
    )(near, *blocks)


def pick_rows(pick, blocks):
    vmem = pl.BlockSpec(memory_space=pltpu.VMEM)
    return pl.pallas_call(
        pick_kernel,
        out_shape=jax.ShapeDtypeStruct((pick.shape[0], blocks[0].shape[1]), jnp.bfloat16),
        in_specs=[vmem] * (1 + len(blocks)),
        out_specs=vmem,
        compiler_params=params(16),
        name="pick_rows",
    )(pick, *blocks)


def join_rows(arrays):
    vmem = pl.BlockSpec(memory_space=pltpu.VMEM)
    shape = (arrays[0].shape[0], sum(array.shape[1] for array in arrays))
    return pl.pallas_call(
        join_kernel,
        out_shape=jax.ShapeDtypeStruct(shape, jnp.bfloat16),
        in_specs=[vmem] * len(arrays),
        out_specs=vmem,
        compiler_params=params(8),
        name="join_rows",
    )(*arrays)


def down_rows(near_count, capacity, scalars, rows, hids, share):
    part = rows[0].shape[1]
    tile = min(part, 512)
    lines = 2 * rows[0].shape[0]
    width = part * PARTS
    whole = lambda array: pl.BlockSpec(array.shape, lambda i: (0, 0))
    return pl.pallas_call(
        functools.partial(down_kernel, near_count, capacity),
        grid=(width // tile,),
        out_shape=jax.ShapeDtypeStruct((share, width), jnp.bfloat16),
        in_specs=[scalar_spec()] + [whole(array) for array in rows + hids],
        out_specs=pl.BlockSpec((share, tile), lambda i: (0, i)),
        scratch_shapes=[pltpu.VMEM((share, lines), jnp.bfloat16)],
        compiler_params=params(32),
        cost_estimate=pl.CostEstimate(
            flops=2 * lines * width * share, bytes_accessed=2 * width * (lines + share), transcendentals=0
        ),
        name="down_rows",
    )(scalars, *rows, *hids)


def local(grad_out, hidden, gates, expert_ids, w_down):
    tok_local, top_count = expert_ids.shape
    far_count = lax.axis_size("far")
    near_count = lax.axis_size("near")
    experts = far_count * near_count
    capacity = max(4, (tok_local * top_count + experts - 1) // experts)
    width = grad_out.shape[1]
    hidden_width = hidden.shape[2]
    row_total = tok_local * top_count
    slot_total = experts * capacity
    near = lax.axis_index("near")
    near_ref = near.astype(jnp.int32).reshape(1)
    part = width // PARTS
    weight = w_down[0]

    def along(array, steps):
        return lax.ppermute(array, "near", [(i, (i + steps) % near_count) for i in range(near_count)])

    def across(array, apart):
        return lax.ppermute(array, "far", [(i, i ^ apart) for i in range(far_count)])

    def swap(array):
        return lax.ppermute(array, "dp", [(i, i ^ 1) for i in range(lax.axis_size("dp"))])

    def line(array):
        return [array] + [along(array, step) for step in range(1, near_count)]

    hidden_rows = hidden.reshape(row_total, hidden_width)
    scalars = jnp.stack([near, lax.axis_index("far"), lax.axis_index("dp")]).astype(jnp.int32)
    prepared = prepare(far_count, near_count, capacity, scalars, expert_ids.T, gates.T, hidden_rows, grad_out)
    prepared = list(prepared)
    parts, sends, back_place = prepared[:PARTS], prepared[PARTS:-1], prepared[-1]
    blocks = line(parts[0])

    rows, total = [], None
    for i in range(PARTS):
        if i == 0:
            picked, pick = first_pick(far_count, near_count, capacity, near_ref, blocks)
            picked, sends, parts = lax.optimization_barrier((picked, sends, parts))
        else:
            picked = pick_rows(pick, line(parts[i]))
            picked, rows[-1] = lax.optimization_barrier((picked, rows[-1]))
        got = lax.all_to_all(
            picked.reshape(far_count, -1, part), "far", split_axis=0, concat_axis=0, tiled=True
        ).reshape(slot_total, part)
        rows.append(got)
    crossed = [sends[0]] + [across(sends[apart], apart) for apart in range(1, far_count)]
    rows[0], crossed = lax.optimization_barrier((rows[0], crossed))
    hids = list(regroup(near_count, capacity, crossed))
    hids = join_rows(hids[:1] + [along(hids[step], step) for step in range(1, near_count)])
    for i in range(PARTS):
        if i:
            rows[i], total, hids = lax.optimization_barrier((rows[i], total, hids))
        product = lax.dot_general(
            rows[i],
            weight[:, i * part : (i + 1) * part],
            (((1,), (1,)), ((), ())),
            preferred_element_type=jnp.float32,
        )
        total = product if total is None else total + product
    came_back = lax.all_to_all(
        total.astype(jnp.bfloat16).reshape(experts, capacity, hidden_width),
        ("far", "near"),
        split_axis=0,
        concat_axis=0,
        tiled=True,
    )

    grad_down = down_rows(
        near_count,
        capacity,
        scalars,
        rows + [swap(array) for array in rows],
        [hids, swap(hids)],
        hidden_width // lax.axis_size("dp"),
    )
    came_back, grad_down = lax.optimization_barrier((came_back, grad_down))

    grad_hidden, grad_gates = close(
        back_place, came_back.reshape(slot_total, hidden_width), gates.T, hidden_rows
    )
    return (grad_hidden.reshape(hidden.shape), grad_gates.T, grad_down[None])


def solution(mesh):
    placed = (
        P(("dp", "far", "near"), None),
        P(("dp", "far", "near"), None, None),
        P(("dp", "far", "near"), None),
        P(("dp", "far", "near"), None),
        P(("far", "near"), None, None),
    )
    return jax.shard_map(
        local,
        mesh=mesh,
        in_specs=placed,
        out_specs=(
            P(("dp", "far", "near"), None, None),
            P(("dp", "far", "near"), None),
            P(("far", "near"), "dp", None),
        ),
        check_vma=False,
    )
```

```python
import functools

import jax
import jax.numpy as jnp
from jax import lax
from jax.experimental import pallas as pl
from jax.experimental.pallas import tpu as pltpu
from jax.sharding import PartitionSpec as P

ID_COLS = 128
PARTS = 2
MIB = 1024 * 1024


def iota(shape, dim):
    return lax.broadcasted_iota(jnp.int32, shape, dim)


def exact_dot(one_hot, values):
    return jnp.dot(one_hot, values, preferred_element_type=jnp.float32)


def split_kernel(ids_ref, tokens_hbm, *refs):
    outs, sem = refs[:-1], refs[-1]
    part = outs[1].shape[1]
    copies = [
        pltpu.make_async_copy(tokens_hbm.at[:, i * part : (i + 1) * part], out.at[:, :part], sem.at[i])
        for i, out in enumerate(outs)
    ]
    for copy in copies:
        copy.start()
    top_count, tok_local = ids_ref.shape
    same = jnp.where(iota((top_count, ID_COLS), 0) == iota((top_count, ID_COLS), 1), 1.0, 0.0).astype(jnp.bfloat16)
    ids = ids_ref[...].astype(jnp.float32).astype(jnp.bfloat16)
    ids = lax.dot_general(ids, same, (((0,), (0,)), ((), ())), preferred_element_type=jnp.float32)
    ids = jnp.where(iota((tok_local, ID_COLS), 1) < top_count, ids, -1.0)
    outs[0][:, part:] = ids.astype(jnp.bfloat16)
    for copy in copies:
        copy.wait()


def send_kernel(far_count, near_count, capacity, scalars_ref, ids_ref, gates_ref, hidden_ref, *refs):
    sends, back_ref = refs[:-1], refs[-1]
    top_count, tok_local = ids_ref.shape
    rows = tok_local * top_count
    experts = far_count * near_count
    slots = experts * capacity
    near, own_far = scalars_ref[0], scalars_ref[1]
    wide = jnp.where(iota((tok_local, rows), 1) // top_count == iota((tok_local, rows), 0), 1.0, 0.0).astype(jnp.bfloat16)
    mine = iota((top_count, rows), 1) % top_count == iota((top_count, rows), 0)

    def line(values):
        spread = jnp.zeros((top_count, rows), jnp.float32)
        for _ in range(3):
            piece = values.astype(jnp.bfloat16)
            values = values - piece.astype(jnp.float32)
            spread = spread + exact_dot(piece, wide)
        return jnp.sum(jnp.where(mine, spread, 0.0), axis=0, keepdims=True)

    ids = line(ids_ref[...].astype(jnp.float32)).astype(jnp.int32)
    gates = line(gates_ref[...])
    named = iota((experts, rows), 0) == ids
    before = jnp.where(iota((rows, rows), 0) < iota((rows, rows), 1), 1.0, 0.0).astype(jnp.bfloat16)
    counts = exact_dot(jnp.where(named, 1.0, 0.0).astype(jnp.bfloat16), before)
    ranks = jnp.sum(jnp.where(named, counts, 0.0), axis=0, keepdims=True).astype(jnp.int32)
    steps = (ids % near_count - near + near_count) % near_count
    out_slots = ((ids // near_count ^ own_far) * near_count + steps) * capacity + ranks
    back_slots = ids * capacity + ranks
    back_ref[...] = jnp.where(iota((slots, rows), 0) == back_slots, 1.0, 0.0).astype(jnp.bfloat16)
    place = iota((slots, rows), 0) == out_slots
    gate = jnp.sum(jnp.where(place, gates, 0.0), axis=1, keepdims=True)
    place = jnp.where(place, 1.0, 0.0).astype(jnp.bfloat16)
    send = (exact_dot(place, hidden_ref[...]) * gate).astype(jnp.bfloat16)
    for i, ref in enumerate(sends):
        ref[...] = send[i * ref.shape[0] : (i + 1) * ref.shape[0]]


def regroup_kernel(far_count, near_count, capacity, *refs):
    ins, outs = refs[:far_count], refs[far_count:]
    rows = jnp.concatenate([ref[...] for ref in ins], axis=0)
    for step, ref in enumerate(outs):
        shape = (ref.shape[0], rows.shape[0])
        row, col = iota(shape, 0), iota(shape, 1)
        source = (row // capacity * near_count + step) * capacity + row % capacity
        ref[...] = exact_dot(jnp.where(col == source, 1.0, 0.0).astype(jnp.bfloat16), rows).astype(jnp.bfloat16)


def close_kernel(back_ref, came_ref, gates_hbm, hidden_hbm, hid_ref, gates_out_ref, gates_ref, hidden_ref, sem):
    copy = pltpu.make_async_copy(hidden_hbm, hidden_ref, sem.at[0])
    small = pltpu.make_async_copy(gates_hbm, gates_ref, sem.at[1])
    small.start()
    copy.start()
    top_count, tok_local = gates_ref.shape
    rows = tok_local * top_count
    back = lax.dot_general(
        back_ref[...], came_ref[...], (((0,), (0,)), ((), ())), preferred_element_type=jnp.float32
    )
    small.wait()
    mine = iota((tok_local, top_count, tok_local), 0) == iota((tok_local, top_count, tok_local), 2)
    gate = jnp.where(mine, gates_ref[...][None], 0.0).reshape(rows, tok_local)
    gate = jnp.sum(gate, axis=1, keepdims=True)
    hid_ref[...] = (gate * back).astype(jnp.bfloat16)
    copy.wait()
    sums = jnp.sum(back * hidden_ref[...].astype(jnp.float32), axis=1, keepdims=True)
    spread = jnp.broadcast_to(sums, (rows, tok_local)).reshape(tok_local, top_count, tok_local)
    gates_out_ref[...] = jnp.sum(jnp.where(mine, spread, 0.0), axis=0)


def picked_rows(pick, blocks, out_ref):
    width = out_ref.shape[1]
    step = min(width, 512)
    for start in range(0, width, step):
        tokens = jnp.concatenate([block[:, start : start + step] for block in blocks], axis=0)
        out_ref[:, start : start + step] = exact_dot(pick, tokens).astype(jnp.bfloat16)


def first_pick_kernel(far_count, near_count, capacity, near_ref, *refs):
    blocks, (out_ref, pick_ref) = refs[:-2], refs[-2:]
    tok_local = blocks[0].shape[0]
    width = out_ref.shape[1]
    near = near_ref[0]
    cols = near_count * tok_local
    slots = far_count * near_count * capacity
    lead = max(8, far_count)
    ids = jnp.concatenate([block[:, width:] for block in blocks], axis=0).astype(jnp.float32)
    ones = jnp.ones((lead, ID_COLS), jnp.bfloat16)
    named = jnp.zeros((lead, cols), jnp.float32)
    for far in range(far_count):
        expert = (far * near_count + near).astype(jnp.float32)
        hit = jnp.where(ids == expert, 1.0, 0.0).astype(jnp.bfloat16)
        line = lax.dot_general(ones, hit, (((1,), (1,)), ((), ())), preferred_element_type=jnp.float32)
        named = jnp.where(iota((lead, cols), 0) == far, line, named)
    row, col = iota((cols, cols), 0), iota((cols, cols), 1)
    before = jnp.where((row < col) & (row // tok_local == col // tok_local), 1.0, 0.0).astype(jnp.bfloat16)
    rank = exact_dot(named.astype(jnp.bfloat16), before)
    place = jnp.where(named > 0.5, rank, float(capacity)).astype(jnp.bfloat16)
    per_far = near_count * capacity
    spread = jnp.where(iota((slots, lead), 0) // per_far == iota((slots, lead), 1), 1.0, 0.0).astype(jnp.bfloat16)
    slot = iota((slots, cols), 0) % per_far
    block = (near - slot // capacity + near_count) % near_count
    pick = (iota((slots, cols), 1) // tok_local == block) & (
        exact_dot(spread, place).astype(jnp.int32) == slot % capacity
    )
    pick = jnp.where(pick, 1.0, 0.0).astype(jnp.bfloat16)
    pick_ref[...] = pick
    picked_rows(pick, blocks, out_ref)


def pick_kernel(pick_ref, *refs):
    picked_rows(pick_ref[...], refs[:-1], refs[-1])


def join_kernel(*refs):
    out_ref = refs[-1]
    start = 0
    for ref in refs[:-1]:
        out_ref[:, start : start + ref.shape[1]] = ref[...]
        start += ref.shape[1]


def down_kernel(near_count, capacity, scalars_ref, *refs):
    rows, hids, (out_ref, turned_ref) = refs[: 2 * PARTS], refs[2 * PARTS : -2], refs[-2:]
    step = pl.program_id(0)
    share, tile = out_ref.shape
    near, far, replica = scalars_ref[0], scalars_ref[1], scalars_ref[2]

    @pl.when(step == 0)
    def _():
        slots, lines = rows[0].shape[0], hids[0].shape[0]
        hidden_width = hids[0].shape[1] // near_count
        row, col = iota((slots, lines), 0), iota((slots, lines), 1)
        match = (row // (near_count * capacity) ^ far == col // capacity) & (row % capacity == col % capacity)
        block = (near - row // capacity % near_count + near_count) % near_count
        for i, ref in enumerate(hids):
            total = jnp.zeros((slots, share), jnp.float32)
            for j in range(near_count):
                start = pl.multiple_of(j * hidden_width + replica * share, 128)
                order = jnp.where(match & (block == j), 1.0, 0.0).astype(jnp.bfloat16)
                total = total + exact_dot(order, ref[:, pl.ds(start, share)])
            turned_ref[:, i * slots : (i + 1) * slots] = total.T.astype(jnp.bfloat16)

    steps = rows[0].shape[1] // tile
    for part in range(PARTS):

        @pl.when(step // steps == part)
        def _(part=part):
            cols = pl.ds(pl.multiple_of(step % steps * tile, 128), tile)
            tokens = jnp.concatenate([ref[:, cols] for ref in rows[part::PARTS]], axis=0)
            out_ref[...] = exact_dot(turned_ref[...], tokens).astype(jnp.bfloat16)


def scalar_spec():
    return pl.BlockSpec(memory_space=pltpu.SMEM)


def params(mib):
    return pltpu.CompilerParams(vmem_limit_bytes=mib * MIB)


def hbm_spec():
    return pl.BlockSpec(memory_space=pltpu.HBM)


def split_rows(ids, tokens):
    tok_local, width = tokens.shape
    part = width // PARTS
    vmem = pl.BlockSpec(memory_space=pltpu.VMEM)
    return pl.pallas_call(
        split_kernel,
        out_shape=[
            jax.ShapeDtypeStruct((tok_local, part + (ID_COLS if i == 0 else 0)), jnp.bfloat16) for i in range(PARTS)
        ],
        in_specs=[vmem, hbm_spec()],
        out_specs=[vmem] * PARTS,
        scratch_shapes=[pltpu.SemaphoreType.DMA((PARTS,))],
        compiler_params=params(8),
        name="split_rows",
    )(ids, tokens)


def send_rows(far_count, near_count, capacity, scalars, ids, gates, hidden):
    slots = far_count * near_count * capacity
    rows, wide = hidden.shape
    vmem = pl.BlockSpec(memory_space=pltpu.VMEM)
    shapes = [(slots // far_count, wide)] * far_count + [(slots, rows)]
    return pl.pallas_call(
        functools.partial(send_kernel, far_count, near_count, capacity),
        out_shape=[jax.ShapeDtypeStruct(shape, jnp.bfloat16) for shape in shapes],
        in_specs=[scalar_spec()] + [vmem] * 3,
        out_specs=[vmem] * len(shapes),
        compiler_params=params(12),
        cost_estimate=pl.CostEstimate(flops=2 * rows * rows * wide, bytes_accessed=4 * rows * wide, transcendentals=0),
        name="send_rows",
    )(scalars, ids, gates, hidden)


def regroup(near_count, capacity, arrays):
    lines = len(arrays) * capacity
    vmem = pl.BlockSpec(memory_space=pltpu.VMEM)
    return pl.pallas_call(
        functools.partial(regroup_kernel, len(arrays), near_count, capacity),
        out_shape=[jax.ShapeDtypeStruct((lines, arrays[0].shape[1]), jnp.bfloat16)] * near_count,
        in_specs=[vmem] * len(arrays),
        out_specs=[vmem] * near_count,
        compiler_params=params(8),
        name="regroup_rows",
    )(*arrays)


def close(back_place, came_back, gates, hidden):
    vmem = pl.BlockSpec(memory_space=pltpu.VMEM)
    return pl.pallas_call(
        close_kernel,
        out_shape=[
            jax.ShapeDtypeStruct(hidden.shape, jnp.bfloat16),
            jax.ShapeDtypeStruct(gates.shape, jnp.float32),
        ],
        in_specs=[vmem, vmem, hbm_spec(), hbm_spec()],
        out_specs=[vmem] * 2,
        scratch_shapes=[
            pltpu.VMEM(gates.shape, gates.dtype),
            pltpu.VMEM(hidden.shape, hidden.dtype),
            pltpu.SemaphoreType.DMA((2,)),
        ],
        compiler_params=params(12),
        name="close_rows",
    )(back_place, came_back, gates, hidden)


def first_pick(far_count, near_count, capacity, near, blocks):
    tok_local, wide = blocks[0].shape
    slots = far_count * near_count * capacity
    vmem = pl.BlockSpec(memory_space=pltpu.VMEM)
    return pl.pallas_call(
        functools.partial(first_pick_kernel, far_count, near_count, capacity),
        out_shape=[
            jax.ShapeDtypeStruct((slots, wide - ID_COLS), jnp.bfloat16),
            jax.ShapeDtypeStruct((slots, near_count * tok_local), jnp.bfloat16),
        ],
        in_specs=[scalar_spec()] + [vmem] * len(blocks),
        out_specs=[vmem] * 2,
        compiler_params=params(16),
        name="first_pick",
    )(near, *blocks)


def pick_rows(pick, blocks):
    vmem = pl.BlockSpec(memory_space=pltpu.VMEM)
    return pl.pallas_call(
        pick_kernel,
        out_shape=jax.ShapeDtypeStruct((pick.shape[0], blocks[0].shape[1]), jnp.bfloat16),
        in_specs=[vmem] * (1 + len(blocks)),
        out_specs=vmem,
        compiler_params=params(16),
        name="pick_rows",
    )(pick, *blocks)


def join_rows(arrays):
    vmem = pl.BlockSpec(memory_space=pltpu.VMEM)
    shape = (arrays[0].shape[0], sum(array.shape[1] for array in arrays))
    return pl.pallas_call(
        join_kernel,
        out_shape=jax.ShapeDtypeStruct(shape, jnp.bfloat16),
        in_specs=[vmem] * len(arrays),
        out_specs=vmem,
        compiler_params=params(8),
        name="join_rows",
    )(*arrays)


def down_rows(near_count, capacity, scalars, rows, hids, share):
    part = rows[0].shape[1]
    tile = min(part, 512)
    lines = 2 * rows[0].shape[0]
    width = part * PARTS
    whole = lambda array: pl.BlockSpec(array.shape, lambda i: (0, 0))
    return pl.pallas_call(
        functools.partial(down_kernel, near_count, capacity),
        grid=(width // tile,),
        out_shape=jax.ShapeDtypeStruct((share, width), jnp.bfloat16),
        in_specs=[scalar_spec()] + [whole(array) for array in rows + hids],
        out_specs=pl.BlockSpec((share, tile), lambda i: (0, i)),
        scratch_shapes=[pltpu.VMEM((share, lines), jnp.bfloat16)],
        compiler_params=params(32),
        cost_estimate=pl.CostEstimate(
            flops=2 * lines * width * share, bytes_accessed=2 * width * (lines + share), transcendentals=0
        ),
        name="down_rows",
    )(scalars, *rows, *hids)


def local(grad_out, hidden, gates, expert_ids, w_down):
    tok_local, top_count = expert_ids.shape
    far_count = lax.axis_size("far")
    near_count = lax.axis_size("near")
    experts = far_count * near_count
    capacity = max(4, (tok_local * top_count + experts - 1) // experts)
    width = grad_out.shape[1]
    hidden_width = hidden.shape[2]
    row_total = tok_local * top_count
    slot_total = experts * capacity
    near = lax.axis_index("near")
    near_ref = near.astype(jnp.int32).reshape(1)
    part = width // PARTS
    weight = w_down[0]

    def along(array, steps):
        return lax.ppermute(array, "near", [(i, (i + steps) % near_count) for i in range(near_count)])

    def across(array, apart):
        return lax.ppermute(array, "far", [(i, i ^ apart) for i in range(far_count)])

    def swap(array):
        return lax.ppermute(array, "dp", [(i, i ^ 1) for i in range(lax.axis_size("dp"))])

    def line(array):
        return [array] + [along(array, step) for step in range(1, near_count)]

    hidden_rows = hidden.reshape(row_total, hidden_width)
    scalars = jnp.stack([near, lax.axis_index("far"), lax.axis_index("dp")]).astype(jnp.int32)
    ids = expert_ids.T
    parts = list(split_rows(ids, grad_out))
    parts[0], ids = lax.optimization_barrier((parts[0], ids))
    blocks = line(parts[0])
    *sends, back_place = send_rows(far_count, near_count, capacity, scalars, ids, gates.T, hidden_rows)

    rows, total = [], None
    for i in range(PARTS):
        if i == 0:
            picked, pick = first_pick(far_count, near_count, capacity, near_ref, blocks)
            picked, sends, parts = lax.optimization_barrier((picked, sends, parts))
        else:
            picked = pick_rows(pick, line(parts[i]))
            crossed = [sends[0]] + [across(sends[apart], apart) for apart in range(1, far_count)]
            picked, rows[-1], crossed = lax.optimization_barrier((picked, rows[-1], crossed))
        got = lax.all_to_all(
            picked.reshape(far_count, -1, part), "far", split_axis=0, concat_axis=0, tiled=True
        ).reshape(slot_total, part)
        rows.append(got)
    hids = list(regroup(near_count, capacity, crossed))
    hids = join_rows(hids[:1] + [along(hids[step], step) for step in range(1, near_count)])
    for i in range(PARTS):
        if i:
            rows[i], total, hids = lax.optimization_barrier((rows[i], total, hids))
        product = lax.dot_general(
            rows[i],
            weight[:, i * part : (i + 1) * part],
            (((1,), (1,)), ((), ())),
            preferred_element_type=jnp.float32,
        )
        total = product if total is None else total + product
    came_back = lax.all_to_all(
        total.astype(jnp.bfloat16).reshape(experts, capacity, hidden_width),
        ("far", "near"),
        split_axis=0,
        concat_axis=0,
        tiled=True,
    )

    grad_down = down_rows(
        near_count,
        capacity,
        scalars,
        rows + [swap(array) for array in rows],
        [hids, swap(hids)],
        hidden_width // lax.axis_size("dp"),
    )
    came_back, grad_down = lax.optimization_barrier((came_back, grad_down))

    grad_hidden, grad_gates = close(
        back_place, came_back.reshape(slot_total, hidden_width), gates.T, hidden_rows
    )
    return (grad_hidden.reshape(hidden.shape), grad_gates.T, grad_down[None])


def solution(mesh):
    placed = (
        P(("dp", "far", "near"), None),
        P(("dp", "far", "near"), None, None),
        P(("dp", "far", "near"), None),
        P(("dp", "far", "near"), None),
        P(("far", "near"), None, None),
    )
    return jax.shard_map(
        local,
        mesh=mesh,
        in_specs=placed,
        out_specs=(
            P(("dp", "far", "near"), None, None),
            P(("dp", "far", "near"), None),
            P(("far", "near"), "dp", None),
        ),
        check_vma=False,
    )
```

```python
import functools

import jax
import jax.numpy as jnp
from jax import lax
from jax.experimental import pallas as pl
from jax.experimental.pallas import tpu as pltpu
from jax.sharding import PartitionSpec as P

ID_COLS = 128
PARTS = 2
TILE = 256
MIB = 1024 * 1024


def iota(shape, dim):
    return lax.broadcasted_iota(jnp.int32, shape, dim)


def part_bounds(width):
    first = width // TILE * 9 // 16 * TILE
    return [(0, first), (first, width)]


def exact_dot(one_hot, values):
    return jnp.dot(one_hot, values, preferred_element_type=jnp.float32)


def split_kernel(ids_ref, tokens_hbm, *refs):
    outs, sem = refs[:-1], refs[-1]
    copies = []
    for i, (start, stop) in enumerate(part_bounds(tokens_hbm.shape[1])):
        target = outs[i].at[:, : stop - start]
        copies.append(pltpu.make_async_copy(tokens_hbm.at[:, start:stop], target, sem.at[i]))
    for copy in copies:
        copy.start()
    top_count, tok_local = ids_ref.shape
    same = jnp.where(iota((top_count, ID_COLS), 0) == iota((top_count, ID_COLS), 1), 1.0, 0.0).astype(jnp.bfloat16)
    ids = ids_ref[...].astype(jnp.float32).astype(jnp.bfloat16)
    ids = lax.dot_general(ids, same, (((0,), (0,)), ((), ())), preferred_element_type=jnp.float32)
    ids = jnp.where(iota((tok_local, ID_COLS), 1) < top_count, ids, -1.0)
    outs[0][:, outs[0].shape[1] - ID_COLS :] = ids.astype(jnp.bfloat16)
    for copy in copies:
        copy.wait()


def send_kernel(far_count, near_count, capacity, scalars_ref, ids_ref, gates_ref, hidden_ref, *refs):
    sends, back_ref = refs[:-1], refs[-1]
    top_count, tok_local = ids_ref.shape
    rows = tok_local * top_count
    experts = far_count * near_count
    slots = experts * capacity
    near, own_far = scalars_ref[0], scalars_ref[1]
    wide = jnp.where(iota((tok_local, rows), 1) // top_count == iota((tok_local, rows), 0), 1.0, 0.0).astype(jnp.bfloat16)
    mine = iota((top_count, rows), 1) % top_count == iota((top_count, rows), 0)

    def line(values):
        spread = jnp.zeros((top_count, rows), jnp.float32)
        for _ in range(3):
            piece = values.astype(jnp.bfloat16)
            values = values - piece.astype(jnp.float32)
            spread = spread + exact_dot(piece, wide)
        return jnp.sum(jnp.where(mine, spread, 0.0), axis=0, keepdims=True)

    ids = line(ids_ref[...].astype(jnp.float32)).astype(jnp.int32)
    gates = line(gates_ref[...])
    named = iota((experts, rows), 0) == ids
    before = jnp.where(iota((rows, rows), 0) < iota((rows, rows), 1), 1.0, 0.0).astype(jnp.bfloat16)
    counts = exact_dot(jnp.where(named, 1.0, 0.0).astype(jnp.bfloat16), before)
    ranks = jnp.sum(jnp.where(named, counts, 0.0), axis=0, keepdims=True).astype(jnp.int32)
    steps = (ids % near_count - near + near_count) % near_count
    out_slots = ((ids // near_count ^ own_far) * near_count + steps) * capacity + ranks
    back_slots = ids * capacity + ranks
    back_ref[...] = jnp.where(iota((slots, rows), 0) == back_slots, 1.0, 0.0).astype(jnp.bfloat16)
    place = iota((slots, rows), 0) == out_slots
    gate = jnp.sum(jnp.where(place, gates, 0.0), axis=1, keepdims=True)
    place = jnp.where(place, 1.0, 0.0).astype(jnp.bfloat16)
    send = (exact_dot(place, hidden_ref[...]) * gate).astype(jnp.bfloat16)
    for i, ref in enumerate(sends):
        ref[...] = send[i * ref.shape[0] : (i + 1) * ref.shape[0]]


def regroup_kernel(far_count, near_count, capacity, *refs):
    ins, outs = refs[:far_count], refs[far_count:]
    rows = jnp.concatenate([ref[...] for ref in ins], axis=0)
    for step, ref in enumerate(outs):
        shape = (ref.shape[0], rows.shape[0])
        row, col = iota(shape, 0), iota(shape, 1)
        source = (row // capacity * near_count + step) * capacity + row % capacity
        ref[...] = exact_dot(jnp.where(col == source, 1.0, 0.0).astype(jnp.bfloat16), rows).astype(jnp.bfloat16)


def close_kernel(back_ref, came_ref, gates_hbm, hidden_hbm, hid_ref, gates_out_ref, gates_ref, hidden_ref, sem):
    copy = pltpu.make_async_copy(hidden_hbm, hidden_ref, sem.at[0])
    small = pltpu.make_async_copy(gates_hbm, gates_ref, sem.at[1])
    small.start()
    copy.start()
    top_count, tok_local = gates_ref.shape
    rows = tok_local * top_count
    back = lax.dot_general(
        back_ref[...], came_ref[...], (((0,), (0,)), ((), ())), preferred_element_type=jnp.float32
    )
    small.wait()
    mine = iota((tok_local, top_count, tok_local), 0) == iota((tok_local, top_count, tok_local), 2)
    gate = jnp.where(mine, gates_ref[...][None], 0.0).reshape(rows, tok_local)
    gate = jnp.sum(gate, axis=1, keepdims=True)
    hid_ref[...] = (gate * back).astype(jnp.bfloat16)
    copy.wait()
    sums = jnp.sum(back * hidden_ref[...].astype(jnp.float32), axis=1, keepdims=True)
    spread = jnp.broadcast_to(sums, (rows, tok_local)).reshape(tok_local, top_count, tok_local)
    gates_out_ref[...] = jnp.sum(jnp.where(mine, spread, 0.0), axis=0)


def picked_rows(pick, blocks, out_ref):
    width = out_ref.shape[1]
    step = TILE
    for start in range(0, width, step):
        tokens = jnp.concatenate([block[:, start : start + step] for block in blocks], axis=0)
        out_ref[:, start : start + step] = exact_dot(pick, tokens).astype(jnp.bfloat16)


def first_pick_kernel(far_count, near_count, capacity, near_ref, *refs):
    blocks, (out_ref, pick_ref) = refs[:-2], refs[-2:]
    tok_local = blocks[0].shape[0]
    width = out_ref.shape[1]
    near = near_ref[0]
    cols = near_count * tok_local
    slots = far_count * near_count * capacity
    lead = max(8, far_count)
    ids = jnp.concatenate([block[:, width:] for block in blocks], axis=0).astype(jnp.float32)
    ones = jnp.ones((lead, ID_COLS), jnp.bfloat16)
    named = jnp.zeros((lead, cols), jnp.float32)
    for far in range(far_count):
        expert = (far * near_count + near).astype(jnp.float32)
        hit = jnp.where(ids == expert, 1.0, 0.0).astype(jnp.bfloat16)
        line = lax.dot_general(ones, hit, (((1,), (1,)), ((), ())), preferred_element_type=jnp.float32)
        named = jnp.where(iota((lead, cols), 0) == far, line, named)
    row, col = iota((cols, cols), 0), iota((cols, cols), 1)
    before = jnp.where((row < col) & (row // tok_local == col // tok_local), 1.0, 0.0).astype(jnp.bfloat16)
    rank = exact_dot(named.astype(jnp.bfloat16), before)
    place = jnp.where(named > 0.5, rank, float(capacity)).astype(jnp.bfloat16)
    per_far = near_count * capacity
    spread = jnp.where(iota((slots, lead), 0) // per_far == iota((slots, lead), 1), 1.0, 0.0).astype(jnp.bfloat16)
    slot = iota((slots, cols), 0) % per_far
    block = (near - slot // capacity + near_count) % near_count
    pick = (iota((slots, cols), 1) // tok_local == block) & (
        exact_dot(spread, place).astype(jnp.int32) == slot % capacity
    )
    pick = jnp.where(pick, 1.0, 0.0).astype(jnp.bfloat16)
    pick_ref[...] = pick
    picked_rows(pick, blocks, out_ref)


def pick_kernel(pick_ref, *refs):
    picked_rows(pick_ref[...], refs[:-1], refs[-1])


def join_kernel(*refs):
    out_ref = refs[-1]
    start = 0
    for ref in refs[:-1]:
        out_ref[:, start : start + ref.shape[1]] = ref[...]
        start += ref.shape[1]


def down_kernel(near_count, capacity, scalars_ref, *refs):
    rows, hids, (out_ref, turned_ref) = refs[: 2 * PARTS], refs[2 * PARTS : -2], refs[-2:]
    step = pl.program_id(0)
    share, tile = out_ref.shape
    near, far, replica = scalars_ref[0], scalars_ref[1], scalars_ref[2]

    @pl.when(step == 0)
    def _():
        slots, lines = rows[0].shape[0], hids[0].shape[0]
        hidden_width = hids[0].shape[1] // near_count
        row, col = iota((slots, lines), 0), iota((slots, lines), 1)
        match = (row // (near_count * capacity) ^ far == col // capacity) & (row % capacity == col % capacity)
        block = (near - row // capacity % near_count + near_count) % near_count
        for i, ref in enumerate(hids):
            total = jnp.zeros((slots, share), jnp.float32)
            for j in range(near_count):
                start = pl.multiple_of(j * hidden_width + replica * share, 128)
                order = jnp.where(match & (block == j), 1.0, 0.0).astype(jnp.bfloat16)
                total = total + exact_dot(order, ref[:, pl.ds(start, share)])
            turned_ref[:, i * slots : (i + 1) * slots] = total.T.astype(jnp.bfloat16)

    done = 0
    for part in range(PARTS):
        steps = rows[part].shape[1] // tile

        @pl.when((step >= done) & (step < done + steps))
        def _(part=part, done=done):
            cols = pl.ds(pl.multiple_of((step - done) * tile, 128), tile)
            tokens = jnp.concatenate([ref[:, cols] for ref in rows[part::PARTS]], axis=0)
            out_ref[...] = exact_dot(turned_ref[...], tokens).astype(jnp.bfloat16)

        done += steps


def scalar_spec():
    return pl.BlockSpec(memory_space=pltpu.SMEM)


def params(mib):
    return pltpu.CompilerParams(vmem_limit_bytes=mib * MIB)


def hbm_spec():
    return pl.BlockSpec(memory_space=pltpu.HBM)


def split_rows(ids, tokens):
    tok_local, width = tokens.shape
    widths = [stop - start for start, stop in part_bounds(width)]
    widths[0] += ID_COLS
    vmem = pl.BlockSpec(memory_space=pltpu.VMEM)
    return pl.pallas_call(
        split_kernel,
        out_shape=[jax.ShapeDtypeStruct((tok_local, part), jnp.bfloat16) for part in widths],
        in_specs=[vmem, hbm_spec()],
        out_specs=[vmem] * PARTS,
        scratch_shapes=[pltpu.SemaphoreType.DMA((PARTS,))],
        compiler_params=params(8),
        name="split_rows",
    )(ids, tokens)


def send_rows(far_count, near_count, capacity, scalars, ids, gates, hidden):
    slots = far_count * near_count * capacity
    rows, wide = hidden.shape
    vmem = pl.BlockSpec(memory_space=pltpu.VMEM)
    shapes = [(slots // far_count, wide)] * far_count + [(slots, rows)]
    return pl.pallas_call(
        functools.partial(send_kernel, far_count, near_count, capacity),
        out_shape=[jax.ShapeDtypeStruct(shape, jnp.bfloat16) for shape in shapes],
        in_specs=[scalar_spec()] + [vmem] * 3,
        out_specs=[vmem] * len(shapes),
        compiler_params=params(12),
        cost_estimate=pl.CostEstimate(flops=2 * rows * rows * wide, bytes_accessed=4 * rows * wide, transcendentals=0),
        name="send_rows",
    )(scalars, ids, gates, hidden)


def regroup(near_count, capacity, arrays):
    lines = len(arrays) * capacity
    vmem = pl.BlockSpec(memory_space=pltpu.VMEM)
    return pl.pallas_call(
        functools.partial(regroup_kernel, len(arrays), near_count, capacity),
        out_shape=[jax.ShapeDtypeStruct((lines, arrays[0].shape[1]), jnp.bfloat16)] * near_count,
        in_specs=[vmem] * len(arrays),
        out_specs=[vmem] * near_count,
        compiler_params=params(8),
        name="regroup_rows",
    )(*arrays)


def close(back_place, came_back, gates, hidden):
    vmem = pl.BlockSpec(memory_space=pltpu.VMEM)
    return pl.pallas_call(
        close_kernel,
        out_shape=[
            jax.ShapeDtypeStruct(hidden.shape, jnp.bfloat16),
            jax.ShapeDtypeStruct(gates.shape, jnp.float32),
        ],
        in_specs=[vmem, vmem, hbm_spec(), hbm_spec()],
        out_specs=[vmem] * 2,
        scratch_shapes=[
            pltpu.VMEM(gates.shape, gates.dtype),
            pltpu.VMEM(hidden.shape, hidden.dtype),
            pltpu.SemaphoreType.DMA((2,)),
        ],
        compiler_params=params(12),
        name="close_rows",
    )(back_place, came_back, gates, hidden)


def first_pick(far_count, near_count, capacity, near, blocks):
    tok_local, wide = blocks[0].shape
    slots = far_count * near_count * capacity
    vmem = pl.BlockSpec(memory_space=pltpu.VMEM)
    return pl.pallas_call(
        functools.partial(first_pick_kernel, far_count, near_count, capacity),
        out_shape=[
            jax.ShapeDtypeStruct((slots, wide - ID_COLS), jnp.bfloat16),
            jax.ShapeDtypeStruct((slots, near_count * tok_local), jnp.bfloat16),
        ],
        in_specs=[scalar_spec()] + [vmem] * len(blocks),
        out_specs=[vmem] * 2,
        compiler_params=params(16),
        name="first_pick",
    )(near, *blocks)


def pick_rows(pick, blocks):
    vmem = pl.BlockSpec(memory_space=pltpu.VMEM)
    return pl.pallas_call(
        pick_kernel,
        out_shape=jax.ShapeDtypeStruct((pick.shape[0], blocks[0].shape[1]), jnp.bfloat16),
        in_specs=[vmem] * (1 + len(blocks)),
        out_specs=vmem,
        compiler_params=params(16),
        name="pick_rows",
    )(pick, *blocks)


def join_rows(arrays):
    vmem = pl.BlockSpec(memory_space=pltpu.VMEM)
    shape = (arrays[0].shape[0], sum(array.shape[1] for array in arrays))
    return pl.pallas_call(
        join_kernel,
        out_shape=jax.ShapeDtypeStruct(shape, jnp.bfloat16),
        in_specs=[vmem] * len(arrays),
        out_specs=vmem,
        compiler_params=params(8),
        name="join_rows",
    )(*arrays)


def down_rows(near_count, capacity, scalars, rows, hids, share):
    tile = TILE
    lines = 2 * rows[0].shape[0]
    width = sum(array.shape[1] for array in rows[:PARTS])
    whole = lambda array: pl.BlockSpec(array.shape, lambda i: (0, 0))
    return pl.pallas_call(
        functools.partial(down_kernel, near_count, capacity),
        grid=(width // tile,),
        out_shape=jax.ShapeDtypeStruct((share, width), jnp.bfloat16),
        in_specs=[scalar_spec()] + [whole(array) for array in rows + hids],
        out_specs=pl.BlockSpec((share, tile), lambda i: (0, i)),
        scratch_shapes=[pltpu.VMEM((share, lines), jnp.bfloat16)],
        compiler_params=params(32),
        cost_estimate=pl.CostEstimate(
            flops=2 * lines * width * share, bytes_accessed=2 * width * (lines + share), transcendentals=0
        ),
        name="down_rows",
    )(scalars, *rows, *hids)


def local(grad_out, hidden, gates, expert_ids, w_down):
    tok_local, top_count = expert_ids.shape
    far_count = lax.axis_size("far")
    near_count = lax.axis_size("near")
    experts = far_count * near_count
    capacity = max(4, (tok_local * top_count + experts - 1) // experts)
    width = grad_out.shape[1]
    hidden_width = hidden.shape[2]
    row_total = tok_local * top_count
    slot_total = experts * capacity
    near = lax.axis_index("near")
    near_ref = near.astype(jnp.int32).reshape(1)
    bounds = part_bounds(width)
    weight = w_down[0]

    def along(array, steps):
        return lax.ppermute(array, "near", [(i, (i + steps) % near_count) for i in range(near_count)])

    def across(array, apart):
        return lax.ppermute(array, "far", [(i, i ^ apart) for i in range(far_count)])

    def swap(array):
        return lax.ppermute(array, "dp", [(i, i ^ 1) for i in range(lax.axis_size("dp"))])

    def line(array):
        return [array] + [along(array, step) for step in range(1, near_count)]

    hidden_rows = hidden.reshape(row_total, hidden_width)
    scalars = jnp.stack([near, lax.axis_index("far"), lax.axis_index("dp")]).astype(jnp.int32)
    ids = expert_ids.T
    parts = list(split_rows(ids, grad_out))
    parts[0], ids = lax.optimization_barrier((parts[0], ids))
    blocks = line(parts[0])
    *sends, back_place = send_rows(far_count, near_count, capacity, scalars, ids, gates.T, hidden_rows)
    crossed = [sends[0]] + [across(sends[apart], apart) for apart in range(1, far_count)]

    rows, total = [], None
    for i in range(PARTS):
        if i == 0:
            picked, pick = first_pick(far_count, near_count, capacity, near_ref, blocks)
            picked, crossed, parts = lax.optimization_barrier((picked, crossed, parts))
        else:
            picked = pick_rows(pick, line(parts[i]))
            picked, rows[-1], crossed = lax.optimization_barrier((picked, rows[-1], crossed))
        got = lax.all_to_all(
            picked.reshape(far_count, -1, picked.shape[1]), "far", split_axis=0, concat_axis=0, tiled=True
        ).reshape(picked.shape)
        rows.append(got)
    hids = list(regroup(near_count, capacity, crossed))
    hids = join_rows(hids[:1] + [along(hids[step], step) for step in range(1, near_count)])
    for i in range(PARTS):
        if i:
            rows[i], total, hids = lax.optimization_barrier((rows[i], total, hids))
        product = lax.dot_general(
            rows[i],
            weight[:, bounds[i][0] : bounds[i][1]],
            (((1,), (1,)), ((), ())),
            preferred_element_type=jnp.float32,
        )
        total = product if total is None else total + product
    came_back = lax.all_to_all(
        total.astype(jnp.bfloat16).reshape(experts, capacity, hidden_width),
        ("far", "near"),
        split_axis=0,
        concat_axis=0,
        tiled=True,
    )

    grad_down = down_rows(
        near_count,
        capacity,
        scalars,
        rows + [swap(array) for array in rows],
        [hids, swap(hids)],
        hidden_width // lax.axis_size("dp"),
    )
    came_back, grad_down = lax.optimization_barrier((came_back, grad_down))

    grad_hidden, grad_gates = close(
        back_place, came_back.reshape(slot_total, hidden_width), gates.T, hidden_rows
    )
    return (grad_hidden.reshape(hidden.shape), grad_gates.T, grad_down[None])


def solution(mesh):
    placed = (
        P(("dp", "far", "near"), None),
        P(("dp", "far", "near"), None, None),
        P(("dp", "far", "near"), None),
        P(("dp", "far", "near"), None),
        P(("far", "near"), None, None),
    )
    return jax.shard_map(
        local,
        mesh=mesh,
        in_specs=placed,
        out_specs=(
            P(("dp", "far", "near"), None, None),
            P(("dp", "far", "near"), None),
            P(("far", "near"), "dp", None),
        ),
        check_vma=False,
    )
```

```python
import functools

import jax
import jax.numpy as jnp
from jax import lax
from jax.experimental import pallas as pl
from jax.experimental.pallas import tpu as pltpu
from jax.sharding import PartitionSpec as P

ID_COLS = 128
PARTS = 2
TILE = 256
MIB = 1024 * 1024


def iota(shape, dim):
    return lax.broadcasted_iota(jnp.int32, shape, dim)


def part_bounds(width):
    first = width // TILE * 9 // 16 * TILE
    return [(0, first), (first, width)]


def exact_dot(one_hot, values):
    return jnp.dot(one_hot, values, preferred_element_type=jnp.float32)


def split_kernel(ids_ref, tokens_hbm, *refs):
    outs, sem = refs[:-1], refs[-1]
    copies = []
    for i, (start, stop) in enumerate(part_bounds(tokens_hbm.shape[1])):
        target = outs[i].at[:, : stop - start]
        copies.append(pltpu.make_async_copy(tokens_hbm.at[:, start:stop], target, sem.at[i]))
    for copy in copies:
        copy.start()
    top_count, tok_local = ids_ref.shape
    same = jnp.where(iota((top_count, ID_COLS), 0) == iota((top_count, ID_COLS), 1), 1.0, 0.0).astype(jnp.bfloat16)
    ids = ids_ref[...].astype(jnp.float32).astype(jnp.bfloat16)
    ids = lax.dot_general(ids, same, (((0,), (0,)), ((), ())), preferred_element_type=jnp.float32)
    ids = jnp.where(iota((tok_local, ID_COLS), 1) < top_count, ids, -1.0)
    outs[0][:, outs[0].shape[1] - ID_COLS :] = ids.astype(jnp.bfloat16)
    for copy in copies:
        copy.wait()


def send_kernel(far_count, near_count, capacity, scalars_ref, ids_ref, gates_ref, hidden_ref, *refs):
    sends, back_ref = refs[:-1], refs[-1]
    top_count, tok_local = ids_ref.shape
    rows = tok_local * top_count
    experts = far_count * near_count
    slots = experts * capacity
    near, own_far = scalars_ref[0], scalars_ref[1]
    wide = jnp.where(iota((tok_local, rows), 1) // top_count == iota((tok_local, rows), 0), 1.0, 0.0).astype(jnp.bfloat16)
    mine = iota((top_count, rows), 1) % top_count == iota((top_count, rows), 0)

    def line(values):
        spread = jnp.zeros((top_count, rows), jnp.float32)
        for _ in range(3):
            piece = values.astype(jnp.bfloat16)
            values = values - piece.astype(jnp.float32)
            spread = spread + exact_dot(piece, wide)
        return jnp.sum(jnp.where(mine, spread, 0.0), axis=0, keepdims=True)

    ids = line(ids_ref[...].astype(jnp.float32)).astype(jnp.int32)
    gates = line(gates_ref[...])
    named = iota((experts, rows), 0) == ids
    before = jnp.where(iota((rows, rows), 0) < iota((rows, rows), 1), 1.0, 0.0).astype(jnp.bfloat16)
    counts = exact_dot(jnp.where(named, 1.0, 0.0).astype(jnp.bfloat16), before)
    ranks = jnp.sum(jnp.where(named, counts, 0.0), axis=0, keepdims=True).astype(jnp.int32)
    steps = (ids % near_count - near + near_count) % near_count
    out_slots = ((ids // near_count ^ own_far) * near_count + steps) * capacity + ranks
    back_slots = ids * capacity + ranks
    back_ref[...] = jnp.where(iota((slots, rows), 0) == back_slots, 1.0, 0.0).astype(jnp.bfloat16)
    place = iota((slots, rows), 0) == out_slots
    gate = jnp.sum(jnp.where(place, gates, 0.0), axis=1, keepdims=True)
    place = jnp.where(place, 1.0, 0.0).astype(jnp.bfloat16)
    send = (exact_dot(place, hidden_ref[...]) * gate).astype(jnp.bfloat16)
    for i, ref in enumerate(sends):
        ref[...] = send[i * ref.shape[0] : (i + 1) * ref.shape[0]]


def regroup_kernel(far_count, near_count, capacity, *refs):
    ins, outs = refs[:far_count], refs[far_count:]
    rows = jnp.concatenate([ref[...] for ref in ins], axis=0)
    for step, ref in enumerate(outs):
        shape = (ref.shape[0], rows.shape[0])
        row, col = iota(shape, 0), iota(shape, 1)
        source = (row // capacity * near_count + step) * capacity + row % capacity
        ref[...] = exact_dot(jnp.where(col == source, 1.0, 0.0).astype(jnp.bfloat16), rows).astype(jnp.bfloat16)


def close_kernel(back_ref, came_ref, gates_hbm, hidden_hbm, hid_ref, gates_out_ref, gates_ref, hidden_ref, sem):
    copy = pltpu.make_async_copy(hidden_hbm, hidden_ref, sem.at[0])
    small = pltpu.make_async_copy(gates_hbm, gates_ref, sem.at[1])
    small.start()
    copy.start()
    top_count, tok_local = gates_ref.shape
    rows = tok_local * top_count
    back = lax.dot_general(
        back_ref[...], came_ref[...], (((0,), (0,)), ((), ())), preferred_element_type=jnp.float32
    )
    small.wait()
    mine = iota((tok_local, top_count, tok_local), 0) == iota((tok_local, top_count, tok_local), 2)
    gate = jnp.where(mine, gates_ref[...][None], 0.0).reshape(rows, tok_local)
    gate = jnp.sum(gate, axis=1, keepdims=True)
    hid_ref[...] = (gate * back).astype(jnp.bfloat16)
    copy.wait()
    sums = jnp.sum(back * hidden_ref[...].astype(jnp.float32), axis=1, keepdims=True)
    spread = jnp.broadcast_to(sums, (rows, tok_local)).reshape(tok_local, top_count, tok_local)
    gates_out_ref[...] = jnp.sum(jnp.where(mine, spread, 0.0), axis=0)


def picked_rows(pick, blocks, out_ref):
    width = out_ref.shape[1]
    step = max(lanes for lanes in range(128, 1025, 128) if width % lanes == 0)
    for start in range(0, width, step):
        tokens = jnp.concatenate([block[:, start : start + step] for block in blocks], axis=0)
        out_ref[:, start : start + step] = exact_dot(pick, tokens).astype(jnp.bfloat16)


def first_pick_kernel(far_count, near_count, capacity, near_ref, *refs):
    blocks, (out_ref, pick_ref) = refs[:-2], refs[-2:]
    tok_local = blocks[0].shape[0]
    width = out_ref.shape[1]
    near = near_ref[0]
    cols = near_count * tok_local
    slots = far_count * near_count * capacity
    lead = max(8, far_count)
    ids = jnp.concatenate([block[:, width:] for block in blocks], axis=0).astype(jnp.float32)
    ones = jnp.ones((lead, ID_COLS), jnp.bfloat16)
    named = jnp.zeros((lead, cols), jnp.float32)
    for far in range(far_count):
        expert = (far * near_count + near).astype(jnp.float32)
        hit = jnp.where(ids == expert, 1.0, 0.0).astype(jnp.bfloat16)
        line = lax.dot_general(ones, hit, (((1,), (1,)), ((), ())), preferred_element_type=jnp.float32)
        named = jnp.where(iota((lead, cols), 0) == far, line, named)
    row, col = iota((cols, cols), 0), iota((cols, cols), 1)
    before = jnp.where((row < col) & (row // tok_local == col // tok_local), 1.0, 0.0).astype(jnp.bfloat16)
    rank = exact_dot(named.astype(jnp.bfloat16), before)
    place = jnp.where(named > 0.5, rank, float(capacity)).astype(jnp.bfloat16)
    per_far = near_count * capacity
    spread = jnp.where(iota((slots, lead), 0) // per_far == iota((slots, lead), 1), 1.0, 0.0).astype(jnp.bfloat16)
    slot = iota((slots, cols), 0) % per_far
    block = (near - slot // capacity + near_count) % near_count
    pick = (iota((slots, cols), 1) // tok_local == block) & (
        exact_dot(spread, place).astype(jnp.int32) == slot % capacity
    )
    pick = jnp.where(pick, 1.0, 0.0).astype(jnp.bfloat16)
    pick_ref[...] = pick
    picked_rows(pick, blocks, out_ref)


def pick_kernel(pick_ref, *refs):
    picked_rows(pick_ref[...], refs[:-1], refs[-1])


def join_kernel(*refs):
    out_ref = refs[-1]
    start = 0
    for ref in refs[:-1]:
        out_ref[:, start : start + ref.shape[1]] = ref[...]
        start += ref.shape[1]


def down_kernel(near_count, capacity, scalars_ref, *refs):
    rows, hids, (out_ref, turned_ref) = refs[: 2 * PARTS], refs[2 * PARTS : -2], refs[-2:]
    step = pl.program_id(0)
    share, tile = out_ref.shape
    near, far, replica = scalars_ref[0], scalars_ref[1], scalars_ref[2]

    @pl.when(step == 0)
    def _():
        slots, lines = rows[0].shape[0], hids[0].shape[0]
        hidden_width = hids[0].shape[1] // near_count
        row, col = iota((slots, lines), 0), iota((slots, lines), 1)
        match = (row // (near_count * capacity) ^ far == col // capacity) & (row % capacity == col % capacity)
        block = (near - row // capacity % near_count + near_count) % near_count
        for i, ref in enumerate(hids):
            total = jnp.zeros((slots, share), jnp.float32)
            for j in range(near_count):
                start = pl.multiple_of(j * hidden_width + replica * share, 128)
                order = jnp.where(match & (block == j), 1.0, 0.0).astype(jnp.bfloat16)
                total = total + exact_dot(order, ref[:, pl.ds(start, share)])
            turned_ref[:, i * slots : (i + 1) * slots] = total.T.astype(jnp.bfloat16)

    bounds = part_bounds(sum(ref.shape[1] for ref in rows[:PARTS]))
    for i in range(bounds[-1][1] // tile):

        @pl.when(step == i)
        def _(i=i):
            pieces = []
            for part, (start, stop) in enumerate(bounds):
                first, last = max(i * tile, start) - start, min((i + 1) * tile, stop) - start
                if first < last:
                    pieces.append(jnp.concatenate([ref[:, first:last] for ref in rows[part::PARTS]], axis=0))
            tokens = pieces[0] if len(pieces) == 1 else jnp.concatenate(pieces, axis=1)
            out_ref[...] = exact_dot(turned_ref[...], tokens).astype(jnp.bfloat16)


def scalar_spec():
    return pl.BlockSpec(memory_space=pltpu.SMEM)


def params(mib):
    return pltpu.CompilerParams(vmem_limit_bytes=mib * MIB)


def hbm_spec():
    return pl.BlockSpec(memory_space=pltpu.HBM)


def split_rows(ids, tokens):
    tok_local, width = tokens.shape
    widths = [stop - start for start, stop in part_bounds(width)]
    widths[0] += ID_COLS
    vmem = pl.BlockSpec(memory_space=pltpu.VMEM)
    return pl.pallas_call(
        split_kernel,
        out_shape=[jax.ShapeDtypeStruct((tok_local, part), jnp.bfloat16) for part in widths],
        in_specs=[vmem, hbm_spec()],
        out_specs=[vmem] * PARTS,
        scratch_shapes=[pltpu.SemaphoreType.DMA((PARTS,))],
        compiler_params=params(8),
        name="split_rows",
    )(ids, tokens)


def send_rows(far_count, near_count, capacity, scalars, ids, gates, hidden):
    slots = far_count * near_count * capacity
    rows, wide = hidden.shape
    vmem = pl.BlockSpec(memory_space=pltpu.VMEM)
    shapes = [(slots // far_count, wide)] * far_count + [(slots, rows)]
    return pl.pallas_call(
        functools.partial(send_kernel, far_count, near_count, capacity),
        out_shape=[jax.ShapeDtypeStruct(shape, jnp.bfloat16) for shape in shapes],
        in_specs=[scalar_spec()] + [vmem] * 3,
        out_specs=[vmem] * len(shapes),
        compiler_params=params(12),
        cost_estimate=pl.CostEstimate(flops=2 * rows * rows * wide, bytes_accessed=4 * rows * wide, transcendentals=0),
        name="send_rows",
    )(scalars, ids, gates, hidden)


def regroup(near_count, capacity, arrays):
    lines = len(arrays) * capacity
    vmem = pl.BlockSpec(memory_space=pltpu.VMEM)
    return pl.pallas_call(
        functools.partial(regroup_kernel, len(arrays), near_count, capacity),
        out_shape=[jax.ShapeDtypeStruct((lines, arrays[0].shape[1]), jnp.bfloat16)] * near_count,
        in_specs=[vmem] * len(arrays),
        out_specs=[vmem] * near_count,
        compiler_params=params(8),
        name="regroup_rows",
    )(*arrays)


def close(back_place, came_back, gates, hidden):
    vmem = pl.BlockSpec(memory_space=pltpu.VMEM)
    return pl.pallas_call(
        close_kernel,
        out_shape=[
            jax.ShapeDtypeStruct(hidden.shape, jnp.bfloat16),
            jax.ShapeDtypeStruct(gates.shape, jnp.float32),
        ],
        in_specs=[vmem, vmem, hbm_spec(), hbm_spec()],
        out_specs=[vmem] * 2,
        scratch_shapes=[
            pltpu.VMEM(gates.shape, gates.dtype),
            pltpu.VMEM(hidden.shape, hidden.dtype),
            pltpu.SemaphoreType.DMA((2,)),
        ],
        compiler_params=params(12),
        name="close_rows",
    )(back_place, came_back, gates, hidden)


def first_pick(far_count, near_count, capacity, near, blocks):
    tok_local, wide = blocks[0].shape
    slots = far_count * near_count * capacity
    vmem = pl.BlockSpec(memory_space=pltpu.VMEM)
    return pl.pallas_call(
        functools.partial(first_pick_kernel, far_count, near_count, capacity),
        out_shape=[
            jax.ShapeDtypeStruct((slots, wide - ID_COLS), jnp.bfloat16),
            jax.ShapeDtypeStruct((slots, near_count * tok_local), jnp.bfloat16),
        ],
        in_specs=[scalar_spec()] + [vmem] * len(blocks),
        out_specs=[vmem] * 2,
        compiler_params=params(16),
        name="first_pick",
    )(near, *blocks)


def pick_rows(pick, blocks):
    vmem = pl.BlockSpec(memory_space=pltpu.VMEM)
    return pl.pallas_call(
        pick_kernel,
        out_shape=jax.ShapeDtypeStruct((pick.shape[0], blocks[0].shape[1]), jnp.bfloat16),
        in_specs=[vmem] * (1 + len(blocks)),
        out_specs=vmem,
        compiler_params=params(16),
        name="pick_rows",
    )(pick, *blocks)


def join_rows(arrays):
    vmem = pl.BlockSpec(memory_space=pltpu.VMEM)
    shape = (arrays[0].shape[0], sum(array.shape[1] for array in arrays))
    return pl.pallas_call(
        join_kernel,
        out_shape=jax.ShapeDtypeStruct(shape, jnp.bfloat16),
        in_specs=[vmem] * len(arrays),
        out_specs=vmem,
        compiler_params=params(8),
        name="join_rows",
    )(*arrays)


def down_rows(near_count, capacity, scalars, rows, hids, share):
    lines = 2 * rows[0].shape[0]
    width = sum(array.shape[1] for array in rows[:PARTS])
    tile = 2 * TILE
    whole = lambda array: pl.BlockSpec(array.shape, lambda i: (0, 0))
    return pl.pallas_call(
        functools.partial(down_kernel, near_count, capacity),
        grid=(width // tile,),
        out_shape=jax.ShapeDtypeStruct((share, width), jnp.bfloat16),
        in_specs=[scalar_spec()] + [whole(array) for array in rows + hids],
        out_specs=pl.BlockSpec((share, tile), lambda i: (0, i)),
        scratch_shapes=[pltpu.VMEM((share, lines), jnp.bfloat16)],
        compiler_params=params(32),
        cost_estimate=pl.CostEstimate(
            flops=2 * lines * width * share, bytes_accessed=2 * width * (lines + share), transcendentals=0
        ),
        name="down_rows",
    )(scalars, *rows, *hids)


def local(grad_out, hidden, gates, expert_ids, w_down):
    tok_local, top_count = expert_ids.shape
    far_count = lax.axis_size("far")
    near_count = lax.axis_size("near")
    experts = far_count * near_count
    capacity = max(4, (tok_local * top_count + experts - 1) // experts)
    width = grad_out.shape[1]
    hidden_width = hidden.shape[2]
    row_total = tok_local * top_count
    slot_total = experts * capacity
    near = lax.axis_index("near")
    near_ref = near.astype(jnp.int32).reshape(1)
    bounds = part_bounds(width)
    weight = w_down[0]

    def along(array, steps):
        return lax.ppermute(array, "near", [(i, (i + steps) % near_count) for i in range(near_count)])

    def across(array, apart):
        return lax.ppermute(array, "far", [(i, i ^ apart) for i in range(far_count)])

    def swap(array):
        return lax.ppermute(array, "dp", [(i, i ^ 1) for i in range(lax.axis_size("dp"))])

    def line(array):
        return [array] + [along(array, step) for step in range(1, near_count)]

    hidden_rows = hidden.reshape(row_total, hidden_width)
    scalars = jnp.stack([near, lax.axis_index("far"), lax.axis_index("dp")]).astype(jnp.int32)
    ids = expert_ids.T
    parts = list(split_rows(ids, grad_out))
    parts[0], ids = lax.optimization_barrier((parts[0], ids))
    blocks = line(parts[0])
    *sends, back_place = send_rows(far_count, near_count, capacity, scalars, ids, gates.T, hidden_rows)
    crossed = [sends[0]] + [across(sends[apart], apart) for apart in range(1, far_count)]

    rows, total = [], None
    for i in range(PARTS):
        if i == 0:
            picked, pick = first_pick(far_count, near_count, capacity, near_ref, blocks)
            picked, crossed, parts = lax.optimization_barrier((picked, crossed, parts))
        else:
            picked = pick_rows(pick, line(parts[i]))
            picked, rows[-1], crossed = lax.optimization_barrier((picked, rows[-1], crossed))
        got = lax.all_to_all(
            picked.reshape(far_count, -1, picked.shape[1]), "far", split_axis=0, concat_axis=0, tiled=True
        ).reshape(picked.shape)
        rows.append(got)
    hids = list(regroup(near_count, capacity, crossed))
    hids = join_rows(hids[:1] + [along(hids[step], step) for step in range(1, near_count)])
    for i in range(PARTS):
        if i:
            rows[i], total, hids = lax.optimization_barrier((rows[i], total, hids))
        product = lax.dot_general(
            rows[i],
            weight[:, bounds[i][0] : bounds[i][1]],
            (((1,), (1,)), ((), ())),
            preferred_element_type=jnp.float32,
        )
        total = product if total is None else total + product
    came_back = lax.all_to_all(
        total.astype(jnp.bfloat16).reshape(experts, capacity, hidden_width),
        ("far", "near"),
        split_axis=0,
        concat_axis=0,
        tiled=True,
    )

    grad_down = down_rows(
        near_count,
        capacity,
        scalars,
        rows + [swap(array) for array in rows],
        [hids, swap(hids)],
        hidden_width // lax.axis_size("dp"),
    )
    came_back, grad_down = lax.optimization_barrier((came_back, grad_down))

    grad_hidden, grad_gates = close(
        back_place, came_back.reshape(slot_total, hidden_width), gates.T, hidden_rows
    )
    return (grad_hidden.reshape(hidden.shape), grad_gates.T, grad_down[None])


def solution(mesh):
    placed = (
        P(("dp", "far", "near"), None),
        P(("dp", "far", "near"), None, None),
        P(("dp", "far", "near"), None),
        P(("dp", "far", "near"), None),
        P(("far", "near"), None, None),
    )
    return jax.shard_map(
        local,
        mesh=mesh,
        in_specs=placed,
        out_specs=(
            P(("dp", "far", "near"), None, None),
            P(("dp", "far", "near"), None),
            P(("far", "near"), "dp", None),
        ),
        check_vma=False,
    )
```

```python
import functools

import jax
import jax.numpy as jnp
from jax import lax
from jax.experimental import pallas as pl
from jax.experimental.pallas import tpu as pltpu
from jax.sharding import PartitionSpec as P

ID_COLS = 128
PARTS = 2
TILE = 256
MIB = 1024 * 1024


def iota(shape, dim):
    return lax.broadcasted_iota(jnp.int32, shape, dim)


def part_bounds(width):
    first = width // TILE * 9 // 16 * TILE
    return [(0, first), (first, width)]


def exact_dot(one_hot, values):
    return jnp.dot(one_hot, values, preferred_element_type=jnp.float32)


def split_kernel(ids_ref, tokens_hbm, *refs):
    outs, sem = refs[:-1], refs[-1]
    copies = []
    for i, (start, stop) in enumerate(part_bounds(tokens_hbm.shape[1])):
        target = outs[i].at[:, : stop - start]
        copies.append(pltpu.make_async_copy(tokens_hbm.at[:, start:stop], target, sem.at[i]))
    for copy in copies:
        copy.start()
    top_count, tok_local = ids_ref.shape
    same = jnp.where(iota((top_count, ID_COLS), 0) == iota((top_count, ID_COLS), 1), 1.0, 0.0).astype(jnp.bfloat16)
    ids = ids_ref[...].astype(jnp.float32).astype(jnp.bfloat16)
    ids = lax.dot_general(ids, same, (((0,), (0,)), ((), ())), preferred_element_type=jnp.float32)
    ids = jnp.where(iota((tok_local, ID_COLS), 1) < top_count, ids, -1.0)
    outs[0][:, outs[0].shape[1] - ID_COLS :] = ids.astype(jnp.bfloat16)
    for copy in copies:
        copy.wait()


def send_kernel(far_count, near_count, capacity, scalars_ref, ids_ref, gates_ref, hidden_ref, *refs):
    sends, back_ref = refs[:-1], refs[-1]
    top_count, tok_local = ids_ref.shape
    rows = tok_local * top_count
    experts = far_count * near_count
    slots = experts * capacity
    near, own_far = scalars_ref[0], scalars_ref[1]
    wide = jnp.where(iota((tok_local, rows), 1) // top_count == iota((tok_local, rows), 0), 1.0, 0.0).astype(jnp.bfloat16)
    mine = iota((top_count, rows), 1) % top_count == iota((top_count, rows), 0)

    def line(values):
        spread = jnp.zeros((top_count, rows), jnp.float32)
        for _ in range(3):
            piece = values.astype(jnp.bfloat16)
            values = values - piece.astype(jnp.float32)
            spread = spread + exact_dot(piece, wide)
        return jnp.sum(jnp.where(mine, spread, 0.0), axis=0, keepdims=True)

    ids = line(ids_ref[...].astype(jnp.float32)).astype(jnp.int32)
    gates = line(gates_ref[...])
    named = iota((experts, rows), 0) == ids
    before = jnp.where(iota((rows, rows), 0) < iota((rows, rows), 1), 1.0, 0.0).astype(jnp.bfloat16)
    counts = exact_dot(jnp.where(named, 1.0, 0.0).astype(jnp.bfloat16), before)
    ranks = jnp.sum(jnp.where(named, counts, 0.0), axis=0, keepdims=True).astype(jnp.int32)
    steps = (ids % near_count - near + near_count) % near_count
    out_slots = ((ids // near_count ^ own_far) * near_count + steps) * capacity + ranks
    back_slots = ids * capacity + ranks
    back_ref[...] = jnp.where(iota((slots, rows), 0) == back_slots, 1.0, 0.0).astype(jnp.bfloat16)
    place = iota((slots, rows), 0) == out_slots
    gate = jnp.sum(jnp.where(place, gates, 0.0), axis=1, keepdims=True)
    place = jnp.where(place, 1.0, 0.0).astype(jnp.bfloat16)
    send = (exact_dot(place, hidden_ref[...]) * gate).astype(jnp.bfloat16)
    for i, ref in enumerate(sends):
        ref[...] = send[i * ref.shape[0] : (i + 1) * ref.shape[0]]


def regroup_kernel(far_count, near_count, capacity, *refs):
    ins, outs = refs[:far_count], refs[far_count:]
    rows = jnp.concatenate([ref[...] for ref in ins], axis=0)
    for step, ref in enumerate(outs):
        shape = (ref.shape[0], rows.shape[0])
        row, col = iota(shape, 0), iota(shape, 1)
        source = (row // capacity * near_count + step) * capacity + row % capacity
        ref[...] = exact_dot(jnp.where(col == source, 1.0, 0.0).astype(jnp.bfloat16), rows).astype(jnp.bfloat16)


def close_kernel(back_ref, came_ref, gates_hbm, hidden_hbm, hid_ref, gates_out_ref, gates_ref, hidden_ref, sem):
    copy = pltpu.make_async_copy(hidden_hbm, hidden_ref, sem.at[0])
    small = pltpu.make_async_copy(gates_hbm, gates_ref, sem.at[1])
    small.start()
    copy.start()
    top_count, tok_local = gates_ref.shape
    rows = tok_local * top_count
    back = lax.dot_general(
        back_ref[...], came_ref[...], (((0,), (0,)), ((), ())), preferred_element_type=jnp.float32
    )
    small.wait()
    mine = iota((tok_local, top_count, tok_local), 0) == iota((tok_local, top_count, tok_local), 2)
    gate = jnp.where(mine, gates_ref[...][None], 0.0).reshape(rows, tok_local)
    gate = jnp.sum(gate, axis=1, keepdims=True)
    hid_ref[...] = (gate * back).astype(jnp.bfloat16)
    copy.wait()
    sums = jnp.sum(back * hidden_ref[...].astype(jnp.float32), axis=1, keepdims=True)
    spread = jnp.broadcast_to(sums, (rows, tok_local)).reshape(tok_local, top_count, tok_local)
    gates_out_ref[...] = jnp.sum(jnp.where(mine, spread, 0.0), axis=0)


def picked_rows(pick, blocks, out_ref):
    width = out_ref.shape[1]
    step = max(lanes for lanes in range(128, 1025, 128) if width % lanes == 0)
    for start in range(0, width, step):
        tokens = jnp.concatenate([block[:, start : start + step] for block in blocks], axis=0)
        out_ref[:, start : start + step] = exact_dot(pick, tokens).astype(jnp.bfloat16)


def first_pick_kernel(far_count, near_count, capacity, near_ref, *refs):
    blocks, (out_ref, pick_ref) = refs[:-2], refs[-2:]
    tok_local = blocks[0].shape[0]
    width = out_ref.shape[1]
    near = near_ref[0]
    cols = near_count * tok_local
    slots = far_count * near_count * capacity
    lead = max(8, far_count)
    ids = jnp.concatenate([block[:, width:] for block in blocks], axis=0).astype(jnp.float32)
    ones = jnp.ones((lead, ID_COLS), jnp.bfloat16)
    named = jnp.zeros((lead, cols), jnp.float32)
    for far in range(far_count):
        expert = (far * near_count + near).astype(jnp.float32)
        hit = jnp.where(ids == expert, 1.0, 0.0).astype(jnp.bfloat16)
        line = lax.dot_general(ones, hit, (((1,), (1,)), ((), ())), preferred_element_type=jnp.float32)
        named = jnp.where(iota((lead, cols), 0) == far, line, named)
    row, col = iota((cols, cols), 0), iota((cols, cols), 1)
    before = jnp.where((row < col) & (row // tok_local == col // tok_local), 1.0, 0.0).astype(jnp.bfloat16)
    rank = exact_dot(named.astype(jnp.bfloat16), before)
    place = jnp.where(named > 0.5, rank, float(capacity)).astype(jnp.bfloat16)
    per_far = near_count * capacity
    spread = jnp.where(iota((slots, lead), 0) // per_far == iota((slots, lead), 1), 1.0, 0.0).astype(jnp.bfloat16)
    slot = iota((slots, cols), 0) % per_far
    block = (near - slot // capacity + near_count) % near_count
    pick = (iota((slots, cols), 1) // tok_local == block) & (
        exact_dot(spread, place).astype(jnp.int32) == slot % capacity
    )
    pick = jnp.where(pick, 1.0, 0.0).astype(jnp.bfloat16)
    pick_ref[...] = pick
    picked_rows(pick, blocks, out_ref)


def pick_kernel(pick_ref, *refs):
    picked_rows(pick_ref[...], refs[:-1], refs[-1])


def join_kernel(*refs):
    out_ref = refs[-1]
    start = 0
    for ref in refs[:-1]:
        out_ref[:, start : start + ref.shape[1]] = ref[...]
        start += ref.shape[1]


def down_kernel(near_count, capacity, scalars_ref, *refs):
    rows, hids, (out_ref, turned_ref) = refs[: 2 * PARTS], refs[2 * PARTS : -2], refs[-2:]
    step = pl.program_id(0)
    share, tile = out_ref.shape
    near, far, replica = scalars_ref[0], scalars_ref[1], scalars_ref[2]

    @pl.when(step == 0)
    def _():
        slots, lines = rows[0].shape[0], hids[0].shape[0]
        hidden_width = hids[0].shape[1] // near_count
        row, col = iota((slots, lines), 0), iota((slots, lines), 1)
        match = (row // (near_count * capacity) ^ far == col // capacity) & (row % capacity == col % capacity)
        block = (near - row // capacity % near_count + near_count) % near_count
        for i, ref in enumerate(hids):
            total = jnp.zeros((slots, share), jnp.float32)
            for j in range(near_count):
                start = pl.multiple_of(j * hidden_width + replica * share, 128)
                order = jnp.where(match & (block == j), 1.0, 0.0).astype(jnp.bfloat16)
                total = total + exact_dot(order, ref[:, pl.ds(start, share)])
            turned_ref[:, i * slots : (i + 1) * slots] = total.T.astype(jnp.bfloat16)

    bounds = part_bounds(sum(ref.shape[1] for ref in rows[:PARTS]))
    for i in range(bounds[-1][1] // tile):

        @pl.when(step == i)
        def _(i=i):
            pieces = []
            for part, (start, stop) in enumerate(bounds):
                first, last = max(i * tile, start) - start, min((i + 1) * tile, stop) - start
                if first < last:
                    pieces.append(jnp.concatenate([ref[:, first:last] for ref in rows[part::PARTS]], axis=0))
            tokens = pieces[0] if len(pieces) == 1 else jnp.concatenate(pieces, axis=1)
            out_ref[...] = exact_dot(turned_ref[...], tokens).astype(jnp.bfloat16)


def scalar_spec():
    return pl.BlockSpec(memory_space=pltpu.SMEM)


def params(mib):
    return pltpu.CompilerParams(vmem_limit_bytes=mib * MIB)


def hbm_spec():
    return pl.BlockSpec(memory_space=pltpu.HBM)


def split_rows(ids, tokens):
    tok_local, width = tokens.shape
    widths = [stop - start for start, stop in part_bounds(width)]
    widths[0] += ID_COLS
    vmem = pl.BlockSpec(memory_space=pltpu.VMEM)
    return pl.pallas_call(
        split_kernel,
        out_shape=[jax.ShapeDtypeStruct((tok_local, part), jnp.bfloat16) for part in widths],
        in_specs=[vmem, hbm_spec()],
        out_specs=[vmem] * PARTS,
        scratch_shapes=[pltpu.SemaphoreType.DMA((PARTS,))],
        compiler_params=params(8),
        name="split_rows",
    )(ids, tokens)


def send_rows(far_count, near_count, capacity, scalars, ids, gates, hidden):
    slots = far_count * near_count * capacity
    rows, wide = hidden.shape
    vmem = pl.BlockSpec(memory_space=pltpu.VMEM)
    shapes = [(slots // far_count, wide)] * far_count + [(slots, rows)]
    return pl.pallas_call(
        functools.partial(send_kernel, far_count, near_count, capacity),
        out_shape=[jax.ShapeDtypeStruct(shape, jnp.bfloat16) for shape in shapes],
        in_specs=[scalar_spec()] + [vmem] * 3,
        out_specs=[vmem] * len(shapes),
        compiler_params=params(12),
        cost_estimate=pl.CostEstimate(flops=2 * rows * rows * wide, bytes_accessed=4 * rows * wide, transcendentals=0),
        name="send_rows",
    )(scalars, ids, gates, hidden)


def regroup(near_count, capacity, arrays):
    lines = len(arrays) * capacity
    vmem = pl.BlockSpec(memory_space=pltpu.VMEM)
    return pl.pallas_call(
        functools.partial(regroup_kernel, len(arrays), near_count, capacity),
        out_shape=[jax.ShapeDtypeStruct((lines, arrays[0].shape[1]), jnp.bfloat16)] * near_count,
        in_specs=[vmem] * len(arrays),
        out_specs=[vmem] * near_count,
        compiler_params=params(8),
        name="regroup_rows",
    )(*arrays)


def close(back_place, came_back, gates, hidden):
    vmem = pl.BlockSpec(memory_space=pltpu.VMEM)
    return pl.pallas_call(
        close_kernel,
        out_shape=[
            jax.ShapeDtypeStruct(hidden.shape, jnp.bfloat16),
            jax.ShapeDtypeStruct(gates.shape, jnp.float32),
        ],
        in_specs=[vmem, vmem, hbm_spec(), hbm_spec()],
        out_specs=[vmem] * 2,
        scratch_shapes=[
            pltpu.VMEM(gates.shape, gates.dtype),
            pltpu.VMEM(hidden.shape, hidden.dtype),
            pltpu.SemaphoreType.DMA((2,)),
        ],
        compiler_params=params(12),
        name="close_rows",
    )(back_place, came_back, gates, hidden)


def first_pick(far_count, near_count, capacity, near, blocks):
    tok_local, wide = blocks[0].shape
    slots = far_count * near_count * capacity
    vmem = pl.BlockSpec(memory_space=pltpu.VMEM)
    return pl.pallas_call(
        functools.partial(first_pick_kernel, far_count, near_count, capacity),
        out_shape=[
            jax.ShapeDtypeStruct((slots, wide - ID_COLS), jnp.bfloat16),
            jax.ShapeDtypeStruct((slots, near_count * tok_local), jnp.bfloat16),
        ],
        in_specs=[scalar_spec()] + [vmem] * len(blocks),
        out_specs=[vmem] * 2,
        compiler_params=params(16),
        name="first_pick",
    )(near, *blocks)


def pick_rows(pick, blocks):
    vmem = pl.BlockSpec(memory_space=pltpu.VMEM)
    return pl.pallas_call(
        pick_kernel,
        out_shape=jax.ShapeDtypeStruct((pick.shape[0], blocks[0].shape[1]), jnp.bfloat16),
        in_specs=[vmem] * (1 + len(blocks)),
        out_specs=vmem,
        compiler_params=params(16),
        name="pick_rows",
    )(pick, *blocks)


def join_rows(arrays):
    vmem = pl.BlockSpec(memory_space=pltpu.VMEM)
    shape = (arrays[0].shape[0], sum(array.shape[1] for array in arrays))
    return pl.pallas_call(
        join_kernel,
        out_shape=jax.ShapeDtypeStruct(shape, jnp.bfloat16),
        in_specs=[vmem] * len(arrays),
        out_specs=vmem,
        compiler_params=params(8),
        name="join_rows",
    )(*arrays)


def down_rows(near_count, capacity, scalars, rows, hids, share):
    lines = 2 * rows[0].shape[0]
    width = sum(array.shape[1] for array in rows[:PARTS])
    tile = 2 * TILE
    whole = lambda array: pl.BlockSpec(array.shape, lambda i: (0, 0))
    return pl.pallas_call(
        functools.partial(down_kernel, near_count, capacity),
        grid=(width // tile,),
        out_shape=jax.ShapeDtypeStruct((share, width), jnp.bfloat16),
        in_specs=[scalar_spec()] + [whole(array) for array in rows + hids],
        out_specs=pl.BlockSpec((share, tile), lambda i: (0, i)),
        scratch_shapes=[pltpu.VMEM((share, lines), jnp.bfloat16)],
        compiler_params=params(32),
        cost_estimate=pl.CostEstimate(
            flops=2 * lines * width * share, bytes_accessed=2 * width * (lines + share), transcendentals=0
        ),
        name="down_rows",
    )(scalars, *rows, *hids)


def local(grad_out, hidden, gates, expert_ids, w_down):
    tok_local, top_count = expert_ids.shape
    far_count = lax.axis_size("far")
    near_count = lax.axis_size("near")
    experts = far_count * near_count
    capacity = max(4, (tok_local * top_count + experts - 1) // experts)
    width = grad_out.shape[1]
    hidden_width = hidden.shape[2]
    row_total = tok_local * top_count
    slot_total = experts * capacity
    near = lax.axis_index("near")
    near_ref = near.astype(jnp.int32).reshape(1)
    bounds = part_bounds(width)
    weight = w_down[0]

    def along(array, steps):
        return lax.ppermute(array, "near", [(i, (i + steps) % near_count) for i in range(near_count)])

    def across(array, apart):
        return lax.ppermute(array, "far", [(i, i ^ apart) for i in range(far_count)])

    def swap(array):
        return lax.ppermute(array, "dp", [(i, i ^ 1) for i in range(lax.axis_size("dp"))])

    def line(array):
        blocks = {0: array}
        for step in sorted(range(1, near_count), key=lambda step: min(step, near_count - step)):
            blocks[step] = along(array, step)
        return [blocks[step] for step in range(near_count)]

    hidden_rows = hidden.reshape(row_total, hidden_width)
    scalars = jnp.stack([near, lax.axis_index("far"), lax.axis_index("dp")]).astype(jnp.int32)
    ids = expert_ids.T
    parts = list(split_rows(ids, grad_out))
    parts[0], ids = lax.optimization_barrier((parts[0], ids))
    blocks = line(parts[0])
    *sends, back_place = send_rows(far_count, near_count, capacity, scalars, ids, gates.T, hidden_rows)
    crossed = [sends[0]] + [across(sends[apart], apart) for apart in range(1, far_count)]

    rows, total = [], None
    for i in range(PARTS):
        if i == 0:
            picked, pick = first_pick(far_count, near_count, capacity, near_ref, blocks)
            picked, crossed, parts = lax.optimization_barrier((picked, crossed, parts))
        else:
            picked = pick_rows(pick, line(parts[i]))
            picked, rows[-1], crossed = lax.optimization_barrier((picked, rows[-1], crossed))
        got = lax.all_to_all(
            picked.reshape(far_count, -1, picked.shape[1]), "far", split_axis=0, concat_axis=0, tiled=True
        ).reshape(picked.shape)
        rows.append(got)
    hids = list(regroup(near_count, capacity, crossed))
    hids = join_rows(hids[:1] + [along(hids[step], step) for step in range(1, near_count)])
    for i in range(PARTS):
        if i:
            rows[i], total, hids = lax.optimization_barrier((rows[i], total, hids))
        product = lax.dot_general(
            rows[i],
            weight[:, bounds[i][0] : bounds[i][1]],
            (((1,), (1,)), ((), ())),
            preferred_element_type=jnp.float32,
        )
        total = product if total is None else total + product
    came_back = lax.all_to_all(
        total.astype(jnp.bfloat16).reshape(experts, capacity, hidden_width),
        ("far", "near"),
        split_axis=0,
        concat_axis=0,
        tiled=True,
    )

    grad_down = down_rows(
        near_count,
        capacity,
        scalars,
        rows + [swap(array) for array in rows],
        [hids, swap(hids)],
        hidden_width // lax.axis_size("dp"),
    )
    came_back, grad_down = lax.optimization_barrier((came_back, grad_down))

    grad_hidden, grad_gates = close(
        back_place, came_back.reshape(slot_total, hidden_width), gates.T, hidden_rows
    )
    return (grad_hidden.reshape(hidden.shape), grad_gates.T, grad_down[None])


def solution(mesh):
    placed = (
        P(("dp", "far", "near"), None),
        P(("dp", "far", "near"), None, None),
        P(("dp", "far", "near"), None),
        P(("dp", "far", "near"), None),
        P(("far", "near"), None, None),
    )
    return jax.shard_map(
        local,
        mesh=mesh,
        in_specs=placed,
        out_specs=(
            P(("dp", "far", "near"), None, None),
            P(("dp", "far", "near"), None),
            P(("far", "near"), "dp", None),
        ),
        check_vma=False,
    )
```

```python
import functools

import jax
import jax.numpy as jnp
from jax import lax
from jax.experimental import pallas as pl
from jax.experimental.pallas import tpu as pltpu
from jax.sharding import PartitionSpec as P

ID_COLS = 128
PARTS = 2
TILE = 256
MIB = 1024 * 1024


def iota(shape, dim):
    return lax.broadcasted_iota(jnp.int32, shape, dim)


def part_bounds(width):
    first = width // TILE * 9 // 16 * TILE
    return [(0, first), (first, width)]


def exact_dot(one_hot, values):
    return jnp.dot(one_hot, values, preferred_element_type=jnp.float32)


def split_kernel(ids_ref, tokens_hbm, *refs):
    outs, sem = refs[:-1], refs[-1]
    copies = []
    for i, (start, stop) in enumerate(part_bounds(tokens_hbm.shape[1])):
        target = outs[i].at[:, : stop - start]
        copies.append(pltpu.make_async_copy(tokens_hbm.at[:, start:stop], target, sem.at[i]))
    for copy in copies:
        copy.start()
    top_count, tok_local = ids_ref.shape
    same = jnp.where(iota((top_count, ID_COLS), 0) == iota((top_count, ID_COLS), 1), 1.0, 0.0).astype(jnp.bfloat16)
    ids = ids_ref[...].astype(jnp.float32).astype(jnp.bfloat16)
    ids = lax.dot_general(ids, same, (((0,), (0,)), ((), ())), preferred_element_type=jnp.float32)
    ids = jnp.where(iota((tok_local, ID_COLS), 1) < top_count, ids, -1.0)
    outs[0][:, outs[0].shape[1] - ID_COLS :] = ids.astype(jnp.bfloat16)
    for copy in copies:
        copy.wait()


def send_kernel(far_count, near_count, capacity, scalars_ref, ids_ref, gates_ref, hidden_ref, *refs):
    sends, back_ref = refs[:-1], refs[-1]
    top_count, tok_local = ids_ref.shape
    rows = tok_local * top_count
    experts = far_count * near_count
    slots = experts * capacity
    near, own_far = scalars_ref[0], scalars_ref[1]
    wide = jnp.where(iota((tok_local, rows), 1) // top_count == iota((tok_local, rows), 0), 1.0, 0.0).astype(jnp.bfloat16)
    mine = iota((top_count, rows), 1) % top_count == iota((top_count, rows), 0)

    def line(values):
        spread = jnp.zeros((top_count, rows), jnp.float32)
        for _ in range(3):
            piece = values.astype(jnp.bfloat16)
            values = values - piece.astype(jnp.float32)
            spread = spread + exact_dot(piece, wide)
        return jnp.sum(jnp.where(mine, spread, 0.0), axis=0, keepdims=True)

    ids = line(ids_ref[...].astype(jnp.float32)).astype(jnp.int32)
    gates = line(gates_ref[...])
    named = iota((experts, rows), 0) == ids
    before = jnp.where(iota((rows, rows), 0) < iota((rows, rows), 1), 1.0, 0.0).astype(jnp.bfloat16)
    counts = exact_dot(jnp.where(named, 1.0, 0.0).astype(jnp.bfloat16), before)
    ranks = jnp.sum(jnp.where(named, counts, 0.0), axis=0, keepdims=True).astype(jnp.int32)
    steps = (ids % near_count - near + near_count) % near_count
    out_slots = ((ids // near_count ^ own_far) * near_count + steps) * capacity + ranks
    back_slots = ids * capacity + ranks
    back_ref[...] = jnp.where(iota((slots, rows), 0) == back_slots, 1.0, 0.0).astype(jnp.bfloat16)
    place = iota((slots, rows), 0) == out_slots
    gate = jnp.sum(jnp.where(place, gates, 0.0), axis=1, keepdims=True)
    place = jnp.where(place, 1.0, 0.0).astype(jnp.bfloat16)
    send = (exact_dot(place, hidden_ref[...]) * gate).astype(jnp.bfloat16)
    for i, ref in enumerate(sends):
        ref[...] = send[i * ref.shape[0] : (i + 1) * ref.shape[0]]


def regroup_kernel(far_count, near_count, capacity, *refs):
    ins, outs = refs[:far_count], refs[far_count:]
    rows = jnp.concatenate([ref[...] for ref in ins], axis=0)
    for step, ref in enumerate(outs):
        shape = (ref.shape[0], rows.shape[0])
        row, col = iota(shape, 0), iota(shape, 1)
        source = (row // capacity * near_count + step) * capacity + row % capacity
        ref[...] = exact_dot(jnp.where(col == source, 1.0, 0.0).astype(jnp.bfloat16), rows).astype(jnp.bfloat16)


def close_kernel(back_ref, came_ref, gates_hbm, hidden_hbm, hid_ref, gates_out_ref, gates_ref, hidden_ref, sem):
    copy = pltpu.make_async_copy(hidden_hbm, hidden_ref, sem.at[0])
    small = pltpu.make_async_copy(gates_hbm, gates_ref, sem.at[1])
    small.start()
    copy.start()
    top_count, tok_local = gates_ref.shape
    rows = tok_local * top_count
    back = lax.dot_general(
        back_ref[...], came_ref[...], (((0,), (0,)), ((), ())), preferred_element_type=jnp.float32
    )
    small.wait()
    mine = iota((tok_local, top_count, tok_local), 0) == iota((tok_local, top_count, tok_local), 2)
    gate = jnp.where(mine, gates_ref[...][None], 0.0).reshape(rows, tok_local)
    gate = jnp.sum(gate, axis=1, keepdims=True)
    hid_ref[...] = (gate * back).astype(jnp.bfloat16)
    copy.wait()
    sums = jnp.sum(back * hidden_ref[...].astype(jnp.float32), axis=1, keepdims=True)
    spread = jnp.broadcast_to(sums, (rows, tok_local)).reshape(tok_local, top_count, tok_local)
    gates_out_ref[...] = jnp.sum(jnp.where(mine, spread, 0.0), axis=0)


def picked_rows(pick, blocks, out_ref):
    width = out_ref.shape[1]
    step = max(lanes for lanes in range(128, 1025, 128) if width % lanes == 0)
    for start in range(0, width, step):
        tokens = jnp.concatenate([block[:, start : start + step] for block in blocks], axis=0)
        out_ref[:, start : start + step] = exact_dot(pick, tokens).astype(jnp.bfloat16)


def first_pick_kernel(far_count, near_count, capacity, near_ref, *refs):
    blocks, (out_ref, pick_ref) = refs[:-2], refs[-2:]
    tok_local = blocks[0].shape[0]
    width = out_ref.shape[1]
    near = near_ref[0]
    cols = near_count * tok_local
    slots = far_count * near_count * capacity
    lead = max(8, far_count)
    ids = jnp.concatenate([block[:, width:] for block in blocks], axis=0).astype(jnp.float32)
    ones = jnp.ones((lead, ID_COLS), jnp.bfloat16)
    named = jnp.zeros((lead, cols), jnp.float32)
    for far in range(far_count):
        expert = (far * near_count + near).astype(jnp.float32)
        hit = jnp.where(ids == expert, 1.0, 0.0).astype(jnp.bfloat16)
        line = lax.dot_general(ones, hit, (((1,), (1,)), ((), ())), preferred_element_type=jnp.float32)
        named = jnp.where(iota((lead, cols), 0) == far, line, named)
    row, col = iota((cols, cols), 0), iota((cols, cols), 1)
    before = jnp.where((row < col) & (row // tok_local == col // tok_local), 1.0, 0.0).astype(jnp.bfloat16)
    rank = exact_dot(named.astype(jnp.bfloat16), before)
    place = jnp.where(named > 0.5, rank, float(capacity)).astype(jnp.bfloat16)
    per_far = near_count * capacity
    spread = jnp.where(iota((slots, lead), 0) // per_far == iota((slots, lead), 1), 1.0, 0.0).astype(jnp.bfloat16)
    slot = iota((slots, cols), 0) % per_far
    block = (near - slot // capacity + near_count) % near_count
    pick = (iota((slots, cols), 1) // tok_local == block) & (
        exact_dot(spread, place).astype(jnp.int32) == slot % capacity
    )
    pick = jnp.where(pick, 1.0, 0.0).astype(jnp.bfloat16)
    pick_ref[...] = pick
    picked_rows(pick, blocks, out_ref)


def pick_kernel(pick_ref, *refs):
    picked_rows(pick_ref[...], refs[:-1], refs[-1])


def join_kernel(*refs):
    out_ref = refs[-1]
    start = 0
    for ref in refs[:-1]:
        out_ref[:, start : start + ref.shape[1]] = ref[...]
        start += ref.shape[1]


def down_kernel(near_count, capacity, scalars_ref, *refs):
    rows, hids, (out_ref, turned_ref) = refs[: 2 * PARTS], refs[2 * PARTS : -2], refs[-2:]
    step = pl.program_id(0)
    share, tile = out_ref.shape
    near, far, replica = scalars_ref[0], scalars_ref[1], scalars_ref[2]

    @pl.when(step == 0)
    def _():
        slots, lines = rows[0].shape[0], hids[0].shape[0]
        hidden_width = hids[0].shape[1] // near_count
        row, col = iota((slots, lines), 0), iota((slots, lines), 1)
        match = (row // (near_count * capacity) ^ far == col // capacity) & (row % capacity == col % capacity)
        block = (near - row // capacity % near_count + near_count) % near_count
        for i, ref in enumerate(hids):
            total = jnp.zeros((slots, share), jnp.float32)
            for j in range(near_count):
                start = pl.multiple_of(j * hidden_width + replica * share, 128)
                order = jnp.where(match & (block == j), 1.0, 0.0).astype(jnp.bfloat16)
                total = total + exact_dot(order, ref[:, pl.ds(start, share)])
            turned_ref[:, i * slots : (i + 1) * slots] = total.T.astype(jnp.bfloat16)

    bounds = part_bounds(sum(ref.shape[1] for ref in rows[:PARTS]))
    for i in range(bounds[-1][1] // tile):

        @pl.when(step == i)
        def _(i=i):
            pieces = []
            for part, (start, stop) in enumerate(bounds):
                first, last = max(i * tile, start) - start, min((i + 1) * tile, stop) - start
                if first < last:
                    pieces.append(jnp.concatenate([ref[:, first:last] for ref in rows[part::PARTS]], axis=0))
            tokens = pieces[0] if len(pieces) == 1 else jnp.concatenate(pieces, axis=1)
            out_ref[...] = exact_dot(turned_ref[...], tokens).astype(jnp.bfloat16)


def scalar_spec():
    return pl.BlockSpec(memory_space=pltpu.SMEM)


def params(mib):
    return pltpu.CompilerParams(vmem_limit_bytes=mib * MIB)


def hbm_spec():
    return pl.BlockSpec(memory_space=pltpu.HBM)


def split_rows(ids, tokens):
    tok_local, width = tokens.shape
    widths = [stop - start for start, stop in part_bounds(width)]
    widths[0] += ID_COLS
    vmem = pl.BlockSpec(memory_space=pltpu.VMEM)
    return pl.pallas_call(
        split_kernel,
        out_shape=[jax.ShapeDtypeStruct((tok_local, part), jnp.bfloat16) for part in widths],
        in_specs=[vmem, hbm_spec()],
        out_specs=[vmem] * PARTS,
        scratch_shapes=[pltpu.SemaphoreType.DMA((PARTS,))],
        compiler_params=params(8),
        name="split_rows",
    )(ids, tokens)


def send_rows(far_count, near_count, capacity, scalars, ids, gates, hidden):
    slots = far_count * near_count * capacity
    rows, wide = hidden.shape
    vmem = pl.BlockSpec(memory_space=pltpu.VMEM)
    shapes = [(slots // far_count, wide)] * far_count + [(slots, rows)]
    return pl.pallas_call(
        functools.partial(send_kernel, far_count, near_count, capacity),
        out_shape=[jax.ShapeDtypeStruct(shape, jnp.bfloat16) for shape in shapes],
        in_specs=[scalar_spec()] + [vmem] * 3,
        out_specs=[vmem] * len(shapes),
        compiler_params=params(12),
        cost_estimate=pl.CostEstimate(flops=2 * rows * rows * wide, bytes_accessed=4 * rows * wide, transcendentals=0),
        name="send_rows",
    )(scalars, ids, gates, hidden)


def regroup(near_count, capacity, arrays):
    lines = len(arrays) * capacity
    vmem = pl.BlockSpec(memory_space=pltpu.VMEM)
    return pl.pallas_call(
        functools.partial(regroup_kernel, len(arrays), near_count, capacity),
        out_shape=[jax.ShapeDtypeStruct((lines, arrays[0].shape[1]), jnp.bfloat16)] * near_count,
        in_specs=[vmem] * len(arrays),
        out_specs=[vmem] * near_count,
        compiler_params=params(8),
        name="regroup_rows",
    )(*arrays)


def close(back_place, came_back, gates, hidden):
    vmem = pl.BlockSpec(memory_space=pltpu.VMEM)
    return pl.pallas_call(
        close_kernel,
        out_shape=[
            jax.ShapeDtypeStruct(hidden.shape, jnp.bfloat16),
            jax.ShapeDtypeStruct(gates.shape, jnp.float32),
        ],
        in_specs=[vmem, vmem, hbm_spec(), hbm_spec()],
        out_specs=[vmem] * 2,
        scratch_shapes=[
            pltpu.VMEM(gates.shape, gates.dtype),
            pltpu.VMEM(hidden.shape, hidden.dtype),
            pltpu.SemaphoreType.DMA((2,)),
        ],
        compiler_params=params(12),
        name="close_rows",
    )(back_place, came_back, gates, hidden)


def first_pick(far_count, near_count, capacity, near, blocks):
    tok_local, wide = blocks[0].shape
    slots = far_count * near_count * capacity
    vmem = pl.BlockSpec(memory_space=pltpu.VMEM)
    return pl.pallas_call(
        functools.partial(first_pick_kernel, far_count, near_count, capacity),
        out_shape=[
            jax.ShapeDtypeStruct((slots, wide - ID_COLS), jnp.bfloat16),
            jax.ShapeDtypeStruct((slots, near_count * tok_local), jnp.bfloat16),
        ],
        in_specs=[scalar_spec()] + [vmem] * len(blocks),
        out_specs=[vmem] * 2,
        compiler_params=params(16),
        name="first_pick",
    )(near, *blocks)


def pick_rows(pick, blocks):
    vmem = pl.BlockSpec(memory_space=pltpu.VMEM)
    return pl.pallas_call(
        pick_kernel,
        out_shape=jax.ShapeDtypeStruct((pick.shape[0], blocks[0].shape[1]), jnp.bfloat16),
        in_specs=[vmem] * (1 + len(blocks)),
        out_specs=vmem,
        compiler_params=params(16),
        name="pick_rows",
    )(pick, *blocks)


def join_rows(arrays):
    vmem = pl.BlockSpec(memory_space=pltpu.VMEM)
    shape = (arrays[0].shape[0], sum(array.shape[1] for array in arrays))
    return pl.pallas_call(
        join_kernel,
        out_shape=jax.ShapeDtypeStruct(shape, jnp.bfloat16),
        in_specs=[vmem] * len(arrays),
        out_specs=vmem,
        compiler_params=params(8),
        name="join_rows",
    )(*arrays)


def down_rows(near_count, capacity, scalars, rows, hids, share):
    lines = 2 * rows[0].shape[0]
    width = sum(array.shape[1] for array in rows[:PARTS])
    tile = 2 * TILE
    whole = lambda array: pl.BlockSpec(array.shape, lambda i: (0, 0))
    return pl.pallas_call(
        functools.partial(down_kernel, near_count, capacity),
        grid=(width // tile,),
        out_shape=jax.ShapeDtypeStruct((share, width), jnp.bfloat16),
        in_specs=[scalar_spec()] + [whole(array) for array in rows + hids],
        out_specs=pl.BlockSpec((share, tile), lambda i: (0, i)),
        scratch_shapes=[pltpu.VMEM((share, lines), jnp.bfloat16)],
        compiler_params=params(32),
        cost_estimate=pl.CostEstimate(
            flops=2 * lines * width * share, bytes_accessed=2 * width * (lines + share), transcendentals=0
        ),
        name="down_rows",
    )(scalars, *rows, *hids)


def local(grad_out, hidden, gates, expert_ids, w_down):
    tok_local, top_count = expert_ids.shape
    far_count = lax.axis_size("far")
    near_count = lax.axis_size("near")
    experts = far_count * near_count
    capacity = max(4, (tok_local * top_count + experts - 1) // experts)
    width = grad_out.shape[1]
    hidden_width = hidden.shape[2]
    row_total = tok_local * top_count
    slot_total = experts * capacity
    near = lax.axis_index("near")
    near_ref = near.astype(jnp.int32).reshape(1)
    bounds = part_bounds(width)
    weight = w_down[0]

    def along(array, steps):
        return lax.ppermute(array, "near", [(i, (i + steps) % near_count) for i in range(near_count)])

    def across(array, apart):
        return lax.ppermute(array, "far", [(i, i ^ apart) for i in range(far_count)])

    def swap(array):
        return lax.ppermute(array, "dp", [(i, i ^ 1) for i in range(lax.axis_size("dp"))])

    def line(array):
        return [array] + [along(array, step) for step in range(1, near_count)]

    hidden_rows = hidden.reshape(row_total, hidden_width)
    scalars = jnp.stack([near, lax.axis_index("far"), lax.axis_index("dp")]).astype(jnp.int32)
    ids = expert_ids.T
    parts = list(split_rows(ids, grad_out))
    parts[0], ids = lax.optimization_barrier((parts[0], ids))
    blocks = line(parts[0])
    *sends, back_place = send_rows(far_count, near_count, capacity, scalars, ids, gates.T, hidden_rows)
    crossed = [sends[0]] + [across(sends[apart], apart) for apart in range(1, far_count)]

    rows, total = [], None
    for i in range(PARTS):
        if i == 0:
            picked, pick = first_pick(far_count, near_count, capacity, near_ref, blocks)
            picked, crossed, parts = lax.optimization_barrier((picked, crossed, parts))
        else:
            picked = pick_rows(pick, line(parts[i]))
            picked, rows[-1], crossed = lax.optimization_barrier((picked, rows[-1], crossed))
        got = lax.all_to_all(
            picked.reshape(far_count, -1, picked.shape[1]), "far", split_axis=0, concat_axis=0, tiled=True
        ).reshape(picked.shape)
        rows.append(got)
    hids = list(regroup(near_count, capacity, crossed))
    hids = join_rows(hids[:1] + [along(hids[step], step) for step in range(1, near_count)])
    for i in range(PARTS):
        if i:
            rows[i], total = lax.optimization_barrier((rows[i], total))
        product = lax.dot_general(
            rows[i],
            weight[:, bounds[i][0] : bounds[i][1]],
            (((1,), (1,)), ((), ())),
            preferred_element_type=jnp.float32,
        )
        total = product if total is None else total + product
    total, hids = lax.optimization_barrier((total, hids))
    came_back = lax.all_to_all(
        total.astype(jnp.bfloat16).reshape(experts, capacity, hidden_width),
        ("far", "near"),
        split_axis=0,
        concat_axis=0,
        tiled=True,
    )

    grad_down = down_rows(
        near_count,
        capacity,
        scalars,
        rows + [swap(array) for array in rows],
        [hids, swap(hids)],
        hidden_width // lax.axis_size("dp"),
    )
    came_back, grad_down = lax.optimization_barrier((came_back, grad_down))

    grad_hidden, grad_gates = close(
        back_place, came_back.reshape(slot_total, hidden_width), gates.T, hidden_rows
    )
    return (grad_hidden.reshape(hidden.shape), grad_gates.T, grad_down[None])


def solution(mesh):
    placed = (
        P(("dp", "far", "near"), None),
        P(("dp", "far", "near"), None, None),
        P(("dp", "far", "near"), None),
        P(("dp", "far", "near"), None),
        P(("far", "near"), None, None),
    )
    return jax.shard_map(
        local,
        mesh=mesh,
        in_specs=placed,
        out_specs=(
            P(("dp", "far", "near"), None, None),
            P(("dp", "far", "near"), None),
            P(("far", "near"), "dp", None),
        ),
        check_vma=False,
    )
```
